32 devices in a mesh: wide: 8 (over z, x), narrow: 4 (over y, core).
Axes of the slice: x: 2, y: 2, z: 4, core: 2. Of those that a mesh axis runs over, the one named last changes fastest.
Arguments:
- tokens: bfloat16 [32768, 512], P(('wide', 'narrow')), may hold values from -6 to 6
- memory: bfloat16 [16384, 512], P(('wide', 'narrow')), may hold values from -6 to 6
- w_wide: bfloat16 [512, 6144], P(('wide', 'narrow'))
- w_tall: bfloat16 [3072, 512], P(('wide', 'narrow'))
- vecs: bfloat16 [512, 18], P(('wide', 'narrow'))
- avg_wide: float32 [512, 6144], P(('wide', 'narrow')), may hold values from -0.25 to 0.25
- avg_tall: float32 [3072, 512], P(('wide', 'narrow')), may hold values from -0.125 to 0.125
- avg_vecs: float32 [512, 18], P(('wide', 'narrow')), may hold values from -3 to 3
- tgt_lengths: int32 [32, 6], P(('wide', 'narrow')), may hold values from 1 to 512, 1024 in all within a row
- src_lengths: int32 [32, 6], P(('wide', 'narrow')), may hold values from 1 to 256, 512 in all within a row
- cotangent: bfloat16 [32768, 512], P(('wide', 'narrow')), may hold values from -6 to 6
Outputs:
- slots: bfloat16 [32768, 512], P(('wide', 'narrow'))
- grad_tokens: float32 [32768, 512], P(('wide', 'narrow'))
- grad_memory: float32 [16384, 512], P(('wide', 'narrow'))
- grad_wide: float32 [512, 6144], P(('wide', 'narrow'))
- grad_tall: float32 [3072, 512], P(('wide', 'narrow'))
- grad_vecs: float32 [512, 18], P(('wide', 'narrow'))
- new_avg_wide: float32 [512, 6144], P(('wide', 'narrow'))
- new_avg_tall: float32 [3072, 512], P(('wide', 'narrow'))
- new_avg_vecs: float32 [512, 18], P(('wide', 'narrow'))
The draws below stay inside these ranges and needn't reach their ends.
Inputs may be any that keep to these rules, and one draw needn't show every extreme that they name: `tgt_lengths`: each row holds the 6 target segment lengths of one device's 1024 rows in order and sums to 1024; the last segment of every row is padding. `src_lengths`: each row holds the 6 source segment lengths of one device's 512 memory rows in order and sums to 512; target segment j reads source segment j.
All inputs are finite; a program needn't handle non-finite values.
Results may differ from the reference program's by a relative error of at most 0.019.
The reference program's roundings to bfloat16 on the way count: a program that leaves them out, or rounds other values in their place, can miss the bound.
Values may be sent and summed in bfloat16 or wider, within the bound.
A program may use at most 192 MiB of HBM per device.

```python
import math
import jax
import jax.numpy as jnp
import numpy as np
from jax import lax

D = 512
HEADS = 8
HEAD_DIM = 64
FF = 2048
TOK_DEV = 1024
SEGS = 6
AVG_STEPS = 4
MAXLEN = 512
SRC_DEV = 512
SRC_MOST = 256
NVEC = 18
TOKENS = 32768
SOURCES = 16384
DEVICES = 32


def draw_w_wide(key, part):
    key = jax.random.fold_in(key, 11)
    unit_values = jax.random.normal(key, (D, 8 * D + FF), jnp.float32)
    column_block = jnp.minimum(jnp.arange(8 * D + FF) // D, 8)
    block_scale = jnp.array([1.4, 1.0, 1.0, 5.6, 1.4, 1.0, 1.0, 5.6, 1.0], jnp.float32)
    scaled = unit_values * block_scale[column_block][None, :] / math.sqrt(D)
    return scaled.astype(jnp.bfloat16)


def draw_w_tall(key, part):
    key = jax.random.fold_in(key, 23)
    unit_values = jax.random.normal(key, (FF + 2 * D, D), jnp.float32)
    row_scale = jnp.where(jnp.arange(FF + 2 * D) < FF, 1.5 / math.sqrt(FF), 1.0 / math.sqrt(2 * D))
    return (unit_values * row_scale[:, None]).astype(jnp.bfloat16)


def draw_vecs(key, part):
    key = jax.random.fold_in(key, 37)
    gain_key = jax.random.fold_in(key, 1)
    bias_key = jax.random.fold_in(key, 2)
    offset = 6 + FF // D
    column = jnp.arange(NVEC)
    is_gain = (column == offset + 2) | (column == offset + 4) | (column == offset + 6)
    gains = 1.0 + 0.4 * jax.random.uniform(gain_key, (D, NVEC), jnp.float32, -1.0, 1.0)
    biases = 0.3 * jax.random.normal(bias_key, (D, NVEC), jnp.float32)
    return jnp.where(is_gain[None, :], gains, biases).astype(jnp.bfloat16)


def block_levels(rng, extent, split, smallest, high):
    level = 1.0
    for position, blocks in split:
        steps = jax.random.uniform(jax.random.fold_in(jax.random.fold_in(rng, 6), position), (blocks,), jnp.float32, smallest / len(split), high / len(split))
        level = level * jnp.repeat(jnp.exp(steps), extent[position] // blocks).reshape((-1,) + (1,) * (len(extent) - 1 - position))
    return level


def profile(number_of, total, most, lean):
    loads = [(1 << 20) // math.isqrt(rank ** lean) + 1 for rank in range(2, number_of + 1)]
    spare, given = total - most - (number_of - 1), [1] * (number_of - 1)
    while spare > 0:
        free = [i for i in range(number_of - 1) if given[i] < most]
        mass, left = sum([loads[i] for i in free]), spare
        for i in free:
            extra = min(most - given[i], max(1, left * loads[i] // mass), spare)
            given[i] = given[i] + extra
            spare = spare - extra
    return np.array([most] + given)


def ragged(own_key, count, total, bound, skew):
    if count == 2:
        one = jax.random.randint(own_key, (), max(1, total - bound), min(bound, total - 1) + 1)
        return jnp.stack([one, total - one])
    tallies = jnp.asarray(profile(count, total, bound, skew), jnp.int32)
    twos = (count - 1) // 2
    source_of, sink = tallies[1:1 + 2 * twos:2], tallies[2:2 + 2 * twos:2]
    margin = jnp.minimum(source_of - 1, bound - sink)
    passed = jax.random.randint(jax.random.fold_in(own_key, 1), (twos,), 0, 1 << 20) % (margin + 1)
    tallies = tallies.at[1:1 + 2 * twos:2].set(source_of - passed).at[2:2 + 2 * twos:2].set(sink + passed)
    return tallies[jax.random.permutation(jax.random.fold_in(own_key, 2), count)]


def bell_draw(rng, dims, deviation, reach, shards=(), held_as=jnp.bfloat16):
    values = deviation * jax.random.normal(rng, dims, jnp.float32)
    if shards:
        values = values * block_levels(rng, dims, shards, -0.22, 0.18)
    return jnp.clip(values, -reach, reach).astype(held_as)


def setup_inputs(seed: int = 0) -> dict:
    splits = jax.random.split(jax.random.key(seed), 12)
    return {
        "tokens": bell_draw(splits[0], (TOKENS, D), 1.0, 6.0, ((0, 32),)),
        "memory": bell_draw(splits[1], (SOURCES, D), 1.0, 6.0, ((0, 32),)),
        "w_wide": draw_w_wide(jax.random.fold_in(splits[11], 71), 0),
        "w_tall": draw_w_tall(jax.random.fold_in(splits[11], 71), 0),
        "vecs": draw_vecs(jax.random.fold_in(splits[11], 71), 0),
        "avg_wide": bell_draw(splits[5], (D, 8 * D + FF), D ** -0.5, 0.25, ((0, 32),), jnp.float32),
        "avg_tall": bell_draw(splits[6], (FF + 2 * D, D), FF ** -0.5, 0.125, ((0, 32),), jnp.float32),
        "avg_vecs": bell_draw(splits[7], (D, NVEC), 0.5, 3.0, ((0, 32),), jnp.float32),
        "tgt_lengths": jax.vmap(lambda own: ragged(own, SEGS, TOK_DEV, MAXLEN, 2))(jax.random.split(splits[8], DEVICES)).reshape((DEVICES, SEGS)).astype(jnp.int32),
        "src_lengths": jax.vmap(lambda own: ragged(own, SEGS, SRC_DEV, SRC_MOST, 2))(jax.random.split(splits[9], DEVICES)).reshape((DEVICES, SEGS)).astype(jnp.int32),
        "cotangent": bell_draw(splits[10], (TOKENS, D), 1.0, 6.0, ((0, 32),)),
    }


PRECISE = lax.Precision.HIGHEST
SCORE_SCALE = 0.125
EPSILON = 1e-05
MASKED = -1e+30

@jax.custom_vjp
def low(v):
    return lax.optimization_barrier(v.astype(jnp.bfloat16)).astype(jnp.float32)

@jax.custom_vjp
def low_back(v):
    return v

def low_keep(v):
    return (low(v), None)

def low_pass(kept, grad):
    return (grad,)

def back_keep(v):
    return (v, None)

def back_low(kept, grad):
    return (low(grad),)
low.defvjp(low_keep, low_pass)
low_back.defvjp(back_keep, back_low)

def segment_numbers(lengths, count):
    endings = jnp.cumsum(lengths.astype(jnp.int32))
    places = jnp.arange(count, dtype=jnp.int32)
    return lax.optimization_barrier(jnp.sum((places[:, None] >= endings[None, :]).astype(jnp.int32), axis=1)).astype(jnp.int32)

def matmul(left, right):
    return jnp.dot(left, right, precision=PRECISE)

def layer_norm(before, norm_gain, norm_shift):
    centred = before - lax.optimization_barrier(jnp.mean(before, axis=-1, keepdims=True))
    inverse = lax.rsqrt(lax.optimization_barrier(jnp.mean(centred * centred, axis=-1, keepdims=True)) + EPSILON)
    return centred * inverse * norm_gain + norm_shift

def attend(queries, keys_in, values_in, query_segment, key_segment):
    row_count = queries.shape[0]
    block_rows = min(512, row_count)
    blocks = row_count // block_rows
    key_heads = keys_in.reshape(keys_in.shape[0], HEADS, HEAD_DIM)
    value_heads = values_in.reshape(values_in.shape[0], HEADS, HEAD_DIM)

    def attend_block(pieces):
        query_block, segment_block = pieces
        scores = jnp.einsum('qhe,khe->hqk', query_block.reshape(block_rows, HEADS, HEAD_DIM), key_heads, precision=PRECISE)
        scores = low_back(scores * SCORE_SCALE)
        allowed = segment_block[:, None] == key_segment[None, :]
        scores = jnp.where(allowed[None], scores, MASKED)
        highest = lax.optimization_barrier(jnp.max(scores, axis=-1, keepdims=True))
        exponent = jnp.exp(scores - highest)
        shares = low(exponent / lax.optimization_barrier(jnp.sum(exponent, axis=-1, keepdims=True)))
        mixed = jnp.einsum('hqk,khe->qhe', shares, value_heads, precision=PRECISE)
        return mixed.reshape(block_rows, HEADS * HEAD_DIM)
    outputs = lax.map(jax.checkpoint(attend_block), (queries.reshape(blocks, block_rows, -1), query_segment.reshape(blocks, block_rows)))
    return outputs.reshape(row_count, -1)

def block_forward(wide_all, tall_all, vectors, token_rows, memory_rows, target_segment, source_segment):
    spread = FF // D
    offset = 6 + spread
    columns = [wide_all[:, index * D:(index + 1) * D] for index in range(8)]
    target_query, target_key, target_value, target_output = (columns[0], columns[1], columns[2], columns[3])
    source_query, source_key, source_value, source_output = (columns[4], columns[5], columns[6], columns[7])
    up_weight = wide_all[:, 8 * D:]
    down_weight = tall_all[:FF]
    slot_left = tall_all[FF:FF + D]
    slot_right = tall_all[FF + D:]
    up_bias = vectors[:, 6:offset].T.reshape(FF)
    valid_rows = (target_segment < SEGS - 1).astype(jnp.float32)[:, None]
    follow = (jnp.concatenate([target_segment[1:], jnp.full((1,), -1, jnp.int32)]) == target_segment).astype(jnp.float32)[:, None]
    queries_self = low(low_back(matmul(token_rows, target_query)) + vectors[:, 0])
    keys_self = low(low_back(matmul(token_rows, target_key)))
    values_self = low(low_back(matmul(token_rows, target_value)) + vectors[:, 1])
    mixed_self = low(low_back(attend(queries_self, keys_self, values_self, target_segment, target_segment)))
    first = layer_norm(token_rows + low_back(matmul(mixed_self, target_output)) + vectors[:, 2], vectors[:, offset + 2], vectors[:, offset + 3])
    first_low = low(first)
    queries_cross = low(low_back(matmul(first_low, source_query)) + vectors[:, 3])
    keys_cross = low(low_back(matmul(memory_rows, source_key)))
    values_cross = low(low_back(matmul(memory_rows, source_value)) + vectors[:, 4])
    mixed_cross = low(low_back(attend(queries_cross, keys_cross, values_cross, target_segment, source_segment)))
    second = layer_norm(first + low_back(matmul(mixed_cross, source_output)) + vectors[:, 5], vectors[:, offset + 4], vectors[:, offset + 5])
    second_low = low(second)
    hidden = low_back(matmul(second_low, up_weight)) + up_bias
    active = low(jax.nn.gelu(hidden))
    third = layer_norm(second + low_back(matmul(active, down_weight)) + vectors[:, offset], vectors[:, offset + 6], vectors[:, offset + 7])
    third_low = low(third)
    right_half = jnp.concatenate([third_low[1:], jnp.zeros((1, D), jnp.float32)]) * follow
    return (matmul(third_low, slot_left) + matmul(right_half, slot_right) + vectors[:, offset + 1]) * valid_rows

def reference(tokens, memory, w_wide, w_tall, vecs, avg_wide, avg_tall, avg_vecs, tgt_lengths, src_lengths, cotangent):
    wide_all = w_wide.astype(jnp.float32)
    tall_all = w_tall.astype(jnp.float32)
    vectors = vecs.astype(jnp.float32)
    token_blocks = tokens.astype(jnp.float32).reshape(DEVICES, TOK_DEV, D)
    memory_blocks = memory.astype(jnp.float32).reshape(DEVICES, SRC_DEV, D)
    seed_blocks = cotangent.astype(jnp.float32).reshape(DEVICES, TOK_DEV, D)

    def device_block(carried, pieces):
        sum_wide, sum_tall, sum_vectors = carried
        token_rows, memory_rows, target_lengths, source_lengths, seed_rows = pieces
        target_segment = segment_numbers(target_lengths, TOK_DEV)
        source_segment = segment_numbers(source_lengths, SRC_DEV)

        def forward(wide_in, tall_in, vectors_in, token_in, memory_in):
            return block_forward(wide_in, tall_in, vectors_in, token_in, memory_in, target_segment, source_segment)
        slot_rows, pull = jax.vjp(forward, wide_all, tall_all, vectors, token_rows, memory_rows)
        grad_wide_block, grad_tall_block, grad_vector_block, grad_token_block, grad_memory_block = pull(seed_rows)
        carried = (sum_wide + grad_wide_block, sum_tall + grad_tall_block, sum_vectors + grad_vector_block)
        return (carried, (slot_rows.astype(jnp.bfloat16), grad_token_block, grad_memory_block))
    start = (jnp.zeros(wide_all.shape, jnp.float32), jnp.zeros(tall_all.shape, jnp.float32), jnp.zeros(vectors.shape, jnp.float32))
    totals, outputs = lax.scan(device_block, start, (token_blocks, memory_blocks, tgt_lengths, src_lengths, seed_blocks))
    slots = outputs[0].reshape(TOKENS, D)
    grad_tokens = outputs[1].reshape(TOKENS, D)
    grad_memory = outputs[2].reshape(SOURCES, D)
    new_avg_wide = avg_wide + (wide_all - avg_wide) / AVG_STEPS
    new_avg_tall = avg_tall + (tall_all - avg_tall) / AVG_STEPS
    new_avg_vecs = avg_vecs + (vectors - avg_vecs) / AVG_STEPS
    return (slots, grad_tokens, grad_memory, totals[0], totals[1], totals[2], new_avg_wide, new_avg_tall, new_avg_vecs)
```

```python
import types

import jax
import jax.numpy as jnp
from jax import lax
from jax.experimental import pallas as pl
from jax.experimental.pallas import tpu as pltpu
from jax.sharding import PartitionSpec as P

D = 512
HEADS = 8
HEAD_DIM = 64
FF = 2048
SEGS = 6
AVG_STEPS = 4


SCORE_SCALE = 0.125
EPSILON = 1e-05
MASKED = -1e30


def matmul(left, right):
    return jnp.dot(left, right, preferred_element_type=jnp.float32)


def matmul_first(left, right):
    return lax.dot_general(
        left, right, (((0,), (0,)), ((), ())), preferred_element_type=jnp.float32
    )


def matmul_last(left, right):
    return lax.dot_general(
        left, right, (((1,), (1,)), ((), ())), preferred_element_type=jnp.float32
    )


def segment_numbers(lengths, count):
    endings = jnp.cumsum(lengths)
    places = jnp.arange(count, dtype=jnp.int32)
    return jnp.sum((places[:, None] >= endings[None, :]).astype(jnp.int32), axis=1)


def norm_forward(before, norm_gain, norm_shift):
    centred = before - jnp.mean(before, axis=-1, keepdims=True)
    inverse = lax.rsqrt(jnp.mean(centred * centred, axis=-1, keepdims=True) + EPSILON)
    normed = centred * inverse
    return (normed * norm_gain + norm_shift, normed, inverse)


def norm_backward(gradient, normed, inverse, norm_gain):
    scaled = gradient * norm_gain
    inner_sum = jnp.mean(scaled * normed, axis=-1, keepdims=True)
    before_grad = inverse * (scaled - jnp.mean(scaled, axis=-1, keepdims=True) - normed * inner_sum)
    return (before_grad, jnp.sum(gradient * normed, axis=0), jnp.sum(gradient, axis=0))


def split_heads(matrix):
    return matrix.reshape(matrix.shape[0], HEADS, HEAD_DIM)


def masked_scores(query_block, key_heads, segment_block, key_segment):
    scores = (
        jnp.einsum(
            "qhe,khe->hqk", split_heads(query_block), key_heads, preferred_element_type=jnp.float32
        )
        * SCORE_SCALE
    )
    allowed = segment_block[:, None] == key_segment[None, :]
    return jnp.where(allowed[None], scores, MASKED)


def attend_forward(queries, keys_in, values_in, query_segment, key_segment):
    row_count = queries.shape[0]
    block_rows = min(512, row_count)
    blocks = row_count // block_rows
    key_heads = split_heads(keys_in)
    value_heads = split_heads(values_in)

    def attend_block(pieces):
        query_block, segment_block = pieces
        scores = masked_scores(query_block, key_heads, segment_block, key_segment)
        highest = jnp.max(scores, axis=-1, keepdims=True)
        exponent = jnp.exp(scores - highest)
        totals = jnp.sum(exponent, axis=-1, keepdims=True)
        shares = (exponent / totals).astype(jnp.bfloat16)
        mixed = jnp.einsum("hqk,khe->qhe", shares, value_heads, preferred_element_type=jnp.float32)
        return (
            mixed.reshape(block_rows, HEADS * HEAD_DIM).astype(jnp.bfloat16),
            (highest + jnp.log(totals))[..., 0],
        )

    mixed, logsum = lax.map(
        attend_block,
        (queries.reshape(blocks, block_rows, -1), query_segment.reshape(blocks, block_rows)),
    )
    return (mixed.reshape(row_count, -1), logsum)


def attend_backward(queries, keys_in, values_in, mixed_grad, logsum, query_segment, key_segment):
    row_count = queries.shape[0]
    block_rows = min(512, row_count)
    blocks = row_count // block_rows
    key_heads = split_heads(keys_in)
    value_heads = split_heads(values_in)

    def backward_block(carried, pieces):
        key_sum, value_sum = carried
        query_block, grad_block, logsum_block, segment_block = pieces
        scores = masked_scores(query_block, key_heads, segment_block, key_segment)
        shares = jnp.exp(scores - logsum_block[..., None])
        grad_heads = split_heads(grad_block)
        share_grad = jnp.einsum(
            "qhe,khe->hqk", grad_heads, value_heads, preferred_element_type=jnp.float32
        )
        inner_sum = jnp.sum(shares * share_grad, axis=-1, keepdims=True)
        score_grad = (shares * (share_grad - inner_sum)).astype(jnp.bfloat16)
        query_grad = (
            jnp.einsum("hqk,khe->qhe", score_grad, key_heads, preferred_element_type=jnp.float32)
            * SCORE_SCALE
        )
        key_sum = (
            key_sum
            + jnp.einsum(
                "hqk,qhe->khe",
                score_grad,
                split_heads(query_block),
                preferred_element_type=jnp.float32,
            )
            * SCORE_SCALE
        )
        value_sum = value_sum + jnp.einsum(
            "hqk,qhe->khe",
            shares.astype(jnp.bfloat16),
            grad_heads,
            preferred_element_type=jnp.float32,
        )
        return ((key_sum, value_sum), query_grad.reshape(block_rows, HEADS * HEAD_DIM))

    zeros_init = jnp.zeros((keys_in.shape[0], HEADS, HEAD_DIM), jnp.float32)
    pieces = (
        queries.reshape(blocks, block_rows, -1),
        mixed_grad.reshape(blocks, block_rows, -1),
        logsum,
        query_segment.reshape(blocks, block_rows),
    )
    (key_sum, value_sum), query_grad = lax.scan(backward_block, (zeros_init, zeros_init), pieces)
    return (
        query_grad.reshape(row_count, -1),
        key_sum.reshape(keys_in.shape[0], -1),
        value_sum.reshape(values_in.shape[0], -1),
    )


def plain_body(
    tokens,
    memory,
    w_wide,
    w_tall,
    vecs,
    avg_wide,
    avg_tall,
    avg_vecs,
    tgt_lengths,
    src_lengths,
    cotangent,
):
    wide_all, tall_all, vector_all = (
        lax.all_gather(w_wide, ("wide", "narrow"), axis=0, tiled=True),
        lax.all_gather(w_tall, ("wide", "narrow"), axis=0, tiled=True),
        lax.all_gather(vecs, ("wide", "narrow"), axis=0, tiled=True),
    )
    vectors = vector_all.astype(jnp.float32)
    spread = FF // D
    offset = 6 + spread
    columns = [wide_all[:, index * D : (index + 1) * D] for index in range(8)]
    target_query, target_key, target_value, target_output = (
        columns[0],
        columns[1],
        columns[2],
        columns[3],
    )
    source_query, source_key, source_value, source_output = (
        columns[4],
        columns[5],
        columns[6],
        columns[7],
    )
    up_weight = wide_all[:, 8 * D :]
    down_weight = tall_all[:FF]
    slot_left = tall_all[FF : FF + D]
    slot_right = tall_all[FF + D :]
    up_bias = vectors[:, 6:offset].T.reshape(FF)
    row_count = tokens.shape[0]
    target_segment = segment_numbers(tgt_lengths[0], row_count)
    source_segment = segment_numbers(src_lengths[0], memory.shape[0])
    valid_rows = (target_segment < SEGS - 1).astype(jnp.float32)[:, None]
    follow = (
        jnp.concatenate([target_segment[1:], jnp.full((1,), -1, jnp.int32)]) == target_segment
    ).astype(jnp.float32)[:, None]
    queries_self = (matmul(tokens, target_query) + vectors[:, 0]).astype(jnp.bfloat16)
    keys_self = matmul(tokens, target_key).astype(jnp.bfloat16)
    values_self = (matmul(tokens, target_value) + vectors[:, 1]).astype(jnp.bfloat16)
    mixed_self, logsum_self = attend_forward(
        queries_self, keys_self, values_self, target_segment, target_segment
    )
    first, normed_first, inverse_first = norm_forward(
        tokens.astype(jnp.float32) + matmul(mixed_self, target_output) + vectors[:, 2],
        vectors[:, offset + 2],
        vectors[:, offset + 3],
    )
    first_low = first.astype(jnp.bfloat16)
    queries_cross = (matmul(first_low, source_query) + vectors[:, 3]).astype(jnp.bfloat16)
    keys_cross = matmul(memory, source_key).astype(jnp.bfloat16)
    values_cross = (matmul(memory, source_value) + vectors[:, 4]).astype(jnp.bfloat16)
    mixed_cross, logsum_cross = attend_forward(
        queries_cross, keys_cross, values_cross, target_segment, source_segment
    )
    second, normed_second, inverse_second = norm_forward(
        first + matmul(mixed_cross, source_output) + vectors[:, 5],
        vectors[:, offset + 4],
        vectors[:, offset + 5],
    )
    second_low = second.astype(jnp.bfloat16)
    hidden = matmul(second_low, up_weight) + up_bias
    active = jax.nn.gelu(hidden).astype(jnp.bfloat16)
    third, normed_third, inverse_third = norm_forward(
        second + matmul(active, down_weight) + vectors[:, offset],
        vectors[:, offset + 6],
        vectors[:, offset + 7],
    )
    third_low = third.astype(jnp.bfloat16)
    right_half = jnp.concatenate([third_low[1:], jnp.zeros((1, D), jnp.bfloat16)]) * follow.astype(
        jnp.bfloat16
    )
    slots = (
        (matmul(third_low, slot_left) + matmul(right_half, slot_right) + vectors[:, offset + 1])
        * valid_rows
    ).astype(jnp.bfloat16)
    seed_grad = cotangent * valid_rows.astype(jnp.bfloat16)
    grad_slot_bias = jnp.sum(seed_grad.astype(jnp.float32), axis=0)
    grad_left = matmul_first(third_low, seed_grad)
    grad_right = matmul_first(right_half, seed_grad)
    right_back = matmul_last(seed_grad, slot_right) * follow
    grad_third = matmul_last(seed_grad, slot_left) + jnp.concatenate(
        [jnp.zeros((1, D), jnp.float32), right_back[:-1]]
    )
    grad_pre_third, grad_gain_third, grad_shift_third = norm_backward(
        grad_third, normed_third, inverse_third, vectors[:, offset + 6]
    )
    pre_third_low = grad_pre_third.astype(jnp.bfloat16)
    grad_down = matmul_first(active, pre_third_low)
    grad_tall_all = jnp.concatenate([grad_down, grad_left, grad_right], axis=0)
    gelu_value, gelu_pull = jax.vjp(jax.nn.gelu, hidden)
    grad_hidden = gelu_pull(matmul_last(pre_third_low, down_weight))[0]
    hidden_low = grad_hidden.astype(jnp.bfloat16)
    grad_up = matmul_first(second_low, hidden_low)
    grad_second = grad_pre_third + matmul_last(hidden_low, up_weight)
    grad_pre_second, grad_gain_second, grad_shift_second = norm_backward(
        grad_second, normed_second, inverse_second, vectors[:, offset + 4]
    )
    pre_second_low = grad_pre_second.astype(jnp.bfloat16)
    grad_source_output = matmul_first(mixed_cross, pre_second_low)
    mixed_cross_grad = matmul_last(pre_second_low, source_output).astype(jnp.bfloat16)
    cross_query_grad, cross_key_grad, cross_value_grad = attend_backward(
        queries_cross,
        keys_cross,
        values_cross,
        mixed_cross_grad,
        logsum_cross,
        target_segment,
        source_segment,
    )
    cross_query_low = cross_query_grad.astype(jnp.bfloat16)
    cross_key_low = cross_key_grad.astype(jnp.bfloat16)
    cross_value_low = cross_value_grad.astype(jnp.bfloat16)
    grad_source_query = matmul_first(first_low, cross_query_low)
    grad_source_key = matmul_first(memory, cross_key_low)
    grad_source_value = matmul_first(memory, cross_value_low)
    grad_memory = matmul_last(cross_key_low, source_key) + matmul_last(
        cross_value_low, source_value
    )
    grad_first = grad_pre_second + matmul_last(cross_query_low, source_query)
    grad_pre_first, grad_gain_first, grad_shift_first = norm_backward(
        grad_first, normed_first, inverse_first, vectors[:, offset + 2]
    )
    pre_first_low = grad_pre_first.astype(jnp.bfloat16)
    grad_target_output = matmul_first(mixed_self, pre_first_low)
    mixed_self_grad = matmul_last(pre_first_low, target_output).astype(jnp.bfloat16)
    self_query_grad, self_key_grad, self_value_grad = attend_backward(
        queries_self,
        keys_self,
        values_self,
        mixed_self_grad,
        logsum_self,
        target_segment,
        target_segment,
    )
    self_query_low = self_query_grad.astype(jnp.bfloat16)
    self_key_low = self_key_grad.astype(jnp.bfloat16)
    self_value_low = self_value_grad.astype(jnp.bfloat16)
    grad_target_query = matmul_first(tokens, self_query_low)
    grad_target_key = matmul_first(tokens, self_key_low)
    grad_target_value = matmul_first(tokens, self_value_low)
    grad_tokens = (
        grad_pre_first
        + matmul_last(self_query_low, target_query)
        + matmul_last(self_key_low, target_key)
        + matmul_last(self_value_low, target_value)
    )
    grad_wide_all = jnp.concatenate(
        [
            grad_target_query,
            grad_target_key,
            grad_target_value,
            grad_target_output,
            grad_source_query,
            grad_source_key,
            grad_source_value,
            grad_source_output,
            grad_up,
        ],
        axis=1,
    )
    bias_front = jnp.stack(
        [
            jnp.sum(self_query_grad, axis=0),
            jnp.sum(self_value_grad, axis=0),
            jnp.sum(grad_pre_first, axis=0),
            jnp.sum(cross_query_grad, axis=0),
            jnp.sum(cross_value_grad, axis=0),
            jnp.sum(grad_pre_second, axis=0),
        ],
        axis=1,
    )
    bias_middle = jnp.sum(grad_hidden, axis=0).reshape(spread, D).T
    bias_back = jnp.stack(
        [
            jnp.sum(grad_pre_third, axis=0),
            grad_slot_bias,
            grad_gain_first,
            grad_shift_first,
            grad_gain_second,
            grad_shift_second,
            grad_gain_third,
            grad_shift_third,
        ],
        axis=1,
    )
    grad_vector_all = jnp.concatenate([bias_front, bias_middle, bias_back], axis=1)
    grad_wide, grad_tall, grad_vecs = (
        lax.psum_scatter(grad_wide_all, ("wide", "narrow"), scatter_dimension=0, tiled=True),
        lax.psum_scatter(grad_tall_all, ("wide", "narrow"), scatter_dimension=0, tiled=True),
        lax.psum_scatter(grad_vector_all, ("wide", "narrow"), scatter_dimension=0, tiled=True),
    )
    new_avg_wide = avg_wide + (w_wide.astype(jnp.float32) - avg_wide) / AVG_STEPS
    new_avg_tall = avg_tall + (w_tall.astype(jnp.float32) - avg_tall) / AVG_STEPS
    new_avg_vecs = avg_vecs + (vecs.astype(jnp.float32) - avg_vecs) / AVG_STEPS
    return (
        slots,
        grad_tokens,
        grad_memory,
        grad_wide,
        grad_tall,
        grad_vecs,
        new_avg_wide,
        new_avg_tall,
        new_avg_vecs,
    )


BF16 = jnp.bfloat16
F32 = jnp.float32
AUG = 80
BIG = 1e30
TILE = 256
MESH_IDS = pl.DeviceIdType.MESH
BIAS_OUT, GAIN = 10, 12
TALL_CUT = 3
OUT_SEMAPHORES = 24
PAIR = 6 * HEAD_DIM
GATHER_STEPS = {
    4: ((0, 0), (1, 0), (0, 1), (2, 0), (1, 1), (0, 2), (3, 0), (0, 3),),
    5: ((2, 1),),
    8: ((4, 0),),
    10: ((1, 2),),
    13: ((3, 1),),
    14: ((1, 3),),
    18: ((5, 0),),
    20: ((2, 2),),
    23: ((4, 1),),
    24: ((2, 3), (6, 0),),
    29: ((3, 2),),
    31: ((7, 0),),
    33: ((3, 3),),
    34: ((5, 1),),
    37: ((8, 0),),
    42: ((4, 2),),
    44: ((6, 1),),
    46: ((4, 3),),
    54: ((7, 1),),
    69: ((5, 2),),
    75: ((8, 1),),
    79: ((5, 3),),
    81: ((6, 2),),
    83: ((7, 2), (6, 3),),
    84: ((8, 2), (7, 3), (8, 3),),
}
SUM_STEPS = {
    2: ((0, 0), (1, 0),),
    3: ((2, 0),),
    7: ((0, 1),),
    8: ((3, 0),),
    9: ((4, 0), (1, 1),),
    10: ((5, 0), (2, 1),),
    11: ((0, 2),),
    12: ((3, 1),),
    13: ((4, 1),),
    14: ((0, 3),),
    15: ((1, 2), (5, 1),),
    16: ((2, 2),),
    17: ((3, 2),),
    19: ((4, 2),),
    20: ((5, 2),),
    21: ((1, 3),),
    23: ((7, 0), (2, 3),),
    24: ((6, 0), (3, 3),),
    25: ((4, 3), (7, 1),),
    26: ((5, 3), (8, 0),),
    27: ((6, 1), (7, 2),),
    28: ((9, 0), (8, 1),),
    29: ((6, 2), (10, 0),),
    30: ((7, 3), (9, 1),),
    31: ((8, 2), (10, 1),),
    33: ((6, 3), (11, 0),),
    34: ((9, 2),),
    36: ((10, 2), (8, 3), (11, 1), (9, 3), (10, 3), (11, 2), (11, 3),),
}


def dot(left, right, left_dim, right_dim):
    return lax.dot_general(
        left, right, (((left_dim,), (right_dim,)), ((), ())), preferred_element_type=F32
    )


def bands(query_rows, key_rows, longest):
    found = []
    for start in range(0, query_rows, TILE):
        if longest is None:
            found.append((0, key_rows))
            continue
        low = max(0, (start - longest + 1) // TILE * TILE)
        high = min(key_rows, -(-(start + TILE + longest - 1) // TILE) * TILE)
        found.append((low, high))
    return found


def column_max(scores):
    rows, columns = scores.shape
    return jnp.max(
        jnp.max(scores.reshape(rows // 64, 64, columns), axis=0), axis=0, keepdims=True
    )


def split_three(value):
    high = value.astype(BF16).astype(F32)
    middle = (value - high).astype(BF16).astype(F32)
    low = (value - high - middle).astype(BF16).astype(F32)
    return high, middle, low


def feature_rows(base, first, parts):
    place = lax.broadcasted_iota(jnp.int32, base.shape, 0)
    for step, part in enumerate(parts):
        base = jnp.where(place == first + step, part, base)
    return base


def gelu_pair(u):
    scale = 0.7978845608028654
    inner = jnp.tanh(scale * (u + 0.044715 * (u * u * u)))
    half = 0.5 * (1.0 + inner)
    slope = half + 0.5 * u * (1.0 - inner * inner) * (scale * (1.0 + 3 * 0.044715 * (u * u)))
    return u * half, slope


def normalize(before, gain, shift):
    centred = before - jnp.mean(before, axis=-1, keepdims=True)
    inverse = lax.rsqrt(jnp.mean(centred * centred, axis=-1, keepdims=True) + EPSILON)
    normed = centred * inverse
    return normed * gain + shift, normed, inverse


def attention_forward(queries, keys, values, mixed, scores, ranges, heads, hooks):
    tiles = len(ranges)

    def put(head, tile):
        low, high = ranges[tile]
        scores[tile % 2][0 : high - low, :] = dot(
            keys[head, :, low:high], queries[head, :, tile * TILE : (tile + 1) * TILE], 0, 0
        )

    put(heads[0], 0)

    def one_head(head, carried):
        for tile, (low, high) in enumerate(ranges):
            if tile + 1 < tiles:
                put(head, tile + 1)
            else:
                put(jnp.minimum(head + 1, heads[1] - 1), 0)
            span = slice(tile * TILE, (tile + 1) * TILE)
            current = scores[tile % 2][0 : high - low, :]
            highest = column_max(current)
            shares = jnp.exp(current - highest).astype(BF16)
            gathered = dot(values[head, :, low:high], shares, 1, 0)
            total = gathered[HEAD_DIM : HEAD_DIM + 1]
            rows = pl.ds(pl.multiple_of(head * HEAD_DIM, HEAD_DIM), HEAD_DIM)
            mixed[rows, span] = (gathered[:HEAD_DIM] * (1.0 / total)).astype(BF16)
            queries[head, HEAD_DIM:, span] = feature_rows(
                queries[head, HEAD_DIM:, span].astype(F32),
                SEGS,
                split_three(-(highest + jnp.log(total))),
            ).astype(BF16)
            for at, hook in hooks.items():
                if at[1] == tile:
                    pl.when(head == at[0])(hook)
        return carried

    lax.fori_loop(heads[0], heads[1], one_head, 0)


def attention_backward(queries, keys, values, grads, outs, sums, shares, score_grads, ranges, hooks):
    key_rows = keys.shape[2]
    key_sum, value_sum = sums
    tiles = len(ranges)

    def put(head, tile):
        low, high = ranges[tile]
        span = slice(tile * TILE, (tile + 1) * TILE)
        share = jnp.exp(dot(keys[head, :, low:high], queries[head, :, span], 0, 0))
        share_grad = dot(values[head, :, low:high], grads[head, :, span], 0, 0)
        shares[tile % 2][0 : high - low, :] = share.astype(BF16)
        score_grads[tile % 2][0 : high - low, :] = (share * share_grad).astype(BF16)

    put(0, 0)

    def one_head(head, carried):
        key_sum[:, 0:key_rows] = jnp.zeros((HEAD_DIM, key_rows), F32)
        value_sum[:, 0:key_rows] = jnp.zeros((HEAD_DIM, key_rows), F32)
        query_out, key_out, value_out = [out(head) for out in outs]
        for tile, (low, high) in enumerate(ranges):
            if tile + 1 < tiles:
                put(head, tile + 1)
            else:
                put(jnp.minimum(head + 1, HEADS - 1), 0)
            span = slice(tile * TILE, (tile + 1) * TILE)
            share = shares[tile % 2][0 : high - low, :]
            score_grad = score_grads[tile % 2][0 : high - low, :]
            query_out[:, span] = (
                dot(keys[head, 0:HEAD_DIM, low:high], score_grad, 1, 0) * SCORE_SCALE
            ).astype(BF16)
            key_sum[:, low:high] += dot(queries[head, 0:HEAD_DIM, span], score_grad, 1, 1)
            value_sum[:, low:high] += dot(grads[head, 0:HEAD_DIM, span], share, 1, 1)
        key_out[...] = key_sum[:, 0:key_rows].astype(BF16)
        value_out[...] = value_sum[:, 0:key_rows].astype(BF16)
        for at, hook in hooks.items():
            pl.when(head == at)(hook)
        return carried

    lax.fori_loop(0, HEADS, one_head, 0)


class Exchange:
    def __init__(self, wide, narrow):
        self.narrow_bits = narrow.bit_length() - 1
        self.count = (wide * narrow).bit_length() - 1
        self.line = 1 << (self.count - 3)
        self.place = (lax.axis_index("wide"), lax.axis_index("narrow"))
        number = self.place[0] * narrow + self.place[1]
        self.bits = [(number >> bit) & 1 for bit in range(self.count)]
        self.own = tuple(self.bits[bit] for bit in reversed(range(self.count)))
        self.far = list(range(3, self.count))
        self.masks = [1, 2, 4] + [other << 3 for other in range(1, self.line)]

    def device(self, mask):
        wide, narrow = self.place
        return (wide ^ (mask >> self.narrow_bits), narrow ^ (mask & ((1 << self.narrow_bits) - 1)))

    def greet(self):
        barrier = pltpu.get_barrier_semaphore()
        for mask in self.masks:
            pl.semaphore_signal(
                barrier, inc=1, device_id=self.device(mask), device_id_type=MESH_IDS
            )

    def meet(self):
        pl.semaphore_wait(pltpu.get_barrier_semaphore(), len(self.masks))

    def by_core(self, split, act):
        if split:
            pl.when(self.bits[0] == 0)(lambda: act((1, 2)))
            pl.when(self.bits[0] == 1)(lambda: act((2, 1)))
        else:
            act((1, 2))

    def view(self, part, open_bits, flipped=0):
        index = tuple(
            slice(None)
            if bit in open_bits
            else (1 - self.bits[bit] if flipped >> bit & 1 else self.bits[bit])
            for bit in reversed(range(self.count))
        )
        return part.ref.at[index + part.where]


class Part:
    def __init__(self, ref, rows=None, columns=None, buffers=(), outs=()):
        cut = lambda ends: slice(None) if ends is None else pl.ds(ends[0], ends[1] - ends[0])
        self.ref, self.where, self.buffers, self.outs = ref, (cut(rows), cut(columns)), buffers, outs


class Transfer:
    def __init__(self, net, pieces, send, receive):
        self.net, self.pieces, self.send, self.receive = net, pieces, send, receive

    def copy(self, piece, part, slot, source, target, mask):
        return pltpu.make_async_remote_copy(
            source,
            target,
            self.send.at[piece, slot, part],
            self.receive.at[piece, slot, part],
            device_id=self.net.device(mask),
            device_id_type=MESH_IDS,
        )

    def finish(self):
        for piece in range(len(self.pieces)):
            for stage in range(4):
                self.each(piece, stage, lambda copy: copy.wait_send())


class Gather(Transfer):
    def each(self, piece, stage, act):
        net = self.net

        def with_order(near):
            first, second = near
            for number, part in enumerate(self.pieces[piece]):
                if stage == 0:
                    for other in range(1, net.line):
                        view = net.view(part, [])
                        act(self.copy(piece, number, other + 3, view, view, other << 3))
                elif stage == 1:
                    view = net.view(part, net.far)
                    act(self.copy(piece, number, 0, view, view, 1 << first))
                elif stage == 2:
                    view = net.view(part, net.far)
                    act(self.copy(piece, number, 1, view, view, 1 << second))
                    view = net.view(part, net.far, 1 << first)
                    act(self.copy(piece, number, 2, view, view, 1 << second))
                else:
                    view = net.view(part, net.far + [1, 2])
                    act(self.copy(piece, number, 3, view, view, 1))

        net.by_core(stage in (1, 2), with_order)

    def start(self, piece):
        if piece < len(self.pieces):
            self.each(piece, 0, lambda copy: copy.start())

    def step(self, piece, stage):
        net = self.net
        self.each(piece, stage, lambda copy: copy.wait_recv())
        if stage == 0:
            self.each(piece, 1, lambda copy: copy.start())
            self.send_second(piece, 0)
            self.start(piece + 2)
        elif stage == 1:
            self.send_second(piece, 1)
        elif stage == 2:
            self.each(piece, 3, lambda copy: copy.start())

    def send_second(self, piece, which):
        net = self.net

        def with_order(near):
            first, second = near
            for number, part in enumerate(self.pieces[piece]):
                view = net.view(part, net.far, which << first)
                self.copy(piece, number, 1 + which, view, view, 1 << second).start()

        net.by_core(True, with_order)


class Sum(Transfer):
    def each(self, piece, stage, act):
        net = self.net

        def with_order(near):
            first, second = near
            for number, part in enumerate(self.pieces[piece]):
                arrive = part.buffers
                if stage == 0:
                    view = net.view(part, net.far + [1, 2], 1)
                    act(self.copy(piece, number, 0, view, arrive[0], 1))
                elif stage == 1:
                    view = net.view(part, net.far, (1 << first) | (1 << second))
                    act(self.copy(piece, number, 1, view, arrive[1], 1 << second))
                elif stage == 2:
                    view = net.view(part, net.far, 1 << second)
                    act(self.copy(piece, number, 2, view, arrive[2], 1 << second))
                    view = net.view(part, net.far, 1 << first)
                    act(self.copy(piece, number, 3, view, arrive[3], 1 << first))
                else:
                    for other in range(1, net.line):
                        view = net.view(part, [], other << 3)
                        act(self.copy(piece, number, other + 3, view, arrive[4].at[other - 1], other << 3))

        net.by_core(stage in (1, 2), with_order)

    def send_one(self, piece, which):
        net = self.net

        def with_order(near):
            bit = near[1 - which]
            for number, part in enumerate(self.pieces[piece]):
                view = net.view(part, net.far, 1 << bit)
                self.copy(
                    piece, number, 2 + which, view, part.buffers[2 + which], 1 << bit
                ).start()

        net.by_core(True, with_order)

    def start(self, piece):
        self.each(piece, 0, lambda copy: copy.start())

    def add(self, piece, stage):
        net = self.net

        def with_order(near):
            rest = sorted(net.far + ([1, 2] if stage == 0 else []))
            flipped = near[0] if stage == 1 else None

            def one_shard(step, carried):
                place = {bit: (step >> at) & 1 for at, bit in enumerate(rest)}
                index = tuple(
                    place[bit]
                    if bit in place
                    else (1 - net.bits[bit] if bit == flipped else net.bits[bit])
                    for bit in reversed(range(net.count))
                )
                arrived = tuple(place[bit] for bit in reversed(rest)) + (slice(None), slice(None))
                for part in self.pieces[piece]:
                    where = index + part.where
                    value = part.ref[where].astype(F32)
                    for buffer in part.buffers[2:4] if stage == 2 else part.buffers[stage : stage + 1]:
                        value = value + buffer[arrived].astype(F32)
                    part.ref[where] = value.astype(part.ref.dtype)
                return carried

            lax.fori_loop(0, 1 << len(rest), one_shard, 0)

        if stage < 3:
            net.by_core(stage == 1, with_order)
            return
        for part in self.pieces[piece]:
            value = part.ref[net.own + part.where].astype(F32)
            for other in range(1, net.line):
                value = value + part.buffers[4][other - 1].astype(F32)
            for low, high, staged, out, semaphore in part.outs:
                staged[...] = value[:, low:high]
                pltpu.make_async_copy(staged, out, semaphore).start()

    def step(self, piece, stage):
        self.each(piece, stage, lambda copy: copy.wait_recv())
        self.add(piece, stage)
        if stage == 0:
            self.each(piece, 1, lambda copy: copy.start())
            self.send_one(piece, 0)
        elif stage == 1:
            self.send_one(piece, 1)
        elif stage == 2:
            self.each(piece, 3, lambda copy: copy.start())

    def finish(self):
        super().finish()
        for piece in self.pieces:
            for part in piece:
                for _, _, staged, out, semaphore in part.outs:
                    pltpu.make_async_copy(staged, out, semaphore).wait()


class Plan:
    def __init__(self, transfer, table):
        self.transfer, self.table, self.stop = transfer, table, 0

    def next(self):
        taken = self.table.get(self.stop, ())
        self.stop += 1

        def act():
            for piece, stage in taken:
                self.transfer.step(piece, stage)

        return act if taken else None

    def now(self):
        act = self.next()
        if act:
            act()

    def loop(self, places):
        found = {place: self.next() for place in places}
        return {place: act for place, act in found.items() if act}


def layer_kernel(r, wide_size, narrow_size):
    net = Exchange(wide_size, narrow_size)
    net.greet()
    devices = wide_size * narrow_size
    wide7, tall7, vec7, gvec7 = r.wide, r.tall, r.vec, r.grad_vec
    wide = wide7.reshape(devices * wide7.shape[-2], wide7.shape[-1])
    tall = tall7.reshape(devices * tall7.shape[-2], tall7.shape[-1])
    slope7 = r.slope
    slope = slope7.reshape(devices * slope7.shape[-2], slope7.shape[-1])
    own_rows = (0, wide7.shape[-2])
    tokens, memory, seed, seed_next = r.tokens, r.memory, r.seed, r.seed_next
    rows, sources = tokens.shape[0], memory.shape[0]
    tiles = rows // TILE
    local = r.local

    wide_moves = [
        (block * D + pair * PAIR // 3, pair * PAIR + block * PAIR // 3, PAIR // 3)
        for pair in range(HEADS // 2)
        for block in range(3)
    ] + [(3 * D, 3 * D, wide7.shape[-1] - 3 * D)]
    loads = [
        pltpu.make_async_copy(
            r.w_wide.at[:, pl.ds(low, width)],
            wide7.at[net.own + (slice(None), pl.ds(high, width))],
            r.own_done.at[number],
        )
        for number, (low, high, width) in enumerate(wide_moves)
    ] + [
        pltpu.make_async_copy(r.w_tall, tall7.at[net.own], local.at[1]),
        pltpu.make_async_copy(r.vecs, vec7.at[net.own], local.at[2]),
        pltpu.make_async_copy(r.tokens_in, tokens, local.at[3]),
        pltpu.make_async_copy(r.memory_in, memory, local.at[4]),
        pltpu.make_async_copy(r.cotangent, seed, local.at[5]),
    ]
    for copy in loads:
        copy.start()

    tall_rows = tall7.shape[-2]
    tall_cuts = [(low, low + tall_rows // TALL_CUT) for low in range(0, tall_rows, tall_rows // TALL_CUT)]

    def wide_part(low, high):
        return [Part(wide7, None, (low, high))]

    gather = Gather(
        net,
        [
            wide_part(0, 2 * PAIR) + [Part(vec7)],
            wide_part(2 * PAIR, 4 * PAIR),
            wide_part(3 * D, 5 * D),
            wide_part(5 * D, 7 * D),
            wide_part(7 * D, 9 * D),
            wide_part(9 * D, 12 * D),
        ]
        + [[Part(tall7, cut)] for cut in tall_cuts],
        r.gather_send,
        r.gather_receive,
    )
    plan = Plan(gather, GATHER_STEPS)
    out_semaphores = iter(range(OUT_SEMAPHORES))

    def out_of(low, high, staged, out):
        return (low, high, staged, out, r.out_done.at[next(out_semaphores)])

    def wide_out(low, high, start):
        columns = pl.ds(start, high - low)
        return out_of(low, high, r.out_wide.at[:, columns], r.grad_wide.at[:, columns])

    def tall_sum(cut, buffers):
        place = pl.ds(cut[0], cut[1] - cut[0])
        out = out_of(0, D, r.out_tall.at[place, :], r.grad_tall.at[place, :])
        return [Part(tall7, cut, None, buffers, [out])]

    def wide_sum(low, high, buffers):
        return [Part(wide7, None, (low, high), buffers, [wide_out(0, high - low, low)])]

    def self_sum(pair):
        third = PAIR // 3
        outs = [
            wide_out(block * third, (block + 1) * third, block * D + pair * third)
            for block in range(3)
        ]
        buffers = [
            buffer.at[
                (slice(None),) * (len(buffer.shape) - 1) + (pl.ds(pair % 2 * PAIR, PAIR),)
            ]
            for buffer in r.in_wide[pair // 2]
        ]
        columns = (pair * PAIR, (pair + 1) * PAIR)
        return [Part(slope7, own_rows, columns, buffers, outs)]

    vec_sum = Part(gvec7, None, None, r.in_vec, [out_of(0, 128, r.out_vec, r.grad_vecs)])
    ranges_of_sum = ((8, 10), (10, 12), (7, 8), (3, 5), (5, 7))
    total = Sum(
        net,
        [tall_sum(cut, buffers) for cut, buffers in zip(tall_cuts, r.in_tall)]
        + [
            wide_sum(low * D, high * D, buffers)
            for (low, high), buffers in zip(ranges_of_sum, r.in_wide)
        ]
        + [self_sum(pair) + ([vec_sum] if pair == HEADS // 2 - 1 else []) for pair in range(HEADS // 2)],
        r.sum_send,
        r.sum_receive,
    )
    TALL, UP, OUT2, MID, KEYS2, SELF = 0, TALL_CUT, TALL_CUT + 2, TALL_CUT + 3, TALL_CUT + 4, TALL_CUT + 5
    sum_plan = Plan(total, SUM_STEPS)

    for copy in loads[:-3]:
        copy.wait()
    net.meet()
    gather.start(0)

    def endings(lengths):
        found, running = [], 0
        for index in range(SEGS):
            running = running + lengths[0, index]
            found.append(running)
        return found

    target_ends = endings(r.tgt_lengths)
    source_ends = endings(r.src_lengths)

    def chosen(ends, count):
        place = lax.broadcasted_iota(jnp.int32, (16, count), 1)
        segment = jnp.zeros((16, count), jnp.int32)
        for end in ends:
            segment = segment + (place >= end).astype(jnp.int32)
        return segment == lax.broadcasted_iota(jnp.int32, (16, count), 0)

    def query_features(ends, count):
        return jnp.where(chosen(ends, count), 1.0, 0.0).astype(BF16)

    def key_features(ends, count):
        row = lax.broadcasted_iota(jnp.int32, (16, count), 0)
        masked = jnp.where(chosen(ends, count), 0.0, -BIG)
        return jnp.where(row < SEGS, masked, jnp.where(row < SEGS + 3, 1.0, 0.0)).astype(BF16)

    def value_features(count):
        row = lax.broadcasted_iota(jnp.int32, (16, count), 0)
        return jnp.where(row < 3, 1.0, 0.0).astype(BF16)

    def every_head(ref, features):
        ref[:, HEAD_DIM:, :] = jnp.broadcast_to(features[None], (HEADS,) + features.shape)

    q, k, v, q2, k2, v2 = r.q, r.k, r.v, r.q2, r.k2, r.v2
    every_head(q, query_features(target_ends, rows))
    every_head(q2, query_features(target_ends, rows))
    every_head(k, key_features(target_ends, rows))
    every_head(k2, key_features(source_ends, sources))
    gather.start(1)
    plan.now()
    every_head(v, value_features(rows))
    every_head(v2, value_features(sources))
    plan.now()

    def position(tile):
        return tile * TILE + lax.broadcasted_iota(jnp.int32, (TILE, 1), 0)

    def valid(tile):
        return jnp.where(position(tile) < target_ends[SEGS - 2], 1.0, 0.0)

    def follow(tile):
        after = position(tile) + 1
        ended = after == target_ends[0]
        for end in target_ends[1:]:
            ended = ended | (after == end)
        return jnp.where(ended, 0.0, 1.0)

    def span(tile):
        return pl.ds(tile * TILE, TILE)

    shift, res = r.shift, r.res
    loads[-1].wait()
    shift[0:8, :] = jnp.zeros((8, D), F32)
    for tile in range(tiles):
        masked = seed[span(tile), :].astype(F32) * valid(tile)
        seed[span(tile), :] = masked.astype(BF16)
        shift[pl.ds(tile * TILE + 8, TILE), :] = masked * follow(tile)
    plan.now()
    for tile in range(tiles):
        seed_next[span(tile), :] = shift[pl.ds(tile * TILE + 7, TILE), :].astype(BF16)
    shift[rows : rows + 8, :] = jnp.zeros((8, D), F32)
    r.grad_rows[...] = jnp.zeros_like(r.grad_rows)
    r.grad_columns[...] = jnp.zeros_like(r.grad_columns)
    loads[-3].wait()
    loads[-2].wait()
    plan.now()

    def row(index):
        return r.row_vectors[index : index + 1, :]

    def column(index):
        return vec7[...].reshape(D, vec7.shape[-1])[:, index : index + 1].astype(F32)

    def heads_of(value):
        return value.reshape(value.shape[0] // HEAD_DIM, HEAD_DIM, value.shape[1])

    def scaled(value):
        return (value.astype(BF16).astype(F32) * SCORE_SCALE).astype(BF16)

    def wide_column(index):
        return wide[:, index * D : (index + 1) * D]

    self_ranges = bands(rows, rows, 512)
    cross_ranges = bands(rows, sources, None)
    a, a2 = r.mixed, r.mixed2
    halves = [(index * HEADS // 2, (index + 1) * HEADS // 2) for index in range(2)]

    bias_rows = PAIR // 3
    identity = lax.broadcasted_iota(jnp.int32, (D, D), 0) == lax.broadcasted_iota(
        jnp.int32, (D, D), 1
    )
    identity = jnp.where(identity, 1.0, 0.0).astype(BF16)
    for index, heads in enumerate(halves):
        plan.now()
        if index == 0:
            r.row_vectors[0 : vec7.shape[-1], :] = dot(
                vec7[...].reshape(D, vec7.shape[-1]), identity, 0, 0
            )
        columns = slice(2 * index * PAIR, 2 * (index + 1) * PAIR)
        biases = []
        for pair in (2 * index, 2 * index + 1):
            place = slice(pair * bias_rows, (pair + 1) * bias_rows)
            biases += [column(0)[place], jnp.zeros((bias_rows, 1), F32), column(1)[place]]
        bias = jnp.concatenate(biases, axis=0)
        for tile in range(tiles):
            both = (dot(wide[:, columns], tokens[span(tile), :], 0, 1) + bias).astype(BF16)
            for pair in range(2):
                group = slice(heads[0] + 2 * pair, heads[0] + 2 * pair + 2)
                for block, ref in enumerate((q, k, v)):
                    start = pair * PAIR + block * bias_rows
                    value = both[start : start + bias_rows]
                    if block == 0:
                        value = (value.astype(F32) * SCORE_SCALE).astype(BF16)
                    ref[group, 0:HEAD_DIM, span(tile)] = heads_of(value)
        plan.now()
        attention_forward(
            q,
            k,
            v,
            a,
            r.scores,
            self_ranges,
            heads,
            plan.loop([(head, tile) for head in range(*heads) for tile in range(tiles)]),
        )

    normed, low, inverse = r.normed, r.low, r.inverse

    def norm_tile(index, tile, before):
        out, unit, rho = normalize(before, row(GAIN + 2 * index), row(GAIN + 2 * index + 1))
        normed[index][span(tile), :] = unit.astype(BF16)
        inverse[span(tile), index : index + 1] = rho
        low[index][span(tile), :] = out.astype(BF16)
        return out

    plan.now()
    for tile in range(tiles):
        before = (
            tokens[span(tile), :].astype(F32) + dot(a[:, span(tile)], wide_column(3), 0, 0) + row(2)
        )
        out = norm_tile(0, tile, before)
        res[span(tile), :] = out
        q2[:, 0:HEAD_DIM, span(tile)] = heads_of(
            scaled(dot(wide_column(4), out.astype(BF16), 0, 1) + column(3))
        )
        plan.now()
    plan.now()
    for tile in range(sources // TILE):
        part = memory[span(tile), :]
        k2[:, 0:HEAD_DIM, span(tile)] = heads_of(dot(wide_column(5), part, 0, 1).astype(BF16))
        v2[:, 0:HEAD_DIM, span(tile)] = heads_of(
            (dot(wide_column(6), part, 0, 1) + column(4)).astype(BF16)
        )
    attention_forward(
        q2,
        k2,
        v2,
        a2,
        r.scores,
        cross_ranges,
        (0, HEADS),
        plan.loop([(head, tile) for head in range(HEADS) for tile in range(tiles)]),
    )
    active = r.active
    plan.now()
    for tile in range(tiles):
        before = res[span(tile), :] + dot(a2[:, span(tile)], wide_column(7), 0, 0) + row(5)
        out = norm_tile(1, tile, before)
        res[span(tile), :] = out
        for block in range(FF // D):
            if tile == 0 and block == 1:
                plan.now()
            columns = slice(block * D, (block + 1) * D)
            u = dot(out.astype(BF16), wide_column(8 + block), 1, 0) + row(6 + block)
            value, derivative = gelu_pair(u)
            active[span(tile), columns] = value.astype(BF16)
            slope[span(tile), columns] = derivative.astype(BF16)
        plan.now()
    plan.now()
    slot_left = tall.at[pl.ds(FF, D), :]
    slot_right = tall.at[pl.ds(FF + D, D), :]
    for tile in range(tiles):
        before = (
            res[span(tile), :] + dot(active[span(tile), :], tall[0:FF, :], 1, 0) + row(BIAS_OUT)
        )
        out = norm_tile(2, tile, before).astype(BF16)
        shift[span(tile), :] = dot(out, slot_right[...], 1, 0)
    low_grad = r.low_grad
    slot_copies = []
    for tile in range(tiles):
        low_grad[span(tile), :] = (
            (
                dot(low[2][span(tile), :], slot_left[...], 1, 0)
                + follow(tile) * shift[pl.ds(tile * TILE + 1, TILE), :]
                + row(BIAS_OUT + 1)
            )
            * valid(tile)
        ).astype(BF16)
        copy = pltpu.make_async_copy(
            low_grad.at[span(tile), :], r.slots.at[span(tile), :], local.at[6 + tile]
        )
        copy.start()
        slot_copies.append(copy)
    gather.finish()

    grad_rows, grad_columns = r.grad_rows, r.grad_columns

    def add_row(index, value):
        grad_rows[index : index + 1, :] += jnp.sum(value, axis=0, keepdims=True)

    def norm_back(index, tile, gradient, bias_row):
        gain = row(GAIN + 2 * index)
        unit = normed[index][span(tile), :].astype(F32)
        scaled_grad = gradient * gain
        inner = jnp.mean(scaled_grad * unit, axis=-1, keepdims=True)
        before = inverse[span(tile), index : index + 1] * (
            scaled_grad - jnp.mean(scaled_grad, axis=-1, keepdims=True) - unit * inner
        )
        add_row(GAIN + 2 * index, gradient * unit)
        add_row(GAIN + 2 * index + 1, gradient)
        add_row(bias_row, before)
        res[span(tile), :] = before
        low_grad[span(tile), :] = before.astype(BF16)

    for tile in range(tiles):
        part = seed[span(tile), :]
        add_row(BIAS_OUT + 1, part.astype(F32))
        gradient = dot(part, slot_left[...], 1, 1) + dot(
            seed_next[span(tile), :], slot_right[...], 1, 1
        )
        slot_copies[tile].wait()
        norm_back(2, tile, gradient, BIAS_OUT)
    slot_left[...] = dot(low[2][...], seed[...], 0, 0).astype(BF16)
    slot_right[...] = dot(low[2][...], seed_next[...], 0, 0).astype(BF16)
    for block in range(FF // D):
        columns = slice(block * D, (block + 1) * D)
        for tile in range(tiles):
            grad = dot(low_grad[span(tile), :], tall[columns, :], 1, 1) * slope[
                span(tile), columns
            ].astype(F32)
            add_row(6 + block, grad)
            slope[span(tile), columns] = grad.astype(BF16)
        tall[columns, :] = dot(active[:, columns], low_grad[...], 0, 0).astype(BF16)
    for cut in range(TALL_CUT):
        total.start(TALL + cut)
    for tile in range(tiles):
        gradient = res[span(tile), :] + dot(
            slope[span(tile), :], wide[:, 8 * D : 8 * D + FF], 1, 1
        )
        norm_back(1, tile, gradient, 5)
        sum_plan.now()
    for block in range(FF // D):
        columns = slice(block * D, (block + 1) * D)
        wide[:, 8 * D + block * D : 8 * D + (block + 1) * D] = dot(
            low[1][...], slope[:, columns], 0, 0
        ).astype(BF16)
        if block % 2 == 1:
            total.start(UP + block // 2)
        sum_plan.now()
    grads = r.mixed_grad

    def mixed_back(weight_index, mixed):
        for tile in range(tiles):
            grad = dot(wide_column(weight_index), low_grad[span(tile), :], 1, 1).astype(BF16)
            grads[:, 0:HEAD_DIM, span(tile)] = heads_of(grad)
            inner = jnp.sum(
                heads_of(grad.astype(F32) * mixed[:, span(tile)].astype(F32)),
                axis=1,
                keepdims=True,
            )
            place = lax.broadcasted_iota(jnp.int32, (HEADS, 16, TILE), 1)
            features = jnp.zeros((HEADS, 16, TILE), F32)
            for step, part in enumerate(split_three(-inner)):
                features = jnp.where(place == step, part, features)
            grads[:, HEAD_DIM:, span(tile)] = features.astype(BF16)
        wide[:, weight_index * D : (weight_index + 1) * D] = dot(
            mixed[...], low_grad[...], 1, 0
        ).astype(BF16)

    mixed_back(7, a2)
    total.start(OUT2)
    sum_plan.now()
    dq2 = active.at[pl.ds(0, D), pl.ds(0, rows)]
    dk2 = active.at[pl.ds(D, D), pl.ds(0, sources)]
    dv2 = active.at[pl.ds(D, D), pl.ds(rows, sources)]

    def head_rows(ref):
        def of(head):
            return ref.at[pl.ds(pl.multiple_of(head * HEAD_DIM, HEAD_DIM), HEAD_DIM), :]

        return of

    sums = (r.key_sum, r.value_sum)
    attention_backward(
        q2,
        k2,
        v2,
        grads,
        [head_rows(ref) for ref in (dq2, dk2, dv2)],
        sums,
        r.shares,
        r.score_grads,
        cross_ranges,
        sum_plan.loop(range(HEADS)),
    )

    def column_sum(index, value):
        grad_columns[:, index : index + 1] += jnp.sum(value.astype(F32), axis=1, keepdims=True)

    for tile in range(tiles):
        gradient = res[span(tile), :] + dot(dq2[:, span(tile)], wide_column(4), 0, 1)
        norm_back(0, tile, gradient, 2)
        sum_plan.now()
    shift[0:sources, :] = dot(dk2[...], wide_column(5), 0, 1) + dot(dv2[...], wide_column(6), 0, 1)
    memory_copy = pltpu.make_async_copy(
        shift.at[pl.ds(0, sources), :], r.grad_memory, local.at[10]
    )
    memory_copy.start()
    wide[:, 5 * D : 6 * D] = dot(memory[...], dk2[...], 0, 1).astype(BF16)
    wide[:, 6 * D : 7 * D] = dot(memory[...], dv2[...], 0, 1).astype(BF16)
    total.start(KEYS2)
    sum_plan.now()
    wide[:, 4 * D : 5 * D] = dot(low[0][...], dq2[...], 0, 1).astype(BF16)
    column_sum(3, dq2[...])
    column_sum(4, dv2[...])
    mixed_back(3, a)
    total.start(MID)
    sum_plan.now()

    def pair_rows(block):
        def of(head):
            pair = head // 2
            row = pair % 2 * PAIR + block * (PAIR // 3) + head % 2 * HEAD_DIM
            start = pl.multiple_of(pair // 2 * rows, rows)
            return active.at[pl.ds(pl.multiple_of(row, HEAD_DIM), HEAD_DIM), pl.ds(start, rows)]

        return of

    def pair_grad(pair):
        return active[pair % 2 * PAIR : (pair % 2 + 1) * PAIR, pair // 2 * rows : (pair // 2 + 1) * rows]

    def start_pair(pair):
        where = (slice(None),) * net.count + (
            slice(0, own_rows[1]),
            slice(pair * PAIR, (pair + 1) * PAIR),
        )
        slope7[where] = (
            dot(tokens[...], pair_grad(pair), 0, 1)
            .astype(BF16)
            .reshape(slope7.shape[: net.count] + (own_rows[1], PAIR))
        )
        if pair == HEADS // 2 - 1:
            for other in range(HEADS // 2):
                place = slice(other * bias_rows, (other + 1) * bias_rows)
                grad = pair_grad(other).astype(F32)
                for index, block in ((0, 0), (1, 2)):
                    grad_columns[place, index : index + 1] = jnp.sum(
                        grad[block * bias_rows : (block + 1) * bias_rows], axis=1, keepdims=True
                    )
            turned = jnp.transpose(r.grad_rows[...]) + grad_columns[...]
            gvec7[...] = turned.reshape(gvec7.shape)
        total.start(SELF + pair)

    hooks = {}
    for head in range(HEADS):
        act = sum_plan.next()

        def hook(head=head, act=act):
            if head % 2 and head < HEADS - 1:
                start_pair(head // 2)
            if act:
                act()

        if act or (head % 2 and head < HEADS - 1):
            hooks[head] = hook
    attention_backward(
        q,
        k,
        v,
        grads,
        [pair_rows(block) for block in range(3)],
        sums,
        r.shares,
        r.score_grads,
        self_ranges,
        hooks,
    )
    start_pair(HEADS // 2 - 1)
    sum_plan.now()
    token_copies = []
    for tile in range(tiles):
        value = res[span(tile), :]
        for side in range(2):
            value = value + dot(
                active[0 : 2 * PAIR, pl.ds(side * rows + tile * TILE, TILE)],
                wide[:, 2 * side * PAIR : 2 * (side + 1) * PAIR],
                0,
                1,
            )
        res[span(tile), :] = value
        copy = pltpu.make_async_copy(
            res.at[span(tile), :], r.grad_tokens.at[span(tile), :], local.at[12 + tile]
        )
        copy.start()
        token_copies.append(copy)
        sum_plan.now()
    sum_plan.now()
    total.finish()
    for copy in token_copies + [memory_copy]:
        copy.wait()


def finish_kernel(*refs):
    given, results, held = refs[:12], refs[12:21], refs[21:33]
    vec_out, semaphores = refs[33], refs[34]
    loads = [
        pltpu.make_async_copy(source, target, semaphores.at[index])
        for index, (source, target) in enumerate(zip(given, held))
    ]
    for copy in loads:
        copy.start()
    stores = []

    def store(index, source):
        copy = pltpu.make_async_copy(source, results[index], semaphores.at[12 + index])
        copy.start()
        stores.append(copy)

    for index in range(12):
        loads[index].wait()
        if index < 5:
            store(index, held[index])
        elif index == 5:
            vec_out[...] = held[5][:, : vec_out.shape[1]]
            store(5, vec_out)
        elif index >= 9:
            average = held[index - 3]
            average[...] += (held[index][...].astype(F32) - average[...]) / AVG_STEPS
            store(index - 3, average)
    for copy in stores:
        copy.wait()


def fused_body(
    wide_size,
    narrow_size,
    tokens,
    memory,
    w_wide,
    w_tall,
    vecs,
    avg_wide,
    avg_tall,
    avg_vecs,
    tgt_lengths,
    src_lengths,
    cotangent,
):
    count = (wide_size * narrow_size).bit_length() - 1
    rows, sources = tokens.shape[0], memory.shape[0]
    wide_rows, wide_columns = w_wide.shape
    tall_rows = w_tall.shape[0]
    vec_rows = vecs.shape[0]
    bits = (2,) * count
    hbm = pl.BlockSpec(memory_space=pl.ANY)
    smem = pl.BlockSpec(memory_space=pltpu.SMEM)
    inputs = dict(
        tgt_lengths=tgt_lengths,
        src_lengths=src_lengths,
        tokens_in=tokens,
        memory_in=memory,
        cotangent=cotangent,
        w_wide=w_wide,
        w_tall=w_tall,
        vecs=vecs,
    )
    outputs = dict(
        slots=jax.ShapeDtypeStruct((rows, D), BF16),
        grad_tokens=jax.ShapeDtypeStruct((rows, D), F32),
        grad_memory=jax.ShapeDtypeStruct((sources, D), F32),
        grad_wide=jax.ShapeDtypeStruct((wide_rows, wide_columns), F32),
        grad_tall=jax.ShapeDtypeStruct((tall_rows, D), F32),
        grad_vecs=jax.ShapeDtypeStruct((vec_rows, 128), F32),
    )

    def arrivals(shape, dtype=BF16):
        line = (1 << (count - 3)) - 1
        far = bits[3:]
        return [
            pltpu.VMEM(lead + shape, dtype) for lead in (bits[1:], far, far, far, (line,))
        ]

    scratch = dict(
        wide=pltpu.VMEM(bits + (wide_rows, wide_columns), BF16),
        tall=pltpu.VMEM(bits + (tall_rows, D), BF16),
        vec=pltpu.VMEM(bits + vecs.shape, BF16),
        grad_vec=pltpu.VMEM(bits + (vec_rows, 128), F32),
        tokens=pltpu.VMEM((rows, D), BF16),
        memory=pltpu.VMEM((sources, D), BF16),
        seed=pltpu.VMEM((rows, D), BF16),
        seed_next=pltpu.VMEM((rows, D), BF16),
        q=pltpu.VMEM((HEADS, AUG, rows), BF16),
        k=pltpu.VMEM((HEADS, AUG, rows), BF16),
        v=pltpu.VMEM((HEADS, AUG, rows), BF16),
        q2=pltpu.VMEM((HEADS, AUG, rows), BF16),
        k2=pltpu.VMEM((HEADS, AUG, sources), BF16),
        v2=pltpu.VMEM((HEADS, AUG, sources), BF16),
        mixed_grad=pltpu.VMEM((HEADS, AUG, rows), BF16),
        mixed=pltpu.VMEM((D, rows), BF16),
        mixed2=pltpu.VMEM((D, rows), BF16),
        active=pltpu.VMEM((rows, FF), BF16),
        slope=pltpu.VMEM(bits + (rows >> count, FF), BF16),
        res=pltpu.VMEM((rows, D), F32),
        low_grad=pltpu.VMEM((rows, D), BF16),
        shift=pltpu.VMEM((rows + 8, D), F32),
        key_sum=pltpu.VMEM((HEAD_DIM, rows), F32),
        value_sum=pltpu.VMEM((HEAD_DIM, rows), F32),
        inverse=pltpu.VMEM((rows, 128), F32),
        row_vectors=pltpu.VMEM((24, D), F32),
        grad_rows=pltpu.VMEM((128, D), F32),
        grad_columns=pltpu.VMEM((D, 128), F32),
        out_wide=pltpu.VMEM((wide_rows, wide_columns), F32),
        out_tall=pltpu.VMEM((tall_rows, D), F32),
        out_vec=pltpu.VMEM((vec_rows, 128), F32),
        normed=[pltpu.VMEM((rows, D), BF16) for _ in range(3)],
        low=[pltpu.VMEM((rows, D), BF16) for _ in range(3)],
        scores=[
            pltpu.VMEM((max(high - low for low, high in bands(rows, rows, 512)), TILE), F32)
            for _ in range(2)
        ],
        shares=[pltpu.VMEM((rows, TILE), BF16) for _ in range(2)],
        score_grads=[pltpu.VMEM((rows, TILE), BF16) for _ in range(2)],
        in_tall=[arrivals((tall_rows // TALL_CUT, D)) for _ in range(TALL_CUT)],
        in_wide=[arrivals((wide_rows, blocks * D)) for blocks in (2, 2, 1, 2, 2)],
        in_vec=arrivals((vec_rows, 128), F32),
        local=pltpu.SemaphoreType.DMA((20,)),
        own_done=pltpu.SemaphoreType.DMA((3 * HEADS // 2 + 1,)),
        out_done=pltpu.SemaphoreType.DMA((OUT_SEMAPHORES,)),
        gather_send=pltpu.SemaphoreType.DMA((6 + TALL_CUT, 3 + (1 << (count - 3)), 2)),
        gather_receive=pltpu.SemaphoreType.DMA((6 + TALL_CUT, 3 + (1 << (count - 3)), 2)),
        sum_send=pltpu.SemaphoreType.DMA((9 + TALL_CUT, 3 + (1 << (count - 3)), 2)),
        sum_receive=pltpu.SemaphoreType.DMA((9 + TALL_CUT, 3 + (1 << (count - 3)), 2)),
    )
    scratch_leaves, scratch_tree = jax.tree.flatten(scratch)
    input_leaves, output_leaves = list(inputs.values()), list(outputs.values())
    names = list(inputs) + list(outputs)
    spec = [smem if value.dtype == jnp.int32 else hbm for value in input_leaves]

    def kernel(*refs):
        held = dict(zip(names, refs))
        held.update(jax.tree.unflatten(scratch_tree, refs[len(names) :]))
        layer_kernel(types.SimpleNamespace(**held), wide_size, narrow_size)

    slots, grad_tokens, grad_memory, grad_wide, grad_tall, grad_vecs = pl.pallas_call(
        kernel,
        out_shape=output_leaves,
        in_specs=spec,
        out_specs=[hbm] * len(outputs),
        scratch_shapes=scratch_leaves,
        compiler_params=pltpu.CompilerParams(
            collective_id=0, has_side_effects=True, vmem_limit_bytes=67_000_000
        ),
    )(*input_leaves)
    done = [slots, grad_tokens, grad_memory, grad_wide, grad_tall, grad_vecs]
    done += [avg_wide, avg_tall, avg_vecs, w_wide, w_tall, vecs]
    shapes = outputs | dict(grad_vecs=jax.ShapeDtypeStruct(vecs.shape, F32))
    return pl.pallas_call(
        finish_kernel,
        out_shape=list(shapes.values())
        + [jax.ShapeDtypeStruct(value.shape, F32) for value in (avg_wide, avg_tall, avg_vecs)],
        in_specs=[hbm] * len(done),
        out_specs=[hbm] * 9,
        scratch_shapes=[pltpu.VMEM(value.shape, value.dtype) for value in done]
        + [pltpu.VMEM(vecs.shape, F32), pltpu.SemaphoreType.DMA((21,))],
    )(*done)


def solution(mesh):
    in_specs = (
        P(("wide", "narrow"), None),
        P(("wide", "narrow"), None),
        P(("wide", "narrow"), None),
        P(("wide", "narrow"), None),
        P(("wide", "narrow"), None),
        P(("wide", "narrow"), None),
        P(("wide", "narrow"), None),
        P(("wide", "narrow"), None),
        P(("wide", "narrow"), None),
        P(("wide", "narrow"), None),
        P(("wide", "narrow"), None),
    )
    out_specs = (
        P(("wide", "narrow"), None),
        P(("wide", "narrow"), None),
        P(("wide", "narrow"), None),
        P(("wide", "narrow"), None),
        P(("wide", "narrow"), None),
        P(("wide", "narrow"), None),
        P(("wide", "narrow"), None),
        P(("wide", "narrow"), None),
        P(("wide", "narrow"), None),
    )
    devices = mesh.shape["wide"] * mesh.shape["narrow"]
    bits = devices.bit_length() - 1

    def body(*args):
        if args[2].shape[0] % 16 or args[3].shape[0] % 16 or devices != 1 << bits or bits < 3:
            return plain_body(*args)
        return fused_body(mesh.shape["wide"], mesh.shape["narrow"], *args)

    return jax.shard_map(body, mesh=mesh, in_specs=in_specs, out_specs=out_specs, check_vma=False)
```

```python
import types

import jax
import jax.numpy as jnp
from jax import lax
from jax.experimental import pallas as pl
from jax.experimental.pallas import tpu as pltpu
from jax.sharding import PartitionSpec as P

D = 512
HEADS = 8
HEAD_DIM = 64
FF = 2048
SEGS = 6
AVG_STEPS = 4


SCORE_SCALE = 0.125
EPSILON = 1e-05
MASKED = -1e30


def matmul(left, right):
    return jnp.dot(left, right, preferred_element_type=jnp.float32)


def matmul_first(left, right):
    return lax.dot_general(
        left, right, (((0,), (0,)), ((), ())), preferred_element_type=jnp.float32
    )


def matmul_last(left, right):
    return lax.dot_general(
        left, right, (((1,), (1,)), ((), ())), preferred_element_type=jnp.float32
    )


def segment_numbers(lengths, count):
    endings = jnp.cumsum(lengths)
    places = jnp.arange(count, dtype=jnp.int32)
    return jnp.sum((places[:, None] >= endings[None, :]).astype(jnp.int32), axis=1)


def norm_forward(before, norm_gain, norm_shift):
    centred = before - jnp.mean(before, axis=-1, keepdims=True)
    inverse = lax.rsqrt(jnp.mean(centred * centred, axis=-1, keepdims=True) + EPSILON)
    normed = centred * inverse
    return (normed * norm_gain + norm_shift, normed, inverse)


def norm_backward(gradient, normed, inverse, norm_gain):
    scaled = gradient * norm_gain
    inner_sum = jnp.mean(scaled * normed, axis=-1, keepdims=True)
    before_grad = inverse * (scaled - jnp.mean(scaled, axis=-1, keepdims=True) - normed * inner_sum)
    return (before_grad, jnp.sum(gradient * normed, axis=0), jnp.sum(gradient, axis=0))


def split_heads(matrix):
    return matrix.reshape(matrix.shape[0], HEADS, HEAD_DIM)


def masked_scores(query_block, key_heads, segment_block, key_segment):
    scores = (
        jnp.einsum(
            "qhe,khe->hqk", split_heads(query_block), key_heads, preferred_element_type=jnp.float32
        )
        * SCORE_SCALE
    )
    allowed = segment_block[:, None] == key_segment[None, :]
    return jnp.where(allowed[None], scores, MASKED)


def attend_forward(queries, keys_in, values_in, query_segment, key_segment):
    row_count = queries.shape[0]
    block_rows = min(512, row_count)
    blocks = row_count // block_rows
    key_heads = split_heads(keys_in)
    value_heads = split_heads(values_in)

    def attend_block(pieces):
        query_block, segment_block = pieces
        scores = masked_scores(query_block, key_heads, segment_block, key_segment)
        highest = jnp.max(scores, axis=-1, keepdims=True)
        exponent = jnp.exp(scores - highest)
        totals = jnp.sum(exponent, axis=-1, keepdims=True)
        shares = (exponent / totals).astype(jnp.bfloat16)
        mixed = jnp.einsum("hqk,khe->qhe", shares, value_heads, preferred_element_type=jnp.float32)
        return (
            mixed.reshape(block_rows, HEADS * HEAD_DIM).astype(jnp.bfloat16),
            (highest + jnp.log(totals))[..., 0],
        )

    mixed, logsum = lax.map(
        attend_block,
        (queries.reshape(blocks, block_rows, -1), query_segment.reshape(blocks, block_rows)),
    )
    return (mixed.reshape(row_count, -1), logsum)


def attend_backward(queries, keys_in, values_in, mixed_grad, logsum, query_segment, key_segment):
    row_count = queries.shape[0]
    block_rows = min(512, row_count)
    blocks = row_count // block_rows
    key_heads = split_heads(keys_in)
    value_heads = split_heads(values_in)

    def backward_block(carried, pieces):
        key_sum, value_sum = carried
        query_block, grad_block, logsum_block, segment_block = pieces
        scores = masked_scores(query_block, key_heads, segment_block, key_segment)
        shares = jnp.exp(scores - logsum_block[..., None])
        grad_heads = split_heads(grad_block)
        share_grad = jnp.einsum(
            "qhe,khe->hqk", grad_heads, value_heads, preferred_element_type=jnp.float32
        )
        inner_sum = jnp.sum(shares * share_grad, axis=-1, keepdims=True)
        score_grad = (shares * (share_grad - inner_sum)).astype(jnp.bfloat16)
        query_grad = (
            jnp.einsum("hqk,khe->qhe", score_grad, key_heads, preferred_element_type=jnp.float32)
            * SCORE_SCALE
        )
        key_sum = (
            key_sum
            + jnp.einsum(
                "hqk,qhe->khe",
                score_grad,
                split_heads(query_block),
                preferred_element_type=jnp.float32,
            )
            * SCORE_SCALE
        )
        value_sum = value_sum + jnp.einsum(
            "hqk,qhe->khe",
            shares.astype(jnp.bfloat16),
            grad_heads,
            preferred_element_type=jnp.float32,
        )
        return ((key_sum, value_sum), query_grad.reshape(block_rows, HEADS * HEAD_DIM))

    zeros_init = jnp.zeros((keys_in.shape[0], HEADS, HEAD_DIM), jnp.float32)
    pieces = (
        queries.reshape(blocks, block_rows, -1),
        mixed_grad.reshape(blocks, block_rows, -1),
        logsum,
        query_segment.reshape(blocks, block_rows),
    )
    (key_sum, value_sum), query_grad = lax.scan(backward_block, (zeros_init, zeros_init), pieces)
    return (
        query_grad.reshape(row_count, -1),
        key_sum.reshape(keys_in.shape[0], -1),
        value_sum.reshape(values_in.shape[0], -1),
    )


def plain_body(
    tokens,
    memory,
    w_wide,
    w_tall,
    vecs,
    avg_wide,
    avg_tall,
    avg_vecs,
    tgt_lengths,
    src_lengths,
    cotangent,
):
    wide_all, tall_all, vector_all = (
        lax.all_gather(w_wide, ("wide", "narrow"), axis=0, tiled=True),
        lax.all_gather(w_tall, ("wide", "narrow"), axis=0, tiled=True),
        lax.all_gather(vecs, ("wide", "narrow"), axis=0, tiled=True),
    )
    vectors = vector_all.astype(jnp.float32)
    spread = FF // D
    offset = 6 + spread
    columns = [wide_all[:, index * D : (index + 1) * D] for index in range(8)]
    target_query, target_key, target_value, target_output = (
        columns[0],
        columns[1],
        columns[2],
        columns[3],
    )
    source_query, source_key, source_value, source_output = (
        columns[4],
        columns[5],
        columns[6],
        columns[7],
    )
    up_weight = wide_all[:, 8 * D :]
    down_weight = tall_all[:FF]
    slot_left = tall_all[FF : FF + D]
    slot_right = tall_all[FF + D :]
    up_bias = vectors[:, 6:offset].T.reshape(FF)
    row_count = tokens.shape[0]
    target_segment = segment_numbers(tgt_lengths[0], row_count)
    source_segment = segment_numbers(src_lengths[0], memory.shape[0])
    valid_rows = (target_segment < SEGS - 1).astype(jnp.float32)[:, None]
    follow = (
        jnp.concatenate([target_segment[1:], jnp.full((1,), -1, jnp.int32)]) == target_segment
    ).astype(jnp.float32)[:, None]
    queries_self = (matmul(tokens, target_query) + vectors[:, 0]).astype(jnp.bfloat16)
    keys_self = matmul(tokens, target_key).astype(jnp.bfloat16)
    values_self = (matmul(tokens, target_value) + vectors[:, 1]).astype(jnp.bfloat16)
    mixed_self, logsum_self = attend_forward(
        queries_self, keys_self, values_self, target_segment, target_segment
    )
    first, normed_first, inverse_first = norm_forward(
        tokens.astype(jnp.float32) + matmul(mixed_self, target_output) + vectors[:, 2],
        vectors[:, offset + 2],
        vectors[:, offset + 3],
    )
    first_low = first.astype(jnp.bfloat16)
    queries_cross = (matmul(first_low, source_query) + vectors[:, 3]).astype(jnp.bfloat16)
    keys_cross = matmul(memory, source_key).astype(jnp.bfloat16)
    values_cross = (matmul(memory, source_value) + vectors[:, 4]).astype(jnp.bfloat16)
    mixed_cross, logsum_cross = attend_forward(
        queries_cross, keys_cross, values_cross, target_segment, source_segment
    )
    second, normed_second, inverse_second = norm_forward(
        first + matmul(mixed_cross, source_output) + vectors[:, 5],
        vectors[:, offset + 4],
        vectors[:, offset + 5],
    )
    second_low = second.astype(jnp.bfloat16)
    hidden = matmul(second_low, up_weight) + up_bias
    active = jax.nn.gelu(hidden).astype(jnp.bfloat16)
    third, normed_third, inverse_third = norm_forward(
        second + matmul(active, down_weight) + vectors[:, offset],
        vectors[:, offset + 6],
        vectors[:, offset + 7],
    )
    third_low = third.astype(jnp.bfloat16)
    right_half = jnp.concatenate([third_low[1:], jnp.zeros((1, D), jnp.bfloat16)]) * follow.astype(
        jnp.bfloat16
    )
    slots = (
        (matmul(third_low, slot_left) + matmul(right_half, slot_right) + vectors[:, offset + 1])
        * valid_rows
    ).astype(jnp.bfloat16)
    seed_grad = cotangent * valid_rows.astype(jnp.bfloat16)
    grad_slot_bias = jnp.sum(seed_grad.astype(jnp.float32), axis=0)
    grad_left = matmul_first(third_low, seed_grad)
    grad_right = matmul_first(right_half, seed_grad)
    right_back = matmul_last(seed_grad, slot_right) * follow
    grad_third = matmul_last(seed_grad, slot_left) + jnp.concatenate(
        [jnp.zeros((1, D), jnp.float32), right_back[:-1]]
    )
    grad_pre_third, grad_gain_third, grad_shift_third = norm_backward(
        grad_third, normed_third, inverse_third, vectors[:, offset + 6]
    )
    pre_third_low = grad_pre_third.astype(jnp.bfloat16)
    grad_down = matmul_first(active, pre_third_low)
    grad_tall_all = jnp.concatenate([grad_down, grad_left, grad_right], axis=0)
    gelu_value, gelu_pull = jax.vjp(jax.nn.gelu, hidden)
    grad_hidden = gelu_pull(matmul_last(pre_third_low, down_weight))[0]
    hidden_low = grad_hidden.astype(jnp.bfloat16)
    grad_up = matmul_first(second_low, hidden_low)
    grad_second = grad_pre_third + matmul_last(hidden_low, up_weight)
    grad_pre_second, grad_gain_second, grad_shift_second = norm_backward(
        grad_second, normed_second, inverse_second, vectors[:, offset + 4]
    )
    pre_second_low = grad_pre_second.astype(jnp.bfloat16)
    grad_source_output = matmul_first(mixed_cross, pre_second_low)
    mixed_cross_grad = matmul_last(pre_second_low, source_output).astype(jnp.bfloat16)
    cross_query_grad, cross_key_grad, cross_value_grad = attend_backward(
        queries_cross,
        keys_cross,
        values_cross,
        mixed_cross_grad,
        logsum_cross,
        target_segment,
        source_segment,
    )
    cross_query_low = cross_query_grad.astype(jnp.bfloat16)
    cross_key_low = cross_key_grad.astype(jnp.bfloat16)
    cross_value_low = cross_value_grad.astype(jnp.bfloat16)
    grad_source_query = matmul_first(first_low, cross_query_low)
    grad_source_key = matmul_first(memory, cross_key_low)
    grad_source_value = matmul_first(memory, cross_value_low)
    grad_memory = matmul_last(cross_key_low, source_key) + matmul_last(
        cross_value_low, source_value
    )
    grad_first = grad_pre_second + matmul_last(cross_query_low, source_query)
    grad_pre_first, grad_gain_first, grad_shift_first = norm_backward(
        grad_first, normed_first, inverse_first, vectors[:, offset + 2]
    )
    pre_first_low = grad_pre_first.astype(jnp.bfloat16)
    grad_target_output = matmul_first(mixed_self, pre_first_low)
    mixed_self_grad = matmul_last(pre_first_low, target_output).astype(jnp.bfloat16)
    self_query_grad, self_key_grad, self_value_grad = attend_backward(
        queries_self,
        keys_self,
        values_self,
        mixed_self_grad,
        logsum_self,
        target_segment,
        target_segment,
    )
    self_query_low = self_query_grad.astype(jnp.bfloat16)
    self_key_low = self_key_grad.astype(jnp.bfloat16)
    self_value_low = self_value_grad.astype(jnp.bfloat16)
    grad_target_query = matmul_first(tokens, self_query_low)
    grad_target_key = matmul_first(tokens, self_key_low)
    grad_target_value = matmul_first(tokens, self_value_low)
    grad_tokens = (
        grad_pre_first
        + matmul_last(self_query_low, target_query)
        + matmul_last(self_key_low, target_key)
        + matmul_last(self_value_low, target_value)
    )
    grad_wide_all = jnp.concatenate(
        [
            grad_target_query,
            grad_target_key,
            grad_target_value,
            grad_target_output,
            grad_source_query,
            grad_source_key,
            grad_source_value,
            grad_source_output,
            grad_up,
        ],
        axis=1,
    )
    bias_front = jnp.stack(
        [
            jnp.sum(self_query_grad, axis=0),
            jnp.sum(self_value_grad, axis=0),
            jnp.sum(grad_pre_first, axis=0),
            jnp.sum(cross_query_grad, axis=0),
            jnp.sum(cross_value_grad, axis=0),
            jnp.sum(grad_pre_second, axis=0),
        ],
        axis=1,
    )
    bias_middle = jnp.sum(grad_hidden, axis=0).reshape(spread, D).T
    bias_back = jnp.stack(
        [
            jnp.sum(grad_pre_third, axis=0),
            grad_slot_bias,
            grad_gain_first,
            grad_shift_first,
            grad_gain_second,
            grad_shift_second,
            grad_gain_third,
            grad_shift_third,
        ],
        axis=1,
    )
    grad_vector_all = jnp.concatenate([bias_front, bias_middle, bias_back], axis=1)
    grad_wide, grad_tall, grad_vecs = (
        lax.psum_scatter(grad_wide_all, ("wide", "narrow"), scatter_dimension=0, tiled=True),
        lax.psum_scatter(grad_tall_all, ("wide", "narrow"), scatter_dimension=0, tiled=True),
        lax.psum_scatter(grad_vector_all, ("wide", "narrow"), scatter_dimension=0, tiled=True),
    )
    new_avg_wide = avg_wide + (w_wide.astype(jnp.float32) - avg_wide) / AVG_STEPS
    new_avg_tall = avg_tall + (w_tall.astype(jnp.float32) - avg_tall) / AVG_STEPS
    new_avg_vecs = avg_vecs + (vecs.astype(jnp.float32) - avg_vecs) / AVG_STEPS
    return (
        slots,
        grad_tokens,
        grad_memory,
        grad_wide,
        grad_tall,
        grad_vecs,
        new_avg_wide,
        new_avg_tall,
        new_avg_vecs,
    )


BF16 = jnp.bfloat16
F32 = jnp.float32
AUG = 80
BIG = 1e30
TILE = 256
MESH_IDS = pl.DeviceIdType.MESH
BIAS_OUT, GAIN = 10, 12
TALL_CUT = 3
OUT_SEMAPHORES = 24
PAIR = 6 * HEAD_DIM
PAIR_GROUPS = ((0,), (1,), (2, 3))
GATHER_STEPS = {
    0: ((0, 0),),
    1: ((0, 1), (1, 0), (0, 2), (1, 1), (2, 0), (0, 3),),
    4: ((3, 0),),
    5: ((1, 2), (2, 1), (1, 3),),
    7: ((4, 0),),
    9: ((3, 1), (5, 0), (2, 2), (2, 3),),
    11: ((4, 1),),
    12: ((6, 0), (3, 2),),
    13: ((5, 1), (7, 0),),
    14: ((3, 3),),
    16: ((4, 2),),
    19: ((6, 1),),
    20: ((4, 3),),
    21: ((8, 0),),
    23: ((5, 2), (9, 0),),
    25: ((7, 1),),
    26: ((5, 3),),
    28: ((6, 2),),
    30: ((8, 1), (6, 3),),
    33: ((9, 1),),
    35: ((7, 2), (8, 2), (7, 3), (8, 3), (9, 2), (9, 3),),
}
SUM_STEPS = {
    3: ((0, 0), (1, 0),),
    4: ((2, 0),),
    9: ((3, 0), (4, 0),),
    10: ((0, 1), (5, 0),),
    11: ((1, 1),),
    13: ((2, 1),),
    15: ((3, 1),),
    21: ((4, 1),),
    23: ((7, 0), (0, 2),),
    24: ((6, 0), (5, 1),),
    25: ((1, 2), (2, 2),),
    26: ((8, 0), (3, 2),),
    27: ((0, 3), (4, 2),),
    28: ((7, 1), (9, 0),),
    29: ((1, 3), (6, 1),),
    30: ((10, 0), (5, 2),),
    31: ((2, 3), (8, 1),),
    32: ((7, 2), (3, 3),),
    33: ((9, 1), (11, 0),),
    35: ((6, 2),),
    36: ((10, 1), (4, 3), (8, 2), (5, 3), (9, 2), (11, 1), (10, 2), (7, 3), (11, 2), (6, 3), (8, 3), (9, 3), (10, 3), (11, 3),),
}


def dot(left, right, left_dim, right_dim):
    return lax.dot_general(
        left, right, (((left_dim,), (right_dim,)), ((), ())), preferred_element_type=F32
    )


def bands(query_rows, key_rows, longest):
    found = []
    for start in range(0, query_rows, TILE):
        if longest is None:
            found.append((0, key_rows))
            continue
        low = max(0, (start - longest + 1) // TILE * TILE)
        high = min(key_rows, -(-(start + TILE + longest - 1) // TILE) * TILE)
        found.append((low, high))
    return found


def column_max(scores):
    rows, columns = scores.shape
    return jnp.max(
        jnp.max(scores.reshape(rows // 64, 64, columns), axis=0), axis=0, keepdims=True
    )


def split_three(value):
    high = value.astype(BF16).astype(F32)
    middle = (value - high).astype(BF16).astype(F32)
    low = (value - high - middle).astype(BF16).astype(F32)
    return high, middle, low


def feature_rows(base, first, parts):
    place = lax.broadcasted_iota(jnp.int32, base.shape, 0)
    for step, part in enumerate(parts):
        base = jnp.where(place == first + step, part, base)
    return base


def gelu_pair(u):
    scale = 0.7978845608028654
    inner = jnp.tanh(scale * (u + 0.044715 * (u * u * u)))
    half = 0.5 * (1.0 + inner)
    slope = half + 0.5 * u * (1.0 - inner * inner) * (scale * (1.0 + 3 * 0.044715 * (u * u)))
    return u * half, slope


def normalize(before, gain, shift):
    centred = before - jnp.mean(before, axis=-1, keepdims=True)
    inverse = lax.rsqrt(jnp.mean(centred * centred, axis=-1, keepdims=True) + EPSILON)
    normed = centred * inverse
    return normed * gain + shift, normed, inverse


def attention_forward(queries, keys, values, mixed, scores, ranges, heads, hooks):
    tiles = len(ranges)

    def put(head, tile):
        low, high = ranges[tile]
        scores[tile % 2][0 : high - low, :] = dot(
            keys[head, :, low:high], queries[head, :, tile * TILE : (tile + 1) * TILE], 0, 0
        )

    put(heads[0], 0)

    def one_head(head, carried):
        for tile, (low, high) in enumerate(ranges):
            if tile + 1 < tiles:
                put(head, tile + 1)
            else:
                put(jnp.minimum(head + 1, heads[1] - 1), 0)
            span = slice(tile * TILE, (tile + 1) * TILE)
            current = scores[tile % 2][0 : high - low, :]
            highest = column_max(current)
            shares = jnp.exp(current - highest).astype(BF16)
            gathered = dot(values[head, :, low:high], shares, 1, 0)
            total = gathered[HEAD_DIM : HEAD_DIM + 1]
            rows = pl.ds(pl.multiple_of(head * HEAD_DIM, HEAD_DIM), HEAD_DIM)
            mixed[rows, span] = (gathered[:HEAD_DIM] * (1.0 / total)).astype(BF16)
            queries[head, HEAD_DIM:, span] = feature_rows(
                queries[head, HEAD_DIM:, span].astype(F32),
                SEGS,
                split_three(-(highest + jnp.log(total))),
            ).astype(BF16)
        for at, hook in hooks.items():
            pl.when(head == at)(hook)
        return carried

    lax.fori_loop(heads[0], heads[1], one_head, 0)


def attention_backward(queries, keys, values, grads, outs, sums, shares, score_grads, ranges, hooks):
    key_rows = keys.shape[2]
    key_sum, value_sum = sums
    tiles = len(ranges)

    def put(head, tile):
        low, high = ranges[tile]
        span = slice(tile * TILE, (tile + 1) * TILE)
        share = jnp.exp(dot(keys[head, :, low:high], queries[head, :, span], 0, 0))
        share_grad = dot(values[head, :, low:high], grads[head, :, span], 0, 0)
        shares[tile % 2][0 : high - low, :] = share.astype(BF16)
        score_grads[tile % 2][0 : high - low, :] = (share * share_grad).astype(BF16)

    put(0, 0)

    def one_head(head, carried):
        key_sum[:, 0:key_rows] = jnp.zeros((HEAD_DIM, key_rows), F32)
        value_sum[:, 0:key_rows] = jnp.zeros((HEAD_DIM, key_rows), F32)
        query_out, key_out, value_out = [out(head) for out in outs]
        for tile, (low, high) in enumerate(ranges):
            if tile + 1 < tiles:
                put(head, tile + 1)
            else:
                put(jnp.minimum(head + 1, HEADS - 1), 0)
            span = slice(tile * TILE, (tile + 1) * TILE)
            share = shares[tile % 2][0 : high - low, :]
            score_grad = score_grads[tile % 2][0 : high - low, :]
            query_out[:, span] = (
                dot(keys[head, 0:HEAD_DIM, low:high], score_grad, 1, 0) * SCORE_SCALE
            ).astype(BF16)
            key_sum[:, low:high] += dot(queries[head, 0:HEAD_DIM, span], score_grad, 1, 1)
            value_sum[:, low:high] += dot(grads[head, 0:HEAD_DIM, span], share, 1, 1)
        key_out[...] = key_sum[:, 0:key_rows].astype(BF16)
        value_out[...] = value_sum[:, 0:key_rows].astype(BF16)
        for at, hook in hooks.items():
            pl.when(head == at)(hook)
        return carried

    lax.fori_loop(0, HEADS, one_head, 0)


class Exchange:
    def __init__(self, wide, narrow):
        self.narrow_bits = narrow.bit_length() - 1
        self.count = (wide * narrow).bit_length() - 1
        self.line = 1 << (self.count - 3)
        self.place = (lax.axis_index("wide"), lax.axis_index("narrow"))
        number = self.place[0] * narrow + self.place[1]
        self.bits = [(number >> bit) & 1 for bit in range(self.count)]
        self.own = tuple(self.bits[bit] for bit in reversed(range(self.count)))
        self.far = list(range(3, self.count))
        self.masks = [1, 2, 4] + [other << 3 for other in range(1, self.line)]
        core = self.bits[0]
        self.first, self.second, self.both = {1: 1 - core, 2: core}, {1: core, 2: 1 - core}, {1: 1, 2: 1}

    def device(self, mask):
        wide, narrow = self.place
        return (wide ^ (mask >> self.narrow_bits), narrow ^ (mask & ((1 << self.narrow_bits) - 1)))

    def greet(self):
        barrier = pltpu.get_barrier_semaphore()
        for mask in self.masks:
            pl.semaphore_signal(
                barrier, inc=1, device_id=self.device(mask), device_id_type=MESH_IDS
            )

    def meet(self):
        pl.semaphore_wait(pltpu.get_barrier_semaphore(), len(self.masks))

    def neighbour(self, second):
        core = self.bits[0]
        take = core if not second else 1 - core
        one, other = self.device(2), self.device(4)
        return tuple(a + (b - a) * take for a, b in zip(one, other))

    def view(self, part, open_bits, flips=None):
        index = tuple(
            slice(None) if bit in open_bits else self.turned(bit, flips)
            for bit in reversed(range(self.count))
        )
        return part.ref.at[index + part.where]

    def turned(self, bit, flips):
        flip = (flips or {}).get(bit, 0)
        return self.bits[bit] + flip - 2 * self.bits[bit] * flip


class Part:
    def __init__(self, ref, rows=None, columns=None, buffers=(), outs=()):
        cut = lambda ends: slice(None) if ends is None else pl.ds(ends[0], ends[1] - ends[0])
        self.ref, self.where, self.buffers, self.outs = ref, (cut(rows), cut(columns)), buffers, outs


class Transfer:
    def __init__(self, net, pieces, send, receive):
        self.net, self.pieces, self.send, self.receive = net, pieces, send, receive
        line = tuple(range(4, 3 + net.line))
        self.stages = (line, (0,), (1, 2), (3,)) if isinstance(self, Gather) else ((0,), (1,), (2, 3), line)

    def copy(self, piece, part, slot, source, target, device):
        return pltpu.make_async_remote_copy(
            source,
            target,
            self.send.at[piece, slot, part],
            self.receive.at[piece, slot, part],
            device_id=device,
            device_id_type=MESH_IDS,
        )

    def each(self, piece, stage, act):
        for number in range(len(self.pieces[piece])):
            for slot in self.stages[stage]:
                act(self.one(piece, number, slot))

    def begin(self, piece, slot):
        for number in range(len(self.pieces[piece])):
            self.one(piece, number, slot).start()

    def finish(self):
        for piece in range(len(self.pieces)):
            for stage in range(4):
                self.each(piece, stage, lambda copy: copy.wait_send())


class Gather(Transfer):
    def one(self, piece, number, slot):
        net, part = self.net, self.pieces[piece][number]
        if slot == 3:
            view, device = net.view(part, net.far + [1, 2]), net.device(1)
        elif slot > 3:
            view, device = net.view(part, []), net.device((slot - 3) << 3)
        else:
            view = net.view(part, net.far, net.first if slot == 2 else None)
            device = net.neighbour(slot > 0)
        return self.copy(piece, number, slot, view, view, device)

    def start(self, piece):
        if piece < len(self.pieces):
            self.each(piece, 0, lambda copy: copy.start())

    def step(self, piece, stage):
        self.each(piece, stage, lambda copy: copy.wait_recv())
        if stage == 0:
            self.begin(piece, 0)
            self.begin(piece, 1)
            if piece == 0:
                self.start(1)
            self.start(piece + 2)
        elif stage == 1:
            self.begin(piece, 2)
        elif stage == 2:
            self.begin(piece, 3)


class Sum(Transfer):
    def one(self, piece, number, slot):
        net, part = self.net, self.pieces[piece][number]
        if slot == 0:
            view, device = net.view(part, net.far + [1, 2], {0: 1}), net.device(1)
        elif slot > 3:
            mask = (slot - 3) << 3
            view, device = net.view(part, [], {bit: mask >> bit & 1 for bit in net.far}), net.device(mask)
        else:
            view = net.view(part, net.far, (None, net.both, net.second, net.first)[slot])
            device = net.neighbour(slot < 3)
        target = part.buffers[4].at[slot - 4] if slot > 3 else part.buffers[slot]
        return self.copy(piece, number, slot, view, target, device)

    def start(self, piece):
        self.begin(piece, 0)

    def add(self, piece, stage):
        net = self.net
        if stage == 3:
            for part in self.pieces[piece]:
                value = part.ref[net.own + part.where].astype(F32)
                for other in range(1, net.line):
                    value = value + part.buffers[4][other - 1].astype(F32)
                for low, high, staged, out, semaphore in part.outs:
                    staged[...] = value[:, low:high]
                    pltpu.make_async_copy(staged, out, semaphore).start()
            return
        rest = net.far + ([1, 2] if stage == 0 else [])
        rest.sort()

        def one_shard(step, carried):
            place = {bit: (step >> at) & 1 for at, bit in enumerate(rest)}
            index = tuple(
                place[bit] if bit in place else net.turned(bit, net.first if stage == 1 else None)
                for bit in reversed(range(net.count))
            )
            arrived = tuple(place[bit] for bit in reversed(rest)) + (slice(None), slice(None))
            for part in self.pieces[piece]:
                where = index + part.where
                if stage == 2:
                    value = (
                        part.ref[where].astype(F32)
                        + part.buffers[2][arrived].astype(F32)
                        + part.buffers[3][arrived].astype(F32)
                    )
                else:
                    value = part.ref[where] + part.buffers[stage][arrived]
                part.ref[where] = value.astype(part.ref.dtype)
            return carried

        lax.fori_loop(0, 1 << len(rest), one_shard, 0, unroll=True)

    def step(self, piece, stage):
        self.each(piece, stage, lambda copy: copy.wait_recv())
        self.add(piece, stage)
        if stage == 0:
            self.begin(piece, 1)
            self.begin(piece, 2)
        elif stage == 1:
            self.begin(piece, 3)
        elif stage == 2:
            self.each(piece, 3, lambda copy: copy.start())

    def finish(self):
        super().finish()
        for piece in self.pieces:
            for part in piece:
                for _, _, staged, out, semaphore in part.outs:
                    pltpu.make_async_copy(staged, out, semaphore).wait()


class Plan:
    def __init__(self, transfer, table):
        self.transfer, self.table, self.stop = transfer, table, 0

    def next(self):
        taken = self.table.get(self.stop, ())
        self.stop += 1

        def act():
            for piece, stage in taken:
                self.transfer.step(piece, stage)

        return act if taken else None

    def now(self):
        act = self.next()
        if act:
            act()

    def loop(self, places):
        found = {place: self.next() for place in places}
        return {place: act for place, act in found.items() if act}


def layer_kernel(r, wide_size, narrow_size):
    net = Exchange(wide_size, narrow_size)
    net.greet()
    devices = wide_size * narrow_size
    wide7, tall7, vec7, gvec7 = r.wide, r.tall, r.vec, r.grad_vec
    wide = wide7.reshape(devices * wide7.shape[-2], wide7.shape[-1])
    tall = tall7.reshape(devices * tall7.shape[-2], tall7.shape[-1])
    slope7 = r.slope
    slope = slope7.reshape(devices * slope7.shape[-2], slope7.shape[-1])
    own_rows = (0, wide7.shape[-2])
    tokens, memory, seed, seed_next = r.tokens, r.memory, r.seed, r.seed_next
    rows, sources = tokens.shape[0], memory.shape[0]
    tiles = rows // TILE
    local = r.local

    wide_moves = [
        (block * D + pair * PAIR // 3, pair * PAIR + block * PAIR // 3, PAIR // 3)
        for pair in range(HEADS // 2)
        for block in range(3)
    ] + [(3 * D, 3 * D, wide7.shape[-1] - 3 * D)]
    loads = [
        pltpu.make_async_copy(
            r.w_wide.at[:, pl.ds(low, width)],
            wide7.at[net.own + (slice(None), pl.ds(high, width))],
            r.own_done.at[number],
        )
        for number, (low, high, width) in enumerate(wide_moves)
    ] + [
        pltpu.make_async_copy(r.w_tall, tall7.at[net.own], local.at[1]),
        pltpu.make_async_copy(r.vecs, vec7.at[net.own], local.at[2]),
        pltpu.make_async_copy(r.tokens_in, tokens, local.at[3]),
        pltpu.make_async_copy(r.memory_in, memory, local.at[4]),
        pltpu.make_async_copy(r.cotangent, seed, local.at[5]),
    ]
    for copy in loads:
        copy.start()

    tall_rows = tall7.shape[-2]
    tall_cuts = [(low, low + tall_rows // TALL_CUT) for low in range(0, tall_rows, tall_rows // TALL_CUT)]

    def wide_part(low, high):
        return [Part(wide7, None, (low, high))]

    gather = Gather(
        net,
        [
            wide_part(0, PAIR) + [Part(vec7)],
            wide_part(PAIR, 2 * PAIR),
            wide_part(2 * PAIR, 4 * PAIR),
            wide_part(3 * D, 5 * D),
            wide_part(5 * D, 7 * D),
            wide_part(7 * D, 9 * D),
            wide_part(9 * D, 12 * D),
        ]
        + [[Part(tall7, cut)] for cut in tall_cuts],
        r.gather_send,
        r.gather_receive,
    )
    plan = Plan(gather, GATHER_STEPS)
    out_semaphores = iter(range(OUT_SEMAPHORES))

    def out_of(low, high, staged, out):
        return (low, high, staged, out, r.out_done.at[next(out_semaphores)])

    def wide_out(low, high, start):
        columns = pl.ds(start, high - low)
        return out_of(low, high, r.out_wide.at[:, columns], r.grad_wide.at[:, columns])

    def tall_sum(cut, buffers):
        place = pl.ds(cut[0], cut[1] - cut[0])
        out = out_of(0, D, r.out_tall.at[place, :], r.grad_tall.at[place, :])
        return [Part(tall7, cut, None, buffers, [out])]

    def wide_sum(low, high, buffers):
        return [Part(wide7, None, (low, high), buffers, [wide_out(0, high - low, low)])]

    def self_sum(pair):
        third = PAIR // 3
        outs = [
            wide_out(block * third, (block + 1) * third, block * D + pair * third)
            for block in range(3)
        ]
        columns = (pair * PAIR, (pair + 1) * PAIR)
        return [Part(slope7, own_rows, columns, r.in_self[pair], outs)]

    vec_sum = Part(gvec7, None, None, r.in_vec, [out_of(0, 128, r.out_vec, r.grad_vecs)])
    ranges_of_sum = ((8, 10), (10, 12), (7, 8), (3, 5), (5, 7))
    total = Sum(
        net,
        [tall_sum(cut, buffers) for cut, buffers in zip(tall_cuts, r.in_tall)]
        + [
            wide_sum(low * D, high * D, buffers)
            for (low, high), buffers in zip(ranges_of_sum, r.in_wide)
        ]
        + [self_sum(pair) + ([vec_sum] if pair == HEADS // 2 - 1 else []) for pair in range(HEADS // 2)],
        r.sum_send,
        r.sum_receive,
    )
    TALL, UP, OUT2, MID, KEYS2, SELF = 0, TALL_CUT, TALL_CUT + 2, TALL_CUT + 3, TALL_CUT + 4, TALL_CUT + 5
    sum_plan = Plan(total, SUM_STEPS)

    for copy in loads[:-3]:
        copy.wait()
    net.meet()
    gather.start(0)

    def endings(lengths):
        found, running = [], 0
        for index in range(SEGS):
            running = running + lengths[0, index]
            found.append(running)
        return found

    target_ends = endings(r.tgt_lengths)
    source_ends = endings(r.src_lengths)

    def chosen(ends, count):
        place = lax.broadcasted_iota(jnp.int32, (16, count), 1)
        segment = jnp.zeros((16, count), jnp.int32)
        for end in ends:
            segment = segment + (place >= end).astype(jnp.int32)
        return segment == lax.broadcasted_iota(jnp.int32, (16, count), 0)

    def query_features(ends, count):
        return jnp.where(chosen(ends, count), 1.0, 0.0).astype(BF16)

    def key_features(ends, count):
        row = lax.broadcasted_iota(jnp.int32, (16, count), 0)
        masked = jnp.where(chosen(ends, count), 0.0, -BIG)
        return jnp.where(row < SEGS, masked, jnp.where(row < SEGS + 3, 1.0, 0.0)).astype(BF16)

    def value_features(count):
        row = lax.broadcasted_iota(jnp.int32, (16, count), 0)
        return jnp.where(row < 3, 1.0, 0.0).astype(BF16)

    def every_head(ref, features):
        ref[:, HEAD_DIM:, :] = jnp.broadcast_to(features[None], (HEADS,) + features.shape)

    q, k, v, q2, k2, v2 = r.q, r.k, r.v, r.q2, r.k2, r.v2
    every_head(q, query_features(target_ends, rows))
    every_head(q2, query_features(target_ends, rows))
    every_head(k, key_features(target_ends, rows))
    every_head(k2, key_features(source_ends, sources))
    every_head(v, value_features(rows))
    every_head(v2, value_features(sources))
    plan.now()

    def position(tile):
        return tile * TILE + lax.broadcasted_iota(jnp.int32, (TILE, 1), 0)

    def valid(tile):
        return jnp.where(position(tile) < target_ends[SEGS - 2], 1.0, 0.0)

    def follow(tile):
        after = position(tile) + 1
        ended = after == target_ends[0]
        for end in target_ends[1:]:
            ended = ended | (after == end)
        return jnp.where(ended, 0.0, 1.0)

    def span(tile):
        return pl.ds(tile * TILE, TILE)

    shift, res = r.shift, r.res
    loads[-1].wait()
    shift[0:8, :] = jnp.zeros((8, D), F32)
    for tile in range(tiles):
        masked = seed[span(tile), :].astype(F32) * valid(tile)
        seed[span(tile), :] = masked.astype(BF16)
        shift[pl.ds(tile * TILE + 8, TILE), :] = masked * follow(tile)
    for tile in range(tiles):
        seed_next[span(tile), :] = shift[pl.ds(tile * TILE + 7, TILE), :].astype(BF16)
    shift[rows : rows + 8, :] = jnp.zeros((8, D), F32)
    r.grad_rows[...] = jnp.zeros_like(r.grad_rows)
    r.grad_columns[...] = jnp.zeros_like(r.grad_columns)
    loads[-3].wait()
    loads[-2].wait()

    def row(index):
        return r.row_vectors[index : index + 1, :]

    def column(index):
        return vec7[...].reshape(D, vec7.shape[-1])[:, index : index + 1].astype(F32)

    def heads_of(value):
        return value.reshape(value.shape[0] // HEAD_DIM, HEAD_DIM, value.shape[1])

    def scaled(value):
        return (value.astype(BF16).astype(F32) * SCORE_SCALE).astype(BF16)

    def wide_column(index):
        return wide[:, index * D : (index + 1) * D]

    self_ranges = bands(rows, rows, 512)
    cross_ranges = bands(rows, sources, None)
    a, a2 = r.mixed, r.mixed2
    bias_rows = PAIR // 3
    identity = lax.broadcasted_iota(jnp.int32, (D, D), 0) == lax.broadcasted_iota(
        jnp.int32, (D, D), 1
    )
    identity = jnp.where(identity, 1.0, 0.0).astype(BF16)
    for index, pairs in enumerate(PAIR_GROUPS):
        plan.now()
        if index == 0:
            r.row_vectors[0 : vec7.shape[-1], :] = dot(
                vec7[...].reshape(D, vec7.shape[-1]), identity, 0, 0
            )
        biases = []
        for pair in pairs:
            place = slice(pair * bias_rows, (pair + 1) * bias_rows)
            biases += [column(0)[place], jnp.zeros((bias_rows, 1), F32), column(1)[place]]
        bias = jnp.concatenate(biases, axis=0)
        for tile in range(tiles):
            both = dot(
                wide[:, pairs[0] * PAIR : (pairs[-1] + 1) * PAIR], tokens[span(tile), :], 0, 1
            )
            both = (both + bias).astype(BF16)
            for place, pair in enumerate(pairs):
                for block, ref in enumerate((q, k, v)):
                    start = place * PAIR + block * bias_rows
                    value = both[start : start + bias_rows]
                    if block == 0:
                        value = (value.astype(F32) * SCORE_SCALE).astype(BF16)
                    ref[2 * pair : 2 * pair + 2, 0:HEAD_DIM, span(tile)] = heads_of(value)
        plan.now()
        heads = (2 * pairs[0], 2 * pairs[-1] + 2)
        attention_forward(
            q,
            k,
            v,
            a,
            r.scores,
            self_ranges,
            heads,
            plan.loop(range(*heads)),
        )

    normed, low, inverse = r.normed, r.low, r.inverse

    def norm_tile(index, tile, before):
        out, unit, rho = normalize(before, row(GAIN + 2 * index), row(GAIN + 2 * index + 1))
        normed[index][span(tile), :] = unit.astype(BF16)
        inverse[span(tile), index : index + 1] = rho
        low[index][span(tile), :] = out.astype(BF16)
        return out

    plan.now()
    for tile in range(tiles):
        before = (
            tokens[span(tile), :].astype(F32) + dot(a[:, span(tile)], wide_column(3), 0, 0) + row(2)
        )
        out = norm_tile(0, tile, before)
        res[span(tile), :] = out
        q2[:, 0:HEAD_DIM, span(tile)] = heads_of(
            scaled(dot(wide_column(4), out.astype(BF16), 0, 1) + column(3))
        )
        plan.now()
    plan.now()
    for tile in range(sources // TILE):
        part = memory[span(tile), :]
        k2[:, 0:HEAD_DIM, span(tile)] = heads_of(dot(wide_column(5), part, 0, 1).astype(BF16))
        v2[:, 0:HEAD_DIM, span(tile)] = heads_of(
            (dot(wide_column(6), part, 0, 1) + column(4)).astype(BF16)
        )
    attention_forward(
        q2,
        k2,
        v2,
        a2,
        r.scores,
        cross_ranges,
        (0, HEADS),
        plan.loop(range(HEADS)),
    )
    active = r.active
    plan.now()
    for tile in range(tiles):
        before = res[span(tile), :] + dot(a2[:, span(tile)], wide_column(7), 0, 0) + row(5)
        out = norm_tile(1, tile, before)
        res[span(tile), :] = out
        for block in range(FF // D):
            if tile == 0 and block == 1:
                plan.now()
            columns = slice(block * D, (block + 1) * D)
            u = dot(out.astype(BF16), wide_column(8 + block), 1, 0) + row(6 + block)
            value, derivative = gelu_pair(u)
            active[span(tile), columns] = value.astype(BF16)
            slope[span(tile), columns] = derivative.astype(BF16)
        plan.now()
    plan.now()
    slot_left = tall.at[pl.ds(FF, D), :]
    slot_right = tall.at[pl.ds(FF + D, D), :]
    for tile in range(tiles):
        before = (
            res[span(tile), :] + dot(active[span(tile), :], tall[0:FF, :], 1, 0) + row(BIAS_OUT)
        )
        out = norm_tile(2, tile, before).astype(BF16)
        shift[span(tile), :] = dot(out, slot_right[...], 1, 0)
    low_grad = r.low_grad
    slot_copies = []
    for tile in range(tiles):
        low_grad[span(tile), :] = (
            (
                dot(low[2][span(tile), :], slot_left[...], 1, 0)
                + follow(tile) * shift[pl.ds(tile * TILE + 1, TILE), :]
                + row(BIAS_OUT + 1)
            )
            * valid(tile)
        ).astype(BF16)
        copy = pltpu.make_async_copy(
            low_grad.at[span(tile), :], r.slots.at[span(tile), :], local.at[6 + tile]
        )
        copy.start()
        slot_copies.append(copy)
    gather.finish()

    grad_rows, grad_columns = r.grad_rows, r.grad_columns

    def add_row(index, value):
        grad_rows[index : index + 1, :] += jnp.sum(value, axis=0, keepdims=True)

    def norm_back(index, tile, gradient, bias_row):
        gain = row(GAIN + 2 * index)
        unit = normed[index][span(tile), :].astype(F32)
        scaled_grad = gradient * gain
        inner = jnp.mean(scaled_grad * unit, axis=-1, keepdims=True)
        before = inverse[span(tile), index : index + 1] * (
            scaled_grad - jnp.mean(scaled_grad, axis=-1, keepdims=True) - unit * inner
        )
        add_row(GAIN + 2 * index, gradient * unit)
        add_row(GAIN + 2 * index + 1, gradient)
        add_row(bias_row, before)
        res[span(tile), :] = before
        low_grad[span(tile), :] = before.astype(BF16)

    for tile in range(tiles):
        part = seed[span(tile), :]
        add_row(BIAS_OUT + 1, part.astype(F32))
        gradient = dot(part, slot_left[...], 1, 1) + dot(
            seed_next[span(tile), :], slot_right[...], 1, 1
        )
        slot_copies[tile].wait()
        norm_back(2, tile, gradient, BIAS_OUT)
    slot_left[...] = dot(low[2][...], seed[...], 0, 0).astype(BF16)
    slot_right[...] = dot(low[2][...], seed_next[...], 0, 0).astype(BF16)
    for block in range(FF // D):
        columns = slice(block * D, (block + 1) * D)
        for tile in range(tiles):
            grad = dot(low_grad[span(tile), :], tall[columns, :], 1, 1) * slope[
                span(tile), columns
            ].astype(F32)
            add_row(6 + block, grad)
            slope[span(tile), columns] = grad.astype(BF16)
        tall[columns, :] = dot(active[:, columns], low_grad[...], 0, 0).astype(BF16)
    for cut in range(TALL_CUT):
        total.start(TALL + cut)
    for tile in range(tiles):
        gradient = res[span(tile), :] + dot(
            slope[span(tile), :], wide[:, 8 * D : 8 * D + FF], 1, 1
        )
        norm_back(1, tile, gradient, 5)
        sum_plan.now()
    for block in range(FF // D):
        columns = slice(block * D, (block + 1) * D)
        wide[:, 8 * D + block * D : 8 * D + (block + 1) * D] = dot(
            low[1][...], slope[:, columns], 0, 0
        ).astype(BF16)
        if block % 2 == 1:
            total.start(UP + block // 2)
        sum_plan.now()
    grads = r.mixed_grad

    def mixed_back(weight_index, mixed):
        for tile in range(tiles):
            grad = dot(wide_column(weight_index), low_grad[span(tile), :], 1, 1).astype(BF16)
            grads[:, 0:HEAD_DIM, span(tile)] = heads_of(grad)
            inner = jnp.sum(
                heads_of(grad.astype(F32) * mixed[:, span(tile)].astype(F32)),
                axis=1,
                keepdims=True,
            )
            place = lax.broadcasted_iota(jnp.int32, (HEADS, 16, TILE), 1)
            features = jnp.zeros((HEADS, 16, TILE), F32)
            for step, part in enumerate(split_three(-inner)):
                features = jnp.where(place == step, part, features)
            grads[:, HEAD_DIM:, span(tile)] = features.astype(BF16)
        wide[:, weight_index * D : (weight_index + 1) * D] = dot(
            mixed[...], low_grad[...], 1, 0
        ).astype(BF16)

    mixed_back(7, a2)
    total.start(OUT2)
    sum_plan.now()
    dq2 = active.at[pl.ds(0, D), pl.ds(0, rows)]
    dk2 = active.at[pl.ds(D, D), pl.ds(0, sources)]
    dv2 = active.at[pl.ds(D, D), pl.ds(rows, sources)]

    def head_rows(ref):
        def of(head):
            return ref.at[pl.ds(pl.multiple_of(head * HEAD_DIM, HEAD_DIM), HEAD_DIM), :]

        return of

    sums = (r.key_sum, r.value_sum)
    attention_backward(
        q2,
        k2,
        v2,
        grads,
        [head_rows(ref) for ref in (dq2, dk2, dv2)],
        sums,
        r.shares,
        r.score_grads,
        cross_ranges,
        sum_plan.loop(range(HEADS)),
    )

    def column_sum(index, value):
        grad_columns[:, index : index + 1] += jnp.sum(value.astype(F32), axis=1, keepdims=True)

    for tile in range(tiles):
        gradient = res[span(tile), :] + dot(dq2[:, span(tile)], wide_column(4), 0, 1)
        norm_back(0, tile, gradient, 2)
        sum_plan.now()
    shift[0:sources, :] = dot(dk2[...], wide_column(5), 0, 1) + dot(dv2[...], wide_column(6), 0, 1)
    memory_copy = pltpu.make_async_copy(
        shift.at[pl.ds(0, sources), :], r.grad_memory, local.at[10]
    )
    memory_copy.start()
    wide[:, 5 * D : 6 * D] = dot(memory[...], dk2[...], 0, 1).astype(BF16)
    wide[:, 6 * D : 7 * D] = dot(memory[...], dv2[...], 0, 1).astype(BF16)
    total.start(KEYS2)
    sum_plan.now()
    wide[:, 4 * D : 5 * D] = dot(low[0][...], dq2[...], 0, 1).astype(BF16)
    column_sum(3, dq2[...])
    column_sum(4, dv2[...])
    mixed_back(3, a)
    total.start(MID)
    sum_plan.now()

    def pair_rows(block):
        def of(head):
            pair = head // 2
            row = pair % 2 * PAIR + block * (PAIR // 3) + head % 2 * HEAD_DIM
            start = pl.multiple_of(pair // 2 * rows, rows)
            return active.at[pl.ds(pl.multiple_of(row, HEAD_DIM), HEAD_DIM), pl.ds(start, rows)]

        return of

    def pair_grad(pair):
        return active[pair % 2 * PAIR : (pair % 2 + 1) * PAIR, pair // 2 * rows : (pair // 2 + 1) * rows]

    def start_pair(pair):
        where = (slice(None),) * net.count + (
            slice(0, own_rows[1]),
            slice(pair * PAIR, (pair + 1) * PAIR),
        )
        slope7[where] = (
            dot(tokens[...], pair_grad(pair), 0, 1)
            .astype(BF16)
            .reshape(slope7.shape[: net.count] + (own_rows[1], PAIR))
        )
        if pair == HEADS // 2 - 1:
            for other in range(HEADS // 2):
                place = slice(other * bias_rows, (other + 1) * bias_rows)
                grad = pair_grad(other).astype(F32)
                for index, block in ((0, 0), (1, 2)):
                    grad_columns[place, index : index + 1] = jnp.sum(
                        grad[block * bias_rows : (block + 1) * bias_rows], axis=1, keepdims=True
                    )
            turned = jnp.transpose(r.grad_rows[...]) + grad_columns[...]
            gvec7[...] = turned.reshape(gvec7.shape)
        total.start(SELF + pair)

    hooks = {}
    for head in range(HEADS):
        act = sum_plan.next()

        def hook(head=head, act=act):
            if head % 2 and head < HEADS - 1:
                start_pair(head // 2)
            if act:
                act()

        if act or (head % 2 and head < HEADS - 1):
            hooks[head] = hook
    attention_backward(
        q,
        k,
        v,
        grads,
        [pair_rows(block) for block in range(3)],
        sums,
        r.shares,
        r.score_grads,
        self_ranges,
        hooks,
    )
    start_pair(HEADS // 2 - 1)
    sum_plan.now()
    token_copies = []
    for tile in range(tiles):
        value = res[span(tile), :]
        for side in range(2):
            value = value + dot(
                active[0 : 2 * PAIR, pl.ds(side * rows + tile * TILE, TILE)],
                wide[:, 2 * side * PAIR : 2 * (side + 1) * PAIR],
                0,
                1,
            )
        res[span(tile), :] = value
        copy = pltpu.make_async_copy(
            res.at[span(tile), :], r.grad_tokens.at[span(tile), :], local.at[12 + tile]
        )
        copy.start()
        token_copies.append(copy)
        sum_plan.now()
    sum_plan.now()
    total.finish()
    for copy in token_copies + [memory_copy]:
        copy.wait()


def finish_kernel(*refs):
    given, results, held = refs[:12], refs[12:21], refs[21:33]
    vec_out, semaphores = refs[33], refs[34]
    loads = [
        pltpu.make_async_copy(source, target, semaphores.at[index])
        for index, (source, target) in enumerate(zip(given, held))
    ]
    for copy in loads:
        copy.start()
    stores = []

    def store(index, source):
        copy = pltpu.make_async_copy(source, results[index], semaphores.at[12 + index])
        copy.start()
        stores.append(copy)

    for index in range(12):
        loads[index].wait()
        if index < 5:
            store(index, held[index])
        elif index == 5:
            vec_out[...] = held[5][:, : vec_out.shape[1]]
            store(5, vec_out)
        elif index >= 9:
            average = held[index - 3]
            average[...] += (held[index][...].astype(F32) - average[...]) / AVG_STEPS
            store(index - 3, average)
    for copy in stores:
        copy.wait()


def fused_body(
    wide_size,
    narrow_size,
    tokens,
    memory,
    w_wide,
    w_tall,
    vecs,
    avg_wide,
    avg_tall,
    avg_vecs,
    tgt_lengths,
    src_lengths,
    cotangent,
):
    count = (wide_size * narrow_size).bit_length() - 1
    rows, sources = tokens.shape[0], memory.shape[0]
    wide_rows, wide_columns = w_wide.shape
    tall_rows = w_tall.shape[0]
    vec_rows = vecs.shape[0]
    bits = (2,) * count
    hbm = pl.BlockSpec(memory_space=pl.ANY)
    smem = pl.BlockSpec(memory_space=pltpu.SMEM)
    inputs = dict(
        tgt_lengths=tgt_lengths,
        src_lengths=src_lengths,
        tokens_in=tokens,
        memory_in=memory,
        cotangent=cotangent,
        w_wide=w_wide,
        w_tall=w_tall,
        vecs=vecs,
    )
    outputs = dict(
        slots=jax.ShapeDtypeStruct((rows, D), BF16),
        grad_tokens=jax.ShapeDtypeStruct((rows, D), F32),
        grad_memory=jax.ShapeDtypeStruct((sources, D), F32),
        grad_wide=jax.ShapeDtypeStruct((wide_rows, wide_columns), F32),
        grad_tall=jax.ShapeDtypeStruct((tall_rows, D), F32),
        grad_vecs=jax.ShapeDtypeStruct((vec_rows, 128), F32),
    )

    def arrivals(shape, dtype=BF16):
        line = (1 << (count - 3)) - 1
        far = bits[3:]
        return [
            pltpu.VMEM(lead + shape, dtype) for lead in (bits[1:], far, far, far, (line,))
        ]

    scratch = dict(
        wide=pltpu.VMEM(bits + (wide_rows, wide_columns), BF16),
        tall=pltpu.VMEM(bits + (tall_rows, D), BF16),
        vec=pltpu.VMEM(bits + vecs.shape, BF16),
        grad_vec=pltpu.VMEM(bits + (vec_rows, 128), F32),
        tokens=pltpu.VMEM((rows, D), BF16),
        memory=pltpu.VMEM((sources, D), BF16),
        seed=pltpu.VMEM((rows, D), BF16),
        seed_next=pltpu.VMEM((rows, D), BF16),
        q=pltpu.VMEM((HEADS, AUG, rows), BF16),
        k=pltpu.VMEM((HEADS, AUG, rows), BF16),
        v=pltpu.VMEM((HEADS, AUG, rows), BF16),
        q2=pltpu.VMEM((HEADS, AUG, rows), BF16),
        k2=pltpu.VMEM((HEADS, AUG, sources), BF16),
        v2=pltpu.VMEM((HEADS, AUG, sources), BF16),
        mixed_grad=pltpu.VMEM((HEADS, AUG, rows), BF16),
        mixed=pltpu.VMEM((D, rows), BF16),
        mixed2=pltpu.VMEM((D, rows), BF16),
        active=pltpu.VMEM((rows, FF), BF16),
        slope=pltpu.VMEM(bits + (rows >> count, FF), BF16),
        res=pltpu.VMEM((rows, D), F32),
        low_grad=pltpu.VMEM((rows, D), BF16),
        shift=pltpu.VMEM((rows + 8, D), F32),
        key_sum=pltpu.VMEM((HEAD_DIM, rows), F32),
        value_sum=pltpu.VMEM((HEAD_DIM, rows), F32),
        inverse=pltpu.VMEM((rows, 128), F32),
        row_vectors=pltpu.VMEM((24, D), F32),
        grad_rows=pltpu.VMEM((128, D), F32),
        grad_columns=pltpu.VMEM((D, 128), F32),
        out_wide=pltpu.VMEM((wide_rows, wide_columns), F32),
        out_tall=pltpu.VMEM((tall_rows, D), F32),
        out_vec=pltpu.VMEM((vec_rows, 128), F32),
        normed=[pltpu.VMEM((rows, D), BF16) for _ in range(3)],
        low=[pltpu.VMEM((rows, D), BF16) for _ in range(3)],
        scores=[
            pltpu.VMEM((max(high - low for low, high in bands(rows, rows, 512)), TILE), F32)
            for _ in range(2)
        ],
        shares=[pltpu.VMEM((rows, TILE), BF16) for _ in range(2)],
        score_grads=[pltpu.VMEM((rows, TILE), BF16) for _ in range(2)],
        in_tall=[arrivals((tall_rows // TALL_CUT, D)) for _ in range(TALL_CUT)],
        in_wide=[arrivals((wide_rows, blocks * D)) for blocks in (2, 2, 1, 2, 2)],
        in_self=[arrivals((wide_rows, PAIR)) for _ in range(HEADS // 2)],
        in_vec=arrivals((vec_rows, 128), F32),
        local=pltpu.SemaphoreType.DMA((20,)),
        own_done=pltpu.SemaphoreType.DMA((3 * HEADS // 2 + 1,)),
        out_done=pltpu.SemaphoreType.DMA((OUT_SEMAPHORES,)),
        gather_send=pltpu.SemaphoreType.DMA((7 + TALL_CUT, 3 + (1 << (count - 3)), 2)),
        gather_receive=pltpu.SemaphoreType.DMA((7 + TALL_CUT, 3 + (1 << (count - 3)), 2)),
        sum_send=pltpu.SemaphoreType.DMA((9 + TALL_CUT, 3 + (1 << (count - 3)), 2)),
        sum_receive=pltpu.SemaphoreType.DMA((9 + TALL_CUT, 3 + (1 << (count - 3)), 2)),
    )
    scratch_leaves, scratch_tree = jax.tree.flatten(scratch)
    input_leaves, output_leaves = list(inputs.values()), list(outputs.values())
    names = list(inputs) + list(outputs)
    spec = [smem if value.dtype == jnp.int32 else hbm for value in input_leaves]

    def kernel(*refs):
        held = dict(zip(names, refs))
        held.update(jax.tree.unflatten(scratch_tree, refs[len(names) :]))
        layer_kernel(types.SimpleNamespace(**held), wide_size, narrow_size)

    slots, grad_tokens, grad_memory, grad_wide, grad_tall, grad_vecs = pl.pallas_call(
        kernel,
        out_shape=output_leaves,
        in_specs=spec,
        out_specs=[hbm] * len(outputs),
        scratch_shapes=scratch_leaves,
        compiler_params=pltpu.CompilerParams(
            collective_id=0, has_side_effects=True, vmem_limit_bytes=67_000_000
        ),
    )(*input_leaves)
    done = [slots, grad_tokens, grad_memory, grad_wide, grad_tall, grad_vecs]
    done += [avg_wide, avg_tall, avg_vecs, w_wide, w_tall, vecs]
    shapes = outputs | dict(grad_vecs=jax.ShapeDtypeStruct(vecs.shape, F32))
    return pl.pallas_call(
        finish_kernel,
        out_shape=list(shapes.values())
        + [jax.ShapeDtypeStruct(value.shape, F32) for value in (avg_wide, avg_tall, avg_vecs)],
        in_specs=[hbm] * len(done),
        out_specs=[hbm] * 9,
        scratch_shapes=[pltpu.VMEM(value.shape, value.dtype) for value in done]
        + [pltpu.VMEM(vecs.shape, F32), pltpu.SemaphoreType.DMA((21,))],
    )(*done)


def solution(mesh):
    in_specs = (
        P(("wide", "narrow"), None),
        P(("wide", "narrow"), None),
        P(("wide", "narrow"), None),
        P(("wide", "narrow"), None),
        P(("wide", "narrow"), None),
        P(("wide", "narrow"), None),
        P(("wide", "narrow"), None),
        P(("wide", "narrow"), None),
        P(("wide", "narrow"), None),
        P(("wide", "narrow"), None),
        P(("wide", "narrow"), None),
    )
    out_specs = (
        P(("wide", "narrow"), None),
        P(("wide", "narrow"), None),
        P(("wide", "narrow"), None),
        P(("wide", "narrow"), None),
        P(("wide", "narrow"), None),
        P(("wide", "narrow"), None),
        P(("wide", "narrow"), None),
        P(("wide", "narrow"), None),
        P(("wide", "narrow"), None),
    )
    devices = mesh.shape["wide"] * mesh.shape["narrow"]
    bits = devices.bit_length() - 1

    def body(*args):
        if args[2].shape[0] % 16 or args[3].shape[0] % 16 or devices != 1 << bits or bits < 3:
            return plain_body(*args)
        return fused_body(mesh.shape["wide"], mesh.shape["narrow"], *args)

    return jax.shard_map(body, mesh=mesh, in_specs=in_specs, out_specs=out_specs, check_vma=False)
```

```python
import types

import jax
import jax.numpy as jnp
from jax import lax
from jax.experimental import pallas as pl
from jax.experimental.pallas import tpu as pltpu
from jax.sharding import PartitionSpec as P

D = 512
HEADS = 8
HEAD_DIM = 64
FF = 2048
SEGS = 6
AVG_STEPS = 4


SCORE_SCALE = 0.125
EPSILON = 1e-05
MASKED = -1e30


def matmul(left, right):
    return jnp.dot(left, right, preferred_element_type=jnp.float32)


def matmul_first(left, right):
    return lax.dot_general(
        left, right, (((0,), (0,)), ((), ())), preferred_element_type=jnp.float32
    )


def matmul_last(left, right):
    return lax.dot_general(
        left, right, (((1,), (1,)), ((), ())), preferred_element_type=jnp.float32
    )


def segment_numbers(lengths, count):
    endings = jnp.cumsum(lengths)
    places = jnp.arange(count, dtype=jnp.int32)
    return jnp.sum((places[:, None] >= endings[None, :]).astype(jnp.int32), axis=1)


def norm_forward(before, norm_gain, norm_shift):
    centred = before - jnp.mean(before, axis=-1, keepdims=True)
    inverse = lax.rsqrt(jnp.mean(centred * centred, axis=-1, keepdims=True) + EPSILON)
    normed = centred * inverse
    return (normed * norm_gain + norm_shift, normed, inverse)


def norm_backward(gradient, normed, inverse, norm_gain):
    scaled = gradient * norm_gain
    inner_sum = jnp.mean(scaled * normed, axis=-1, keepdims=True)
    before_grad = inverse * (scaled - jnp.mean(scaled, axis=-1, keepdims=True) - normed * inner_sum)
    return (before_grad, jnp.sum(gradient * normed, axis=0), jnp.sum(gradient, axis=0))


def split_heads(matrix):
    return matrix.reshape(matrix.shape[0], HEADS, HEAD_DIM)


def masked_scores(query_block, key_heads, segment_block, key_segment):
    scores = (
        jnp.einsum(
            "qhe,khe->hqk", split_heads(query_block), key_heads, preferred_element_type=jnp.float32
        )
        * SCORE_SCALE
    )
    allowed = segment_block[:, None] == key_segment[None, :]
    return jnp.where(allowed[None], scores, MASKED)


def attend_forward(queries, keys_in, values_in, query_segment, key_segment):
    row_count = queries.shape[0]
    block_rows = min(512, row_count)
    blocks = row_count // block_rows
    key_heads = split_heads(keys_in)
    value_heads = split_heads(values_in)

    def attend_block(pieces):
        query_block, segment_block = pieces
        scores = masked_scores(query_block, key_heads, segment_block, key_segment)
        highest = jnp.max(scores, axis=-1, keepdims=True)
        exponent = jnp.exp(scores - highest)
        totals = jnp.sum(exponent, axis=-1, keepdims=True)
        shares = (exponent / totals).astype(jnp.bfloat16)
        mixed = jnp.einsum("hqk,khe->qhe", shares, value_heads, preferred_element_type=jnp.float32)
        return (
            mixed.reshape(block_rows, HEADS * HEAD_DIM).astype(jnp.bfloat16),
            (highest + jnp.log(totals))[..., 0],
        )

    mixed, logsum = lax.map(
        attend_block,
        (queries.reshape(blocks, block_rows, -1), query_segment.reshape(blocks, block_rows)),
    )
    return (mixed.reshape(row_count, -1), logsum)


def attend_backward(queries, keys_in, values_in, mixed_grad, logsum, query_segment, key_segment):
    row_count = queries.shape[0]
    block_rows = min(512, row_count)
    blocks = row_count // block_rows
    key_heads = split_heads(keys_in)
    value_heads = split_heads(values_in)

    def backward_block(carried, pieces):
        key_sum, value_sum = carried
        query_block, grad_block, logsum_block, segment_block = pieces
        scores = masked_scores(query_block, key_heads, segment_block, key_segment)
        shares = jnp.exp(scores - logsum_block[..., None])
        grad_heads = split_heads(grad_block)
        share_grad = jnp.einsum(
            "qhe,khe->hqk", grad_heads, value_heads, preferred_element_type=jnp.float32
        )
        inner_sum = jnp.sum(shares * share_grad, axis=-1, keepdims=True)
        score_grad = (shares * (share_grad - inner_sum)).astype(jnp.bfloat16)
        query_grad = (
            jnp.einsum("hqk,khe->qhe", score_grad, key_heads, preferred_element_type=jnp.float32)
            * SCORE_SCALE
        )
        key_sum = (
            key_sum
            + jnp.einsum(
                "hqk,qhe->khe",
                score_grad,
                split_heads(query_block),
                preferred_element_type=jnp.float32,
            )
            * SCORE_SCALE
        )
        value_sum = value_sum + jnp.einsum(
            "hqk,qhe->khe",
            shares.astype(jnp.bfloat16),
            grad_heads,
            preferred_element_type=jnp.float32,
        )
        return ((key_sum, value_sum), query_grad.reshape(block_rows, HEADS * HEAD_DIM))

    zeros_init = jnp.zeros((keys_in.shape[0], HEADS, HEAD_DIM), jnp.float32)
    pieces = (
        queries.reshape(blocks, block_rows, -1),
        mixed_grad.reshape(blocks, block_rows, -1),
        logsum,
        query_segment.reshape(blocks, block_rows),
    )
    (key_sum, value_sum), query_grad = lax.scan(backward_block, (zeros_init, zeros_init), pieces)
    return (
        query_grad.reshape(row_count, -1),
        key_sum.reshape(keys_in.shape[0], -1),
        value_sum.reshape(values_in.shape[0], -1),
    )


def plain_body(
    tokens,
    memory,
    w_wide,
    w_tall,
    vecs,
    avg_wide,
    avg_tall,
    avg_vecs,
    tgt_lengths,
    src_lengths,
    cotangent,
):
    wide_all, tall_all, vector_all = (
        lax.all_gather(w_wide, ("wide", "narrow"), axis=0, tiled=True),
        lax.all_gather(w_tall, ("wide", "narrow"), axis=0, tiled=True),
        lax.all_gather(vecs, ("wide", "narrow"), axis=0, tiled=True),
    )
    vectors = vector_all.astype(jnp.float32)
    spread = FF // D
    offset = 6 + spread
    columns = [wide_all[:, index * D : (index + 1) * D] for index in range(8)]
    target_query, target_key, target_value, target_output = (
        columns[0],
        columns[1],
        columns[2],
        columns[3],
    )
    source_query, source_key, source_value, source_output = (
        columns[4],
        columns[5],
        columns[6],
        columns[7],
    )
    up_weight = wide_all[:, 8 * D :]
    down_weight = tall_all[:FF]
    slot_left = tall_all[FF : FF + D]
    slot_right = tall_all[FF + D :]
    up_bias = vectors[:, 6:offset].T.reshape(FF)
    row_count = tokens.shape[0]
    target_segment = segment_numbers(tgt_lengths[0], row_count)
    source_segment = segment_numbers(src_lengths[0], memory.shape[0])
    valid_rows = (target_segment < SEGS - 1).astype(jnp.float32)[:, None]
    follow = (
        jnp.concatenate([target_segment[1:], jnp.full((1,), -1, jnp.int32)]) == target_segment
    ).astype(jnp.float32)[:, None]
    queries_self = (matmul(tokens, target_query) + vectors[:, 0]).astype(jnp.bfloat16)
    keys_self = matmul(tokens, target_key).astype(jnp.bfloat16)
    values_self = (matmul(tokens, target_value) + vectors[:, 1]).astype(jnp.bfloat16)
    mixed_self, logsum_self = attend_forward(
        queries_self, keys_self, values_self, target_segment, target_segment
    )
    first, normed_first, inverse_first = norm_forward(
        tokens.astype(jnp.float32) + matmul(mixed_self, target_output) + vectors[:, 2],
        vectors[:, offset + 2],
        vectors[:, offset + 3],
    )
    first_low = first.astype(jnp.bfloat16)
    queries_cross = (matmul(first_low, source_query) + vectors[:, 3]).astype(jnp.bfloat16)
    keys_cross = matmul(memory, source_key).astype(jnp.bfloat16)
    values_cross = (matmul(memory, source_value) + vectors[:, 4]).astype(jnp.bfloat16)
    mixed_cross, logsum_cross = attend_forward(
        queries_cross, keys_cross, values_cross, target_segment, source_segment
    )
    second, normed_second, inverse_second = norm_forward(
        first + matmul(mixed_cross, source_output) + vectors[:, 5],
        vectors[:, offset + 4],
        vectors[:, offset + 5],
    )
    second_low = second.astype(jnp.bfloat16)
    hidden = matmul(second_low, up_weight) + up_bias
    active = jax.nn.gelu(hidden).astype(jnp.bfloat16)
    third, normed_third, inverse_third = norm_forward(
        second + matmul(active, down_weight) + vectors[:, offset],
        vectors[:, offset + 6],
        vectors[:, offset + 7],
    )
    third_low = third.astype(jnp.bfloat16)
    right_half = jnp.concatenate([third_low[1:], jnp.zeros((1, D), jnp.bfloat16)]) * follow.astype(
        jnp.bfloat16
    )
    slots = (
        (matmul(third_low, slot_left) + matmul(right_half, slot_right) + vectors[:, offset + 1])
        * valid_rows
    ).astype(jnp.bfloat16)
    seed_grad = cotangent * valid_rows.astype(jnp.bfloat16)
    grad_slot_bias = jnp.sum(seed_grad.astype(jnp.float32), axis=0)
    grad_left = matmul_first(third_low, seed_grad)
    grad_right = matmul_first(right_half, seed_grad)
    right_back = matmul_last(seed_grad, slot_right) * follow
    grad_third = matmul_last(seed_grad, slot_left) + jnp.concatenate(
        [jnp.zeros((1, D), jnp.float32), right_back[:-1]]
    )
    grad_pre_third, grad_gain_third, grad_shift_third = norm_backward(
        grad_third, normed_third, inverse_third, vectors[:, offset + 6]
    )
    pre_third_low = grad_pre_third.astype(jnp.bfloat16)
    grad_down = matmul_first(active, pre_third_low)
    grad_tall_all = jnp.concatenate([grad_down, grad_left, grad_right], axis=0)
    gelu_value, gelu_pull = jax.vjp(jax.nn.gelu, hidden)
    grad_hidden = gelu_pull(matmul_last(pre_third_low, down_weight))[0]
    hidden_low = grad_hidden.astype(jnp.bfloat16)
    grad_up = matmul_first(second_low, hidden_low)
    grad_second = grad_pre_third + matmul_last(hidden_low, up_weight)
    grad_pre_second, grad_gain_second, grad_shift_second = norm_backward(
        grad_second, normed_second, inverse_second, vectors[:, offset + 4]
    )
    pre_second_low = grad_pre_second.astype(jnp.bfloat16)
    grad_source_output = matmul_first(mixed_cross, pre_second_low)
    mixed_cross_grad = matmul_last(pre_second_low, source_output).astype(jnp.bfloat16)
    cross_query_grad, cross_key_grad, cross_value_grad = attend_backward(
        queries_cross,
        keys_cross,
        values_cross,
        mixed_cross_grad,
        logsum_cross,
        target_segment,
        source_segment,
    )
    cross_query_low = cross_query_grad.astype(jnp.bfloat16)
    cross_key_low = cross_key_grad.astype(jnp.bfloat16)
    cross_value_low = cross_value_grad.astype(jnp.bfloat16)
    grad_source_query = matmul_first(first_low, cross_query_low)
    grad_source_key = matmul_first(memory, cross_key_low)
    grad_source_value = matmul_first(memory, cross_value_low)
    grad_memory = matmul_last(cross_key_low, source_key) + matmul_last(
        cross_value_low, source_value
    )
    grad_first = grad_pre_second + matmul_last(cross_query_low, source_query)
    grad_pre_first, grad_gain_first, grad_shift_first = norm_backward(
        grad_first, normed_first, inverse_first, vectors[:, offset + 2]
    )
    pre_first_low = grad_pre_first.astype(jnp.bfloat16)
    grad_target_output = matmul_first(mixed_self, pre_first_low)
    mixed_self_grad = matmul_last(pre_first_low, target_output).astype(jnp.bfloat16)
    self_query_grad, self_key_grad, self_value_grad = attend_backward(
        queries_self,
        keys_self,
        values_self,
        mixed_self_grad,
        logsum_self,
        target_segment,
        target_segment,
    )
    self_query_low = self_query_grad.astype(jnp.bfloat16)
    self_key_low = self_key_grad.astype(jnp.bfloat16)
    self_value_low = self_value_grad.astype(jnp.bfloat16)
    grad_target_query = matmul_first(tokens, self_query_low)
    grad_target_key = matmul_first(tokens, self_key_low)
    grad_target_value = matmul_first(tokens, self_value_low)
    grad_tokens = (
        grad_pre_first
        + matmul_last(self_query_low, target_query)
        + matmul_last(self_key_low, target_key)
        + matmul_last(self_value_low, target_value)
    )
    grad_wide_all = jnp.concatenate(
        [
            grad_target_query,
            grad_target_key,
            grad_target_value,
            grad_target_output,
            grad_source_query,
            grad_source_key,
            grad_source_value,
            grad_source_output,
            grad_up,
        ],
        axis=1,
    )
    bias_front = jnp.stack(
        [
            jnp.sum(self_query_grad, axis=0),
            jnp.sum(self_value_grad, axis=0),
            jnp.sum(grad_pre_first, axis=0),
            jnp.sum(cross_query_grad, axis=0),
            jnp.sum(cross_value_grad, axis=0),
            jnp.sum(grad_pre_second, axis=0),
        ],
        axis=1,
    )
    bias_middle = jnp.sum(grad_hidden, axis=0).reshape(spread, D).T
    bias_back = jnp.stack(
        [
            jnp.sum(grad_pre_third, axis=0),
            grad_slot_bias,
            grad_gain_first,
            grad_shift_first,
            grad_gain_second,
            grad_shift_second,
            grad_gain_third,
            grad_shift_third,
        ],
        axis=1,
    )
    grad_vector_all = jnp.concatenate([bias_front, bias_middle, bias_back], axis=1)
    grad_wide, grad_tall, grad_vecs = (
        lax.psum_scatter(grad_wide_all, ("wide", "narrow"), scatter_dimension=0, tiled=True),
        lax.psum_scatter(grad_tall_all, ("wide", "narrow"), scatter_dimension=0, tiled=True),
        lax.psum_scatter(grad_vector_all, ("wide", "narrow"), scatter_dimension=0, tiled=True),
    )
    new_avg_wide = avg_wide + (w_wide.astype(jnp.float32) - avg_wide) / AVG_STEPS
    new_avg_tall = avg_tall + (w_tall.astype(jnp.float32) - avg_tall) / AVG_STEPS
    new_avg_vecs = avg_vecs + (vecs.astype(jnp.float32) - avg_vecs) / AVG_STEPS
    return (
        slots,
        grad_tokens,
        grad_memory,
        grad_wide,
        grad_tall,
        grad_vecs,
        new_avg_wide,
        new_avg_tall,
        new_avg_vecs,
    )


BF16 = jnp.bfloat16
F32 = jnp.float32
AUG = 80
BIG = 1e30
TILE = 256
MESH_IDS = pl.DeviceIdType.MESH
BIAS_OUT, GAIN = 10, 12
TALL_CUT = 3
OUT_SEMAPHORES = 24
PAIR = 6 * HEAD_DIM
PAIR_GROUPS = ((0,), (1,), (2, 3))
GATHER_STEPS = {
    0: ((0, 0),),
    1: ((1, 0), (0, 2), (1, 1), (2, 0), (0, 3),),
    2: ((9, 0),),
    4: ((3, 0),),
    5: ((1, 2), (2, 1), (1, 3),),
    7: ((4, 0),),
    9: ((3, 1), (5, 0), (2, 2), (2, 3),),
    11: ((4, 1),),
    12: ((6, 0), (9, 1), (3, 2),),
    13: ((5, 1), (7, 0),),
    14: ((3, 3),),
    16: ((4, 2),),
    19: ((6, 1),),
    20: ((4, 3),),
    21: ((8, 0),),
    23: ((5, 2),),
    25: ((7, 1),),
    26: ((5, 3),),
    28: ((6, 2),),
    30: ((8, 1), (6, 3),),
    32: ((9, 2),),
    33: ((7, 2),),
    35: ((9, 3), (8, 2), (7, 3), (8, 3),),
}
SUM_STEPS = {
    5: ((0, 0),),
    10: ((1, 0),),
    12: ((0, 1),),
    16: ((1, 1),),
    24: ((0, 2), (2, 0),),
    25: ((1, 2), (3, 0),),
    27: ((4, 0), (2, 1),),
    29: ((3, 1), (0, 3),),
    30: ((5, 0), (4, 1),),
    34: ((2, 2),),
    35: ((3, 2), (6, 0),),
    36: ((1, 3), (7, 0),),
    40: ((5, 1),),
    42: ((4, 2),),
    44: ((6, 1), (7, 1), (5, 2), (6, 2), (7, 2), (2, 3), (3, 3), (4, 3), (5, 3), (6, 3), (7, 3),),
}


def dot(left, right, left_dim, right_dim):
    return lax.dot_general(
        left, right, (((left_dim,), (right_dim,)), ((), ())), preferred_element_type=F32
    )


def bands(query_rows, key_rows, longest):
    found = []
    for start in range(0, query_rows, TILE):
        if longest is None:
            found.append((0, key_rows))
            continue
        low = max(0, (start - longest + 1) // TILE * TILE)
        high = min(key_rows, -(-(start + TILE + longest - 1) // TILE) * TILE)
        found.append((low, high))
    return found


def column_max(scores):
    rows, columns = scores.shape
    return jnp.max(
        jnp.max(scores.reshape(rows // 64, 64, columns), axis=0), axis=0, keepdims=True
    )


def split_three(value):
    high = value.astype(BF16).astype(F32)
    middle = (value - high).astype(BF16).astype(F32)
    low = (value - high - middle).astype(BF16).astype(F32)
    return high, middle, low


def feature_rows(base, first, parts):
    place = lax.broadcasted_iota(jnp.int32, base.shape, 0)
    for step, part in enumerate(parts):
        base = jnp.where(place == first + step, part, base)
    return base


def gelu_pair(u):
    scale = 0.7978845608028654
    inner = jnp.tanh(scale * (u + 0.044715 * (u * u * u)))
    half = 0.5 * (1.0 + inner)
    slope = half + 0.5 * u * (1.0 - inner * inner) * (scale * (1.0 + 3 * 0.044715 * (u * u)))
    return u * half, slope


def normalize(before, gain, shift):
    centred = before - jnp.mean(before, axis=-1, keepdims=True)
    inverse = lax.rsqrt(jnp.mean(centred * centred, axis=-1, keepdims=True) + EPSILON)
    normed = centred * inverse
    return normed * gain + shift, normed, inverse


def attention_forward(queries, keys, values, mixed, scores, ranges, heads, hooks):
    tiles = len(ranges)

    def put(head, tile):
        low, high = ranges[tile]
        scores[tile % 2][0 : high - low, :] = dot(
            keys[head, :, low:high], queries[head, :, tile * TILE : (tile + 1) * TILE], 0, 0
        )

    put(heads[0], 0)

    def one_head(head, carried):
        for tile, (low, high) in enumerate(ranges):
            if tile + 1 < tiles:
                put(head, tile + 1)
            else:
                put(jnp.minimum(head + 1, heads[1] - 1), 0)
            span = slice(tile * TILE, (tile + 1) * TILE)
            current = scores[tile % 2][0 : high - low, :]
            highest = column_max(current)
            shares = jnp.exp(current - highest).astype(BF16)
            gathered = dot(values[head, :, low:high], shares, 1, 0)
            total = gathered[HEAD_DIM : HEAD_DIM + 1]
            rows = pl.ds(pl.multiple_of(head * HEAD_DIM, HEAD_DIM), HEAD_DIM)
            mixed[rows, span] = (gathered[:HEAD_DIM] * (1.0 / total)).astype(BF16)
            queries[head, HEAD_DIM:, span] = feature_rows(
                queries[head, HEAD_DIM:, span].astype(F32),
                SEGS,
                split_three(-(highest + jnp.log(total))),
            ).astype(BF16)
        for at, hook in hooks.items():
            pl.when(head == at)(hook)
        return carried

    lax.fori_loop(heads[0], heads[1], one_head, 0)


def attention_backward(queries, keys, values, grads, outs, sums, shares, score_grads, ranges, hooks):
    key_rows = keys.shape[2]
    key_sum, value_sum = sums
    tiles = len(ranges)

    def put(head, tile):
        low, high = ranges[tile]
        span = slice(tile * TILE, (tile + 1) * TILE)
        share = jnp.exp(dot(keys[head, :, low:high], queries[head, :, span], 0, 0))
        share_grad = dot(values[head, :, low:high], grads[head, :, span], 0, 0)
        shares[tile % 2][0 : high - low, :] = share.astype(BF16)
        score_grads[tile % 2][0 : high - low, :] = (share * share_grad).astype(BF16)

    put(0, 0)

    def one_head(head, carried):
        key_sum[:, 0:key_rows] = jnp.zeros((HEAD_DIM, key_rows), F32)
        value_sum[:, 0:key_rows] = jnp.zeros((HEAD_DIM, key_rows), F32)
        query_out, key_out, value_out = [out(head) for out in outs]
        for tile, (low, high) in enumerate(ranges):
            if tile + 1 < tiles:
                put(head, tile + 1)
            else:
                put(jnp.minimum(head + 1, HEADS - 1), 0)
            span = slice(tile * TILE, (tile + 1) * TILE)
            share = shares[tile % 2][0 : high - low, :]
            score_grad = score_grads[tile % 2][0 : high - low, :]
            query_out[:, span] = (
                dot(keys[head, 0:HEAD_DIM, low:high], score_grad, 1, 0) * SCORE_SCALE
            ).astype(BF16)
            key_sum[:, low:high] += dot(queries[head, 0:HEAD_DIM, span], score_grad, 1, 1)
            value_sum[:, low:high] += dot(grads[head, 0:HEAD_DIM, span], share, 1, 1)
        key_out[...] = key_sum[:, 0:key_rows].astype(BF16)
        value_out[...] = value_sum[:, 0:key_rows].astype(BF16)
        for at, hook in hooks.items():
            pl.when(head == at)(hook)
        return carried

    lax.fori_loop(0, HEADS, one_head, 0)


class Exchange:
    def __init__(self, wide, narrow):
        self.narrow_bits = narrow.bit_length() - 1
        self.count = (wide * narrow).bit_length() - 1
        self.line = 1 << (self.count - 3)
        self.place = (lax.axis_index("wide"), lax.axis_index("narrow"))
        number = self.place[0] * narrow + self.place[1]
        self.bits = [(number >> bit) & 1 for bit in range(self.count)]
        self.own = tuple(self.bits[bit] for bit in reversed(range(self.count)))
        self.far = list(range(3, self.count))
        self.masks = [1, 2, 4, 6] + [other << 3 for other in range(1, self.line)]
        core = self.bits[0]
        self.first, self.second, self.both = {1: 1 - core, 2: core}, {1: core, 2: 1 - core}, {1: 1, 2: 1}

    def device(self, mask):
        wide, narrow = self.place
        return (wide ^ (mask >> self.narrow_bits), narrow ^ (mask & ((1 << self.narrow_bits) - 1)))

    def greet(self):
        barrier = pltpu.get_barrier_semaphore()
        for mask in self.masks:
            pl.semaphore_signal(
                barrier, inc=1, device_id=self.device(mask), device_id_type=MESH_IDS
            )

    def meet(self):
        pl.semaphore_wait(pltpu.get_barrier_semaphore(), len(self.masks))

    def neighbour(self, second):
        core = self.bits[0]
        take = core if not second else 1 - core
        one, other = self.device(2), self.device(4)
        return tuple(a + (b - a) * take for a, b in zip(one, other))

    def view(self, part, open_bits, flips=None):
        index = tuple(
            slice(None) if bit in open_bits else self.turned(bit, flips)
            for bit in reversed(range(self.count))
        )
        return part.ref.at[index + part.where]

    def turned(self, bit, flips):
        flip = (flips or {}).get(bit, 0)
        return self.bits[bit] + flip - 2 * self.bits[bit] * flip


class Part:
    def __init__(self, ref, rows=None, columns=None, buffers=(), outs=()):
        cut = lambda ends: slice(None) if ends is None else pl.ds(ends[0], ends[1] - ends[0])
        self.ref, self.where, self.buffers, self.outs = ref, (cut(rows), cut(columns)), buffers, outs


class Transfer:
    def __init__(self, net, pieces, send, receive):
        self.net, self.pieces, self.send, self.receive = net, pieces, send, receive
        self.line = tuple(range(4, 3 + net.line))

    def copy(self, piece, part, slot, source, target, device):
        return pltpu.make_async_remote_copy(
            source,
            target,
            self.send.at[piece, slot, part],
            self.receive.at[piece, slot, part],
            device_id=device,
            device_id_type=MESH_IDS,
        )

    def each(self, piece, stage, act):
        for number in range(len(self.pieces[piece])):
            for slot in self.slots(piece, stage):
                act(self.one(piece, number, slot))

    def begin(self, piece, slot):
        for number in range(len(self.pieces[piece])):
            self.one(piece, number, slot).start()

    def finish(self):
        for piece in range(len(self.pieces)):
            for stage in range(4):
                self.each(piece, stage, lambda copy: copy.wait_send())


class Gather(Transfer):
    def __init__(self, net, pieces, send, receive):
        super().__init__(net, pieces, send, receive)
        self.last = len(pieces) - 1

    def slots(self, piece, stage):
        if piece == 0:
            return (self.line, (), (0, 1, 2), (3,))[stage]
        if piece == self.last:
            return ((0, 1), (2,), self.line, (3,))[stage]
        return (self.line, (0,), (1, 2), (3,))[stage]

    def one(self, piece, number, slot):
        net, part = self.net, self.pieces[piece][number]
        lines = [] if piece == self.last else net.far
        if slot == 3:
            view, device = net.view(part, net.far + [1, 2]), net.device(1)
        elif slot > 3:
            near = [1, 2] if piece == self.last else []
            view, device = net.view(part, near), net.device((slot - 3) << 3)
        elif slot == 2 and piece == 0:
            view, device = net.view(part, lines), net.device(6)
        else:
            view = net.view(part, lines, net.first if slot == 2 else None)
            device = net.neighbour(slot > 0)
        return self.copy(piece, number, slot, view, view, device)

    def start(self, piece):
        if piece == self.last:
            self.begin(piece, 0)
            self.begin(piece, 1)
        else:
            self.each(piece, 0, lambda copy: copy.start())

    def step(self, piece, stage):
        self.each(piece, stage, lambda copy: copy.wait_recv())
        if piece == self.last and stage < 2:
            self.each(piece, stage + 1, lambda copy: copy.start())
        elif stage == 0:
            self.begin(piece, 0)
            self.begin(piece, 1)
            if piece == 0:
                self.begin(0, 2)
                self.start(1)
            if piece + 2 < self.last:
                self.start(piece + 2)
        elif stage == 1 and piece:
            self.begin(piece, 2)
        elif stage == 2:
            self.begin(piece, 3)


class Sum(Transfer):
    def slots(self, piece, stage):
        return ((0,), (1,), (2, 3), self.line)[stage]

    def one(self, piece, number, slot):
        net, part = self.net, self.pieces[piece][number]
        if slot == 0:
            view, device = net.view(part, net.far + [1, 2], {0: 1}), net.device(1)
        elif slot > 3:
            mask = (slot - 3) << 3
            view, device = net.view(part, [], {bit: mask >> bit & 1 for bit in net.far}), net.device(mask)
        else:
            view = net.view(part, net.far, (None, net.both, net.second, net.first)[slot])
            device = net.neighbour(slot < 3)
        target = part.buffers[4].at[slot - 4] if slot > 3 else part.buffers[slot]
        return self.copy(piece, number, slot, view, target, device)

    def start(self, piece):
        self.begin(piece, 0)

    def add(self, piece, stage):
        net = self.net
        if stage == 3:
            for part in self.pieces[piece]:
                value = part.ref[net.own + part.where].astype(F32)
                for other in range(1, net.line):
                    value = value + part.buffers[4][other - 1].astype(F32)
                for low, high, staged, out, semaphore in part.outs:
                    staged[...] = value[:, low:high]
                    pltpu.make_async_copy(staged, out, semaphore).start()
            return
        rest = net.far + ([1, 2] if stage == 0 else [])
        rest.sort()

        def one_shard(step, carried):
            place = {bit: (step >> at) & 1 for at, bit in enumerate(rest)}
            index = tuple(
                place[bit] if bit in place else net.turned(bit, net.first if stage == 1 else None)
                for bit in reversed(range(net.count))
            )
            arrived = tuple(place[bit] for bit in reversed(rest)) + (slice(None), slice(None))
            for part in self.pieces[piece]:
                where = index + part.where
                if stage == 2:
                    value = (
                        part.ref[where].astype(F32)
                        + part.buffers[2][arrived].astype(F32)
                        + part.buffers[3][arrived].astype(F32)
                    )
                else:
                    value = part.ref[where] + part.buffers[stage][arrived]
                part.ref[where] = value.astype(part.ref.dtype)
            return carried

        lax.fori_loop(0, 1 << len(rest), one_shard, 0, unroll=True)

    def step(self, piece, stage):
        self.each(piece, stage, lambda copy: copy.wait_recv())
        self.add(piece, stage)
        if stage == 0:
            self.begin(piece, 1)
            self.begin(piece, 2)
        elif stage == 1:
            self.begin(piece, 3)
        elif stage == 2:
            self.each(piece, 3, lambda copy: copy.start())

    def finish(self):
        super().finish()
        for piece in self.pieces:
            for part in piece:
                for _, _, staged, out, semaphore in part.outs:
                    pltpu.make_async_copy(staged, out, semaphore).wait()


class Plan:
    def __init__(self, transfer, table):
        self.transfer, self.table, self.stop = transfer, table, 0

    def next(self):
        taken = self.table.get(self.stop, ())
        self.stop += 1

        def act():
            for piece, stage in taken:
                self.transfer.step(piece, stage)

        return act if taken else None

    def now(self):
        act = self.next()
        if act:
            act()

    def loop(self, places):
        found = {place: self.next() for place in places}
        return {place: act for place, act in found.items() if act}


def layer_kernel(r, wide_size, narrow_size):
    net = Exchange(wide_size, narrow_size)
    net.greet()
    devices = wide_size * narrow_size
    wide7, tall7, vec7, gvec7 = r.wide, r.tall, r.vec, r.grad_vec
    wide = wide7.reshape(devices * wide7.shape[-2], wide7.shape[-1])
    tall = tall7.reshape(devices * tall7.shape[-2], tall7.shape[-1])
    slope7 = r.slope
    slope = slope7.reshape(devices * slope7.shape[-2], slope7.shape[-1])
    own_rows = (0, wide7.shape[-2])
    tokens, memory, seed, seed_next = r.tokens, r.memory, r.seed, r.seed_next
    rows, sources = tokens.shape[0], memory.shape[0]
    tiles = rows // TILE
    local = r.local

    wide_moves = [
        (block * D + pair * PAIR // 3, pair * PAIR + block * PAIR // 3, PAIR // 3)
        for pair in range(HEADS // 2)
        for block in range(3)
    ] + [(3 * D, 3 * D, wide7.shape[-1] - 3 * D)]
    loads = [
        pltpu.make_async_copy(
            r.w_wide.at[:, pl.ds(low, width)],
            wide7.at[net.own + (slice(None), pl.ds(high, width))],
            r.own_done.at[number],
        )
        for number, (low, high, width) in enumerate(wide_moves)
    ] + [
        pltpu.make_async_copy(r.w_tall, tall7.at[net.own], local.at[1]),
        pltpu.make_async_copy(r.vecs, vec7.at[net.own], local.at[2]),
        pltpu.make_async_copy(r.tokens_in, tokens, local.at[3]),
        pltpu.make_async_copy(r.memory_in, memory, local.at[4]),
        pltpu.make_async_copy(r.cotangent, seed, local.at[5]),
    ]
    for copy in loads:
        copy.start()

    tall_rows = tall7.shape[-2]
    tall_cuts = [(low, low + tall_rows // TALL_CUT) for low in range(0, tall_rows, tall_rows // TALL_CUT)]

    def wide_part(low, high):
        return [Part(wide7, None, (low, high))]

    gather = Gather(
        net,
        [
            wide_part(0, PAIR) + [Part(vec7)],
            wide_part(PAIR, 2 * PAIR),
            wide_part(2 * PAIR, 4 * PAIR),
            wide_part(3 * D, 5 * D),
            wide_part(5 * D, 7 * D),
            wide_part(7 * D, 9 * D),
            wide_part(9 * D, 12 * D),
        ]
        + [[Part(tall7, cut)] for cut in tall_cuts],
        r.gather_send,
        r.gather_receive,
    )
    plan = Plan(gather, GATHER_STEPS)
    out_semaphores = iter(range(OUT_SEMAPHORES))

    def out_of(low, high, staged, out):
        return (low, high, staged, out, r.out_done.at[next(out_semaphores)])

    def wide_out(low, high, start):
        columns = pl.ds(start, high - low)
        return out_of(low, high, r.out_wide.at[:, columns], r.grad_wide.at[:, columns])

    def wide_sum(low, high, buffers):
        return [Part(wide7, None, (low, high), buffers, [wide_out(0, high - low, low)])]

    def self_sum(pair):
        third = PAIR // 3
        outs = [
            wide_out(block * third, (block + 1) * third, block * D + pair * third)
            for block in range(3)
        ]
        columns = (pair * PAIR, (pair + 1) * PAIR)
        return [Part(slope7, own_rows, columns, r.in_self[pair], outs)]

    vec_out = out_of(0, 128, r.out_vec, r.grad_vecs)
    total = Sum(
        net,
        [
            [Part(tall7, None, None, r.in_tall, [out_of(0, D, r.out_tall, r.grad_tall)])],
            wide_sum(8 * D, 12 * D, r.in_up),
            wide_sum(3 * D, 8 * D, r.in_mid),
        ]
        + [self_sum(pair) for pair in range(HEADS // 2)]
        + [[Part(gvec7, None, None, r.in_vec, [vec_out])]],
        r.sum_send,
        r.sum_receive,
    )
    TALL, UP, MID, SELF = range(4)
    VECTORS = SELF + HEADS // 2
    sum_plan = Plan(total, SUM_STEPS)

    for copy in loads[:-3]:
        copy.wait()
    net.meet()
    gather.start(0)
    gather.start(gather.last)

    def endings(lengths):
        found, running = [], 0
        for index in range(SEGS):
            running = running + lengths[0, index]
            found.append(running)
        return found

    target_ends = endings(r.tgt_lengths)
    source_ends = endings(r.src_lengths)

    def chosen(ends, count):
        place = lax.broadcasted_iota(jnp.int32, (16, count), 1)
        segment = jnp.zeros((16, count), jnp.int32)
        for end in ends:
            segment = segment + (place >= end).astype(jnp.int32)
        return segment == lax.broadcasted_iota(jnp.int32, (16, count), 0)

    def query_features(ends, count):
        return jnp.where(chosen(ends, count), 1.0, 0.0).astype(BF16)

    def key_features(ends, count):
        row = lax.broadcasted_iota(jnp.int32, (16, count), 0)
        masked = jnp.where(chosen(ends, count), 0.0, -BIG)
        return jnp.where(row < SEGS, masked, jnp.where(row < SEGS + 3, 1.0, 0.0)).astype(BF16)

    def value_features(count):
        row = lax.broadcasted_iota(jnp.int32, (16, count), 0)
        return jnp.where(row < 3, 1.0, 0.0).astype(BF16)

    def every_head(ref, features):
        ref[:, HEAD_DIM:, :] = jnp.broadcast_to(features[None], (HEADS,) + features.shape)

    q, k, v, q2, k2, v2 = r.q, r.k, r.v, r.q2, r.k2, r.v2
    every_head(q, query_features(target_ends, rows))
    every_head(q2, query_features(target_ends, rows))
    every_head(k, key_features(target_ends, rows))
    every_head(k2, key_features(source_ends, sources))
    every_head(v, value_features(rows))
    every_head(v2, value_features(sources))
    plan.now()

    def position(tile):
        return tile * TILE + lax.broadcasted_iota(jnp.int32, (TILE, 1), 0)

    def valid(tile):
        return jnp.where(position(tile) < target_ends[SEGS - 2], 1.0, 0.0)

    def follow(tile):
        after = position(tile) + 1
        ended = after == target_ends[0]
        for end in target_ends[1:]:
            ended = ended | (after == end)
        return jnp.where(ended, 0.0, 1.0)

    def span(tile):
        return pl.ds(tile * TILE, TILE)

    shift, res = r.shift, r.res
    loads[-1].wait()
    shift[0:8, :] = jnp.zeros((8, D), F32)
    for tile in range(tiles):
        masked = seed[span(tile), :].astype(F32) * valid(tile)
        seed[span(tile), :] = masked.astype(BF16)
        shift[pl.ds(tile * TILE + 8, TILE), :] = masked * follow(tile)
    for tile in range(tiles):
        seed_next[span(tile), :] = shift[pl.ds(tile * TILE + 7, TILE), :].astype(BF16)
    r.grad_rows[...] = jnp.zeros_like(r.grad_rows)
    r.grad_columns[...] = jnp.zeros_like(r.grad_columns)
    loads[-3].wait()
    loads[-2].wait()

    def row(index):
        return r.row_vectors[index : index + 1, :]

    def column(index):
        return vec7[...].reshape(D, vec7.shape[-1])[:, index : index + 1].astype(F32)

    def heads_of(value):
        return value.reshape(value.shape[0] // HEAD_DIM, HEAD_DIM, value.shape[1])

    def scaled(value):
        return (value.astype(BF16).astype(F32) * SCORE_SCALE).astype(BF16)

    def wide_column(index):
        return wide[:, index * D : (index + 1) * D]

    self_ranges = bands(rows, rows, 512)
    cross_ranges = bands(rows, sources, None)
    a, a2 = r.mixed, r.mixed2
    bias_rows = PAIR // 3
    identity = lax.broadcasted_iota(jnp.int32, (D, D), 0) == lax.broadcasted_iota(
        jnp.int32, (D, D), 1
    )
    identity = jnp.where(identity, 1.0, 0.0).astype(BF16)
    for index, pairs in enumerate(PAIR_GROUPS):
        plan.now()
        if index == 0:
            r.row_vectors[0 : vec7.shape[-1], :] = dot(
                vec7[...].reshape(D, vec7.shape[-1]), identity, 0, 0
            )
        biases = []
        for pair in pairs:
            place = slice(pair * bias_rows, (pair + 1) * bias_rows)
            biases += [column(0)[place], jnp.zeros((bias_rows, 1), F32), column(1)[place]]
        bias = jnp.concatenate(biases, axis=0)
        for tile in range(tiles):
            both = dot(
                wide[:, pairs[0] * PAIR : (pairs[-1] + 1) * PAIR], tokens[span(tile), :], 0, 1
            )
            both = (both + bias).astype(BF16)
            for place, pair in enumerate(pairs):
                for block, ref in enumerate((q, k, v)):
                    start = place * PAIR + block * bias_rows
                    value = both[start : start + bias_rows]
                    if block == 0:
                        value = (value.astype(F32) * SCORE_SCALE).astype(BF16)
                    ref[2 * pair : 2 * pair + 2, 0:HEAD_DIM, span(tile)] = heads_of(value)
        plan.now()
        heads = (2 * pairs[0], 2 * pairs[-1] + 2)
        attention_forward(
            q,
            k,
            v,
            a,
            r.scores,
            self_ranges,
            heads,
            plan.loop(range(*heads)),
        )

    normed, low, inverse = r.normed, r.low, r.inverse

    def norm_tile(index, tile, before):
        out, unit, rho = normalize(before, row(GAIN + 2 * index), row(GAIN + 2 * index + 1))
        normed[index][span(tile), :] = unit.astype(BF16)
        inverse[span(tile), index : index + 1] = rho
        low[index][span(tile), :] = out.astype(BF16)
        return out

    plan.now()
    for tile in range(tiles):
        before = (
            tokens[span(tile), :].astype(F32) + dot(a[:, span(tile)], wide_column(3), 0, 0) + row(2)
        )
        out = norm_tile(0, tile, before)
        res[span(tile), :] = out
        q2[:, 0:HEAD_DIM, span(tile)] = heads_of(
            scaled(dot(wide_column(4), out.astype(BF16), 0, 1) + column(3))
        )
        plan.now()
    plan.now()
    for tile in range(sources // TILE):
        part = memory[span(tile), :]
        k2[:, 0:HEAD_DIM, span(tile)] = heads_of(dot(wide_column(5), part, 0, 1).astype(BF16))
        v2[:, 0:HEAD_DIM, span(tile)] = heads_of(
            (dot(wide_column(6), part, 0, 1) + column(4)).astype(BF16)
        )
    attention_forward(
        q2,
        k2,
        v2,
        a2,
        r.scores,
        cross_ranges,
        (0, HEADS),
        plan.loop(range(HEADS)),
    )
    active = r.active
    plan.now()
    for tile in range(tiles):
        before = res[span(tile), :] + dot(a2[:, span(tile)], wide_column(7), 0, 0) + row(5)
        out = norm_tile(1, tile, before)
        res[span(tile), :] = out
        for block in range(FF // D):
            if tile == 0 and block == 1:
                plan.now()
            columns = slice(block * D, (block + 1) * D)
            u = dot(out.astype(BF16), wide_column(8 + block), 1, 0) + row(6 + block)
            value, derivative = gelu_pair(u)
            active[span(tile), columns] = value.astype(BF16)
            slope[span(tile), columns] = derivative.astype(BF16)
        plan.now()
    plan.now()
    slot_left = tall.at[pl.ds(FF, D), :]
    slot_right = tall.at[pl.ds(FF + D, D), :]
    for tile in range(tiles):
        before = (
            res[span(tile), :] + dot(active[span(tile), :], tall[0:FF, :], 1, 0) + row(BIAS_OUT)
        )
        norm_tile(2, tile, before)
    low_grad = r.low_grad
    gather.finish()

    grad_rows, grad_columns = r.grad_rows, r.grad_columns

    def add_row(index, value):
        grad_rows[index : index + 1, :] += jnp.sum(value, axis=0, keepdims=True)

    def norm_back(index, tile, gradient, bias_row):
        gain = row(GAIN + 2 * index)
        unit = normed[index][span(tile), :].astype(F32)
        scaled_grad = gradient * gain
        inner = jnp.mean(scaled_grad * unit, axis=-1, keepdims=True)
        before = inverse[span(tile), index : index + 1] * (
            scaled_grad - jnp.mean(scaled_grad, axis=-1, keepdims=True) - unit * inner
        )
        add_row(GAIN + 2 * index, gradient * unit)
        add_row(GAIN + 2 * index + 1, gradient)
        add_row(bias_row, before)
        res[span(tile), :] = before
        low_grad[span(tile), :] = before.astype(BF16)

    for tile in range(tiles):
        part = seed[span(tile), :]
        add_row(BIAS_OUT + 1, part.astype(F32))
        gradient = dot(part, slot_left[...], 1, 1) + dot(
            seed_next[span(tile), :], slot_right[...], 1, 1
        )
        norm_back(2, tile, gradient, BIAS_OUT)
    grad_left = dot(low[2][...], seed[...], 0, 0).astype(BF16)
    seed[0:D, :] = slot_left[...]
    slot_left[...] = grad_left
    grad_right = dot(low[2][...], seed_next[...], 0, 0).astype(BF16)
    seed[D : 2 * D, :] = slot_right[...]
    slot_right[...] = grad_right
    for block in range(FF // D):
        columns = slice(block * D, (block + 1) * D)
        for tile in range(tiles):
            grad = dot(low_grad[span(tile), :], tall[columns, :], 1, 1) * slope[
                span(tile), columns
            ].astype(F32)
            add_row(6 + block, grad)
            slope[span(tile), columns] = grad.astype(BF16)
        tall[columns, :] = dot(active[:, columns], low_grad[...], 0, 0).astype(BF16)
    total.start(TALL)
    for tile in range(tiles):
        gradient = res[span(tile), :] + dot(
            slope[span(tile), :], wide[:, 8 * D : 8 * D + FF], 1, 1
        )
        norm_back(1, tile, gradient, 5)
        sum_plan.now()
    for block in range(FF // D):
        columns = slice(block * D, (block + 1) * D)
        wide[:, 8 * D + block * D : 8 * D + (block + 1) * D] = dot(
            low[1][...], slope[:, columns], 0, 0
        ).astype(BF16)
        if block == FF // D - 1:
            total.start(UP)
        sum_plan.now()
    grads = r.mixed_grad

    def mixed_back(weight_index, mixed):
        for tile in range(tiles):
            grad = dot(wide_column(weight_index), low_grad[span(tile), :], 1, 1).astype(BF16)
            grads[:, 0:HEAD_DIM, span(tile)] = heads_of(grad)
            inner = jnp.sum(
                heads_of(grad.astype(F32) * mixed[:, span(tile)].astype(F32)),
                axis=1,
                keepdims=True,
            )
            place = lax.broadcasted_iota(jnp.int32, (HEADS, 16, TILE), 1)
            features = jnp.zeros((HEADS, 16, TILE), F32)
            for step, part in enumerate(split_three(-inner)):
                features = jnp.where(place == step, part, features)
            grads[:, HEAD_DIM:, span(tile)] = features.astype(BF16)
        wide[:, weight_index * D : (weight_index + 1) * D] = dot(
            mixed[...], low_grad[...], 1, 0
        ).astype(BF16)

    mixed_back(7, a2)
    sum_plan.now()
    dq2 = active.at[pl.ds(0, D), pl.ds(0, rows)]
    dk2 = active.at[pl.ds(D, D), pl.ds(0, sources)]
    dv2 = active.at[pl.ds(D, D), pl.ds(rows, sources)]

    def head_rows(ref):
        def of(head):
            return ref.at[pl.ds(pl.multiple_of(head * HEAD_DIM, HEAD_DIM), HEAD_DIM), :]

        return of

    sums = (r.key_sum, r.value_sum)
    attention_backward(
        q2,
        k2,
        v2,
        grads,
        [head_rows(ref) for ref in (dq2, dk2, dv2)],
        sums,
        r.shares,
        r.score_grads,
        cross_ranges,
        sum_plan.loop(range(HEADS)),
    )

    def column_sum(index, value):
        grad_columns[:, index : index + 1] += jnp.sum(value.astype(F32), axis=1, keepdims=True)

    for tile in range(tiles):
        gradient = res[span(tile), :] + dot(dq2[:, span(tile)], wide_column(4), 0, 1)
        norm_back(0, tile, gradient, 2)
        sum_plan.now()
    shift[0:sources, :] = dot(dk2[...], wide_column(5), 0, 1) + dot(dv2[...], wide_column(6), 0, 1)
    memory_copy = pltpu.make_async_copy(
        shift.at[pl.ds(0, sources), :], r.grad_memory, local.at[10]
    )
    memory_copy.start()
    wide[:, 5 * D : 6 * D] = dot(memory[...], dk2[...], 0, 1).astype(BF16)
    wide[:, 6 * D : 7 * D] = dot(memory[...], dv2[...], 0, 1).astype(BF16)
    sum_plan.now()
    wide[:, 4 * D : 5 * D] = dot(low[0][...], dq2[...], 0, 1).astype(BF16)
    column_sum(3, dq2[...])
    column_sum(4, dv2[...])
    mixed_back(3, a)
    total.start(MID)
    sum_plan.now()

    def pair_rows(block):
        def of(head):
            pair = head // 2
            row = pair % 2 * PAIR + block * (PAIR // 3) + head % 2 * HEAD_DIM
            start = pl.multiple_of(pair // 2 * rows, rows)
            return active.at[pl.ds(pl.multiple_of(row, HEAD_DIM), HEAD_DIM), pl.ds(start, rows)]

        return of

    def pair_grad(pair):
        return active[pair % 2 * PAIR : (pair % 2 + 1) * PAIR, pair // 2 * rows : (pair // 2 + 1) * rows]

    def start_pair(pair):
        where = (slice(None),) * net.count + (
            slice(0, own_rows[1]),
            slice(pair * PAIR, (pair + 1) * PAIR),
        )
        slope7[where] = (
            dot(tokens[...], pair_grad(pair), 0, 1)
            .astype(BF16)
            .reshape(slope7.shape[: net.count] + (own_rows[1], PAIR))
        )
        total.start(SELF + pair)

    def start_vectors():
        for pair in range(HEADS // 2):
            place = slice(pair * bias_rows, (pair + 1) * bias_rows)
            grad = pair_grad(pair).astype(F32)
            for index, block in ((0, 0), (1, 2)):
                grad_columns[place, index : index + 1] = jnp.sum(
                    grad[block * bias_rows : (block + 1) * bias_rows], axis=1, keepdims=True
                )
        turned = jnp.transpose(r.grad_rows[...]) + grad_columns[...]
        gvec7[...] = turned.reshape(gvec7.shape)
        total.start(VECTORS)

    hooks = {}
    for head in range(HEADS):
        act = sum_plan.next()

        def hook(head=head, act=act):
            if head % 2 and head < HEADS - 1:
                start_pair(head // 2)
            if act:
                act()

        if act or (head % 2 and head < HEADS - 1):
            hooks[head] = hook
    attention_backward(
        q,
        k,
        v,
        grads,
        [pair_rows(block) for block in range(3)],
        sums,
        r.shares,
        r.score_grads,
        self_ranges,
        hooks,
    )
    start_pair(HEADS // 2 - 1)
    start_vectors()
    sum_plan.now()

    memory_copy.wait()
    shift[rows : rows + 8, :] = jnp.zeros((8, D), F32)
    for tile in range(tiles):
        shift[span(tile), :] = dot(low[2][span(tile), :], seed[D : 2 * D, :], 1, 0)
        sum_plan.now()
    token_copies = []
    for tile in range(tiles):
        low_grad[span(tile), :] = (
            (
                dot(low[2][span(tile), :], seed[0:D, :], 1, 0)
                + follow(tile) * shift[pl.ds(tile * TILE + 1, TILE), :]
                + row(BIAS_OUT + 1)
            )
            * valid(tile)
        ).astype(BF16)
        copy = pltpu.make_async_copy(
            low_grad.at[span(tile), :], r.slots.at[span(tile), :], local.at[6 + tile]
        )
        copy.start()
        token_copies.append(copy)
        sum_plan.now()
    for tile in range(tiles):
        value = res[span(tile), :]
        for side in range(2):
            value = value + dot(
                active[0 : 2 * PAIR, pl.ds(side * rows + tile * TILE, TILE)],
                wide[:, 2 * side * PAIR : 2 * (side + 1) * PAIR],
                0,
                1,
            )
        res[span(tile), :] = value
        copy = pltpu.make_async_copy(
            res.at[span(tile), :], r.grad_tokens.at[span(tile), :], local.at[12 + tile]
        )
        copy.start()
        token_copies.append(copy)
        sum_plan.now()
    sum_plan.now()
    total.finish()
    for copy in token_copies:
        copy.wait()


def finish_kernel(*refs):
    given, results, held = refs[:12], refs[12:21], refs[21:33]
    vec_out, semaphores = refs[33], refs[34]
    loads = [
        pltpu.make_async_copy(source, target, semaphores.at[index])
        for index, (source, target) in enumerate(zip(given, held))
    ]
    for copy in loads:
        copy.start()
    stores = []

    def store(index, source):
        copy = pltpu.make_async_copy(source, results[index], semaphores.at[12 + index])
        copy.start()
        stores.append(copy)

    for index in range(12):
        loads[index].wait()
        if index < 5:
            store(index, held[index])
        elif index == 5:
            vec_out[...] = held[5][:, : vec_out.shape[1]]
            store(5, vec_out)
        elif index >= 9:
            average = held[index - 3]
            average[...] += (held[index][...].astype(F32) - average[...]) / AVG_STEPS
            store(index - 3, average)
    for copy in stores:
        copy.wait()


def fused_body(
    wide_size,
    narrow_size,
    tokens,
    memory,
    w_wide,
    w_tall,
    vecs,
    avg_wide,
    avg_tall,
    avg_vecs,
    tgt_lengths,
    src_lengths,
    cotangent,
):
    count = (wide_size * narrow_size).bit_length() - 1
    rows, sources = tokens.shape[0], memory.shape[0]
    wide_rows, wide_columns = w_wide.shape
    tall_rows = w_tall.shape[0]
    vec_rows = vecs.shape[0]
    bits = (2,) * count
    hbm = pl.BlockSpec(memory_space=pl.ANY)
    smem = pl.BlockSpec(memory_space=pltpu.SMEM)
    inputs = dict(
        tgt_lengths=tgt_lengths,
        src_lengths=src_lengths,
        tokens_in=tokens,
        memory_in=memory,
        cotangent=cotangent,
        w_wide=w_wide,
        w_tall=w_tall,
        vecs=vecs,
    )
    outputs = dict(
        slots=jax.ShapeDtypeStruct((rows, D), BF16),
        grad_tokens=jax.ShapeDtypeStruct((rows, D), F32),
        grad_memory=jax.ShapeDtypeStruct((sources, D), F32),
        grad_wide=jax.ShapeDtypeStruct((wide_rows, wide_columns), F32),
        grad_tall=jax.ShapeDtypeStruct((tall_rows, D), F32),
        grad_vecs=jax.ShapeDtypeStruct((vec_rows, 128), F32),
    )

    def arrivals(shape, dtype=BF16):
        line = (1 << (count - 3)) - 1
        far = bits[3:]
        return [
            pltpu.VMEM(lead + shape, dtype) for lead in (bits[1:], far, far, far, (line,))
        ]

    scratch = dict(
        wide=pltpu.VMEM(bits + (wide_rows, wide_columns), BF16),
        tall=pltpu.VMEM(bits + (tall_rows, D), BF16),
        vec=pltpu.VMEM(bits + vecs.shape, BF16),
        grad_vec=pltpu.VMEM(bits + (vec_rows, 128), F32),
        tokens=pltpu.VMEM((rows, D), BF16),
        memory=pltpu.VMEM((sources, D), BF16),
        seed=pltpu.VMEM((rows, D), BF16),
        seed_next=pltpu.VMEM((rows, D), BF16),
        q=pltpu.VMEM((HEADS, AUG, rows), BF16),
        k=pltpu.VMEM((HEADS, AUG, rows), BF16),
        v=pltpu.VMEM((HEADS, AUG, rows), BF16),
        q2=pltpu.VMEM((HEADS, AUG, rows), BF16),
        k2=pltpu.VMEM((HEADS, AUG, sources), BF16),
        v2=pltpu.VMEM((HEADS, AUG, sources), BF16),
        mixed_grad=pltpu.VMEM((HEADS, AUG, rows), BF16),
        mixed=pltpu.VMEM((D, rows), BF16),
        mixed2=pltpu.VMEM((D, rows), BF16),
        active=pltpu.VMEM((rows, FF), BF16),
        slope=pltpu.VMEM(bits + (rows >> count, FF), BF16),
        res=pltpu.VMEM((rows, D), F32),
        low_grad=pltpu.VMEM((rows, D), BF16),
        shift=pltpu.VMEM((rows + 8, D), F32),
        key_sum=pltpu.VMEM((HEAD_DIM, rows), F32),
        value_sum=pltpu.VMEM((HEAD_DIM, rows), F32),
        inverse=pltpu.VMEM((rows, 128), F32),
        row_vectors=pltpu.VMEM((24, D), F32),
        grad_rows=pltpu.VMEM((128, D), F32),
        grad_columns=pltpu.VMEM((D, 128), F32),
        out_wide=pltpu.VMEM((wide_rows, wide_columns), F32),
        out_tall=pltpu.VMEM((tall_rows, D), F32),
        out_vec=pltpu.VMEM((vec_rows, 128), F32),
        normed=[pltpu.VMEM((rows, D), BF16) for _ in range(3)],
        low=[pltpu.VMEM((rows, D), BF16) for _ in range(3)],
        scores=[
            pltpu.VMEM((max(high - low for low, high in bands(rows, rows, 512)), TILE), F32)
            for _ in range(2)
        ],
        shares=[pltpu.VMEM((rows, TILE), BF16) for _ in range(2)],
        score_grads=[pltpu.VMEM((rows, TILE), BF16) for _ in range(2)],
        in_tall=arrivals((tall_rows, D)),
        in_up=arrivals((wide_rows, FF)),
        in_mid=arrivals((wide_rows, 5 * D)),
        in_self=[arrivals((wide_rows, PAIR)) for _ in range(HEADS // 2)],
        in_vec=arrivals((vec_rows, 128), F32),
        local=pltpu.SemaphoreType.DMA((20,)),
        own_done=pltpu.SemaphoreType.DMA((3 * HEADS // 2 + 1,)),
        out_done=pltpu.SemaphoreType.DMA((OUT_SEMAPHORES,)),
        gather_send=pltpu.SemaphoreType.DMA((7 + TALL_CUT, 3 + (1 << (count - 3)), 2)),
        gather_receive=pltpu.SemaphoreType.DMA((7 + TALL_CUT, 3 + (1 << (count - 3)), 2)),
        sum_send=pltpu.SemaphoreType.DMA((4 + HEADS // 2, 3 + (1 << (count - 3)), 1)),
        sum_receive=pltpu.SemaphoreType.DMA((4 + HEADS // 2, 3 + (1 << (count - 3)), 1)),
    )
    scratch_leaves, scratch_tree = jax.tree.flatten(scratch)
    input_leaves, output_leaves = list(inputs.values()), list(outputs.values())
    names = list(inputs) + list(outputs)
    spec = [smem if value.dtype == jnp.int32 else hbm for value in input_leaves]

    def kernel(*refs):
        held = dict(zip(names, refs))
        held.update(jax.tree.unflatten(scratch_tree, refs[len(names) :]))
        layer_kernel(types.SimpleNamespace(**held), wide_size, narrow_size)

    slots, grad_tokens, grad_memory, grad_wide, grad_tall, grad_vecs = pl.pallas_call(
        kernel,
        out_shape=output_leaves,
        in_specs=spec,
        out_specs=[hbm] * len(outputs),
        scratch_shapes=scratch_leaves,
        compiler_params=pltpu.CompilerParams(
            collective_id=0, has_side_effects=True, vmem_limit_bytes=67_000_000
        ),
    )(*input_leaves)
    done = [slots, grad_tokens, grad_memory, grad_wide, grad_tall, grad_vecs]
    done += [avg_wide, avg_tall, avg_vecs, w_wide, w_tall, vecs]
    shapes = outputs | dict(grad_vecs=jax.ShapeDtypeStruct(vecs.shape, F32))
    return pl.pallas_call(
        finish_kernel,
        out_shape=list(shapes.values())
        + [jax.ShapeDtypeStruct(value.shape, F32) for value in (avg_wide, avg_tall, avg_vecs)],
        in_specs=[hbm] * len(done),
        out_specs=[hbm] * 9,
        scratch_shapes=[pltpu.VMEM(value.shape, value.dtype) for value in done]
        + [pltpu.VMEM(vecs.shape, F32), pltpu.SemaphoreType.DMA((21,))],
    )(*done)


def solution(mesh):
    in_specs = (
        P(("wide", "narrow"), None),
        P(("wide", "narrow"), None),
        P(("wide", "narrow"), None),
        P(("wide", "narrow"), None),
        P(("wide", "narrow"), None),
        P(("wide", "narrow"), None),
        P(("wide", "narrow"), None),
        P(("wide", "narrow"), None),
        P(("wide", "narrow"), None),
        P(("wide", "narrow"), None),
        P(("wide", "narrow"), None),
    )
    out_specs = (
        P(("wide", "narrow"), None),
        P(("wide", "narrow"), None),
        P(("wide", "narrow"), None),
        P(("wide", "narrow"), None),
        P(("wide", "narrow"), None),
        P(("wide", "narrow"), None),
        P(("wide", "narrow"), None),
        P(("wide", "narrow"), None),
        P(("wide", "narrow"), None),
    )
    devices = mesh.shape["wide"] * mesh.shape["narrow"]
    bits = devices.bit_length() - 1

    def body(*args):
        if args[2].shape[0] % 16 or args[3].shape[0] % 16 or devices != 1 << bits or bits < 3:
            return plain_body(*args)
        return fused_body(mesh.shape["wide"], mesh.shape["narrow"], *args)

    return jax.shard_map(body, mesh=mesh, in_specs=in_specs, out_specs=out_specs, check_vma=False)
```

```python
import types

import jax
import jax.numpy as jnp
from jax import lax
from jax.experimental import pallas as pl
from jax.experimental.pallas import tpu as pltpu
from jax.sharding import PartitionSpec as P

D = 512
HEADS = 8
HEAD_DIM = 64
FF = 2048
SEGS = 6
AVG_STEPS = 4


SCORE_SCALE = 0.125
EPSILON = 1e-05
MASKED = -1e30


def matmul(left, right):
    return jnp.dot(left, right, preferred_element_type=jnp.float32)


def matmul_first(left, right):
    return lax.dot_general(
        left, right, (((0,), (0,)), ((), ())), preferred_element_type=jnp.float32
    )


def matmul_last(left, right):
    return lax.dot_general(
        left, right, (((1,), (1,)), ((), ())), preferred_element_type=jnp.float32
    )


def segment_numbers(lengths, count):
    endings = jnp.cumsum(lengths)
    places = jnp.arange(count, dtype=jnp.int32)
    return jnp.sum((places[:, None] >= endings[None, :]).astype(jnp.int32), axis=1)


def norm_forward(before, norm_gain, norm_shift):
    centred = before - jnp.mean(before, axis=-1, keepdims=True)
    inverse = lax.rsqrt(jnp.mean(centred * centred, axis=-1, keepdims=True) + EPSILON)
    normed = centred * inverse
    return (normed * norm_gain + norm_shift, normed, inverse)


def norm_backward(gradient, normed, inverse, norm_gain):
    scaled = gradient * norm_gain
    inner_sum = jnp.mean(scaled * normed, axis=-1, keepdims=True)
    before_grad = inverse * (scaled - jnp.mean(scaled, axis=-1, keepdims=True) - normed * inner_sum)
    return (before_grad, jnp.sum(gradient * normed, axis=0), jnp.sum(gradient, axis=0))


def split_heads(matrix):
    return matrix.reshape(matrix.shape[0], HEADS, HEAD_DIM)


def masked_scores(query_block, key_heads, segment_block, key_segment):
    scores = (
        jnp.einsum(
            "qhe,khe->hqk", split_heads(query_block), key_heads, preferred_element_type=jnp.float32
        )
        * SCORE_SCALE
    )
    allowed = segment_block[:, None] == key_segment[None, :]
    return jnp.where(allowed[None], scores, MASKED)


def attend_forward(queries, keys_in, values_in, query_segment, key_segment):
    row_count = queries.shape[0]
    block_rows = min(512, row_count)
    blocks = row_count // block_rows
    key_heads = split_heads(keys_in)
    value_heads = split_heads(values_in)

    def attend_block(pieces):
        query_block, segment_block = pieces
        scores = masked_scores(query_block, key_heads, segment_block, key_segment)
        highest = jnp.max(scores, axis=-1, keepdims=True)
        exponent = jnp.exp(scores - highest)
        totals = jnp.sum(exponent, axis=-1, keepdims=True)
        shares = (exponent / totals).astype(jnp.bfloat16)
        mixed = jnp.einsum("hqk,khe->qhe", shares, value_heads, preferred_element_type=jnp.float32)
        return (
            mixed.reshape(block_rows, HEADS * HEAD_DIM).astype(jnp.bfloat16),
            (highest + jnp.log(totals))[..., 0],
        )

    mixed, logsum = lax.map(
        attend_block,
        (queries.reshape(blocks, block_rows, -1), query_segment.reshape(blocks, block_rows)),
    )
    return (mixed.reshape(row_count, -1), logsum)


def attend_backward(queries, keys_in, values_in, mixed_grad, logsum, query_segment, key_segment):
    row_count = queries.shape[0]
    block_rows = min(512, row_count)
    blocks = row_count // block_rows
    key_heads = split_heads(keys_in)
    value_heads = split_heads(values_in)

    def backward_block(carried, pieces):
        key_sum, value_sum = carried
        query_block, grad_block, logsum_block, segment_block = pieces
        scores = masked_scores(query_block, key_heads, segment_block, key_segment)
        shares = jnp.exp(scores - logsum_block[..., None])
        grad_heads = split_heads(grad_block)
        share_grad = jnp.einsum(
            "qhe,khe->hqk", grad_heads, value_heads, preferred_element_type=jnp.float32
        )
        inner_sum = jnp.sum(shares * share_grad, axis=-1, keepdims=True)
        score_grad = (shares * (share_grad - inner_sum)).astype(jnp.bfloat16)
        query_grad = (
            jnp.einsum("hqk,khe->qhe", score_grad, key_heads, preferred_element_type=jnp.float32)
            * SCORE_SCALE
        )
        key_sum = (
            key_sum
            + jnp.einsum(
                "hqk,qhe->khe",
                score_grad,
                split_heads(query_block),
                preferred_element_type=jnp.float32,
            )
            * SCORE_SCALE
        )
        value_sum = value_sum + jnp.einsum(
            "hqk,qhe->khe",
            shares.astype(jnp.bfloat16),
            grad_heads,
            preferred_element_type=jnp.float32,
        )
        return ((key_sum, value_sum), query_grad.reshape(block_rows, HEADS * HEAD_DIM))

    zeros_init = jnp.zeros((keys_in.shape[0], HEADS, HEAD_DIM), jnp.float32)
    pieces = (
        queries.reshape(blocks, block_rows, -1),
        mixed_grad.reshape(blocks, block_rows, -1),
        logsum,
        query_segment.reshape(blocks, block_rows),
    )
    (key_sum, value_sum), query_grad = lax.scan(backward_block, (zeros_init, zeros_init), pieces)
    return (
        query_grad.reshape(row_count, -1),
        key_sum.reshape(keys_in.shape[0], -1),
        value_sum.reshape(values_in.shape[0], -1),
    )


def plain_body(
    tokens,
    memory,
    w_wide,
    w_tall,
    vecs,
    avg_wide,
    avg_tall,
    avg_vecs,
    tgt_lengths,
    src_lengths,
    cotangent,
):
    wide_all, tall_all, vector_all = (
        lax.all_gather(w_wide, ("wide", "narrow"), axis=0, tiled=True),
        lax.all_gather(w_tall, ("wide", "narrow"), axis=0, tiled=True),
        lax.all_gather(vecs, ("wide", "narrow"), axis=0, tiled=True),
    )
    vectors = vector_all.astype(jnp.float32)
    spread = FF // D
    offset = 6 + spread
    columns = [wide_all[:, index * D : (index + 1) * D] for index in range(8)]
    target_query, target_key, target_value, target_output = (
        columns[0],
        columns[1],
        columns[2],
        columns[3],
    )
    source_query, source_key, source_value, source_output = (
        columns[4],
        columns[5],
        columns[6],
        columns[7],
    )
    up_weight = wide_all[:, 8 * D :]
    down_weight = tall_all[:FF]
    slot_left = tall_all[FF : FF + D]
    slot_right = tall_all[FF + D :]
    up_bias = vectors[:, 6:offset].T.reshape(FF)
    row_count = tokens.shape[0]
    target_segment = segment_numbers(tgt_lengths[0], row_count)
    source_segment = segment_numbers(src_lengths[0], memory.shape[0])
    valid_rows = (target_segment < SEGS - 1).astype(jnp.float32)[:, None]
    follow = (
        jnp.concatenate([target_segment[1:], jnp.full((1,), -1, jnp.int32)]) == target_segment
    ).astype(jnp.float32)[:, None]
    queries_self = (matmul(tokens, target_query) + vectors[:, 0]).astype(jnp.bfloat16)
    keys_self = matmul(tokens, target_key).astype(jnp.bfloat16)
    values_self = (matmul(tokens, target_value) + vectors[:, 1]).astype(jnp.bfloat16)
    mixed_self, logsum_self = attend_forward(
        queries_self, keys_self, values_self, target_segment, target_segment
    )
    first, normed_first, inverse_first = norm_forward(
        tokens.astype(jnp.float32) + matmul(mixed_self, target_output) + vectors[:, 2],
        vectors[:, offset + 2],
        vectors[:, offset + 3],
    )
    first_low = first.astype(jnp.bfloat16)
    queries_cross = (matmul(first_low, source_query) + vectors[:, 3]).astype(jnp.bfloat16)
    keys_cross = matmul(memory, source_key).astype(jnp.bfloat16)
    values_cross = (matmul(memory, source_value) + vectors[:, 4]).astype(jnp.bfloat16)
    mixed_cross, logsum_cross = attend_forward(
        queries_cross, keys_cross, values_cross, target_segment, source_segment
    )
    second, normed_second, inverse_second = norm_forward(
        first + matmul(mixed_cross, source_output) + vectors[:, 5],
        vectors[:, offset + 4],
        vectors[:, offset + 5],
    )
    second_low = second.astype(jnp.bfloat16)
    hidden = matmul(second_low, up_weight) + up_bias
    active = jax.nn.gelu(hidden).astype(jnp.bfloat16)
    third, normed_third, inverse_third = norm_forward(
        second + matmul(active, down_weight) + vectors[:, offset],
        vectors[:, offset + 6],
        vectors[:, offset + 7],
    )
    third_low = third.astype(jnp.bfloat16)
    right_half = jnp.concatenate([third_low[1:], jnp.zeros((1, D), jnp.bfloat16)]) * follow.astype(
        jnp.bfloat16
    )
    slots = (
        (matmul(third_low, slot_left) + matmul(right_half, slot_right) + vectors[:, offset + 1])
        * valid_rows
    ).astype(jnp.bfloat16)
    seed_grad = cotangent * valid_rows.astype(jnp.bfloat16)
    grad_slot_bias = jnp.sum(seed_grad.astype(jnp.float32), axis=0)
    grad_left = matmul_first(third_low, seed_grad)
    grad_right = matmul_first(right_half, seed_grad)
    right_back = matmul_last(seed_grad, slot_right) * follow
    grad_third = matmul_last(seed_grad, slot_left) + jnp.concatenate(
        [jnp.zeros((1, D), jnp.float32), right_back[:-1]]
    )
    grad_pre_third, grad_gain_third, grad_shift_third = norm_backward(
        grad_third, normed_third, inverse_third, vectors[:, offset + 6]
    )
    pre_third_low = grad_pre_third.astype(jnp.bfloat16)
    grad_down = matmul_first(active, pre_third_low)
    grad_tall_all = jnp.concatenate([grad_down, grad_left, grad_right], axis=0)
    gelu_value, gelu_pull = jax.vjp(jax.nn.gelu, hidden)
    grad_hidden = gelu_pull(matmul_last(pre_third_low, down_weight))[0]
    hidden_low = grad_hidden.astype(jnp.bfloat16)
    grad_up = matmul_first(second_low, hidden_low)
    grad_second = grad_pre_third + matmul_last(hidden_low, up_weight)
    grad_pre_second, grad_gain_second, grad_shift_second = norm_backward(
        grad_second, normed_second, inverse_second, vectors[:, offset + 4]
    )
    pre_second_low = grad_pre_second.astype(jnp.bfloat16)
    grad_source_output = matmul_first(mixed_cross, pre_second_low)
    mixed_cross_grad = matmul_last(pre_second_low, source_output).astype(jnp.bfloat16)
    cross_query_grad, cross_key_grad, cross_value_grad = attend_backward(
        queries_cross,
        keys_cross,
        values_cross,
        mixed_cross_grad,
        logsum_cross,
        target_segment,
        source_segment,
    )
    cross_query_low = cross_query_grad.astype(jnp.bfloat16)
    cross_key_low = cross_key_grad.astype(jnp.bfloat16)
    cross_value_low = cross_value_grad.astype(jnp.bfloat16)
    grad_source_query = matmul_first(first_low, cross_query_low)
    grad_source_key = matmul_first(memory, cross_key_low)
    grad_source_value = matmul_first(memory, cross_value_low)
    grad_memory = matmul_last(cross_key_low, source_key) + matmul_last(
        cross_value_low, source_value
    )
    grad_first = grad_pre_second + matmul_last(cross_query_low, source_query)
    grad_pre_first, grad_gain_first, grad_shift_first = norm_backward(
        grad_first, normed_first, inverse_first, vectors[:, offset + 2]
    )
    pre_first_low = grad_pre_first.astype(jnp.bfloat16)
    grad_target_output = matmul_first(mixed_self, pre_first_low)
    mixed_self_grad = matmul_last(pre_first_low, target_output).astype(jnp.bfloat16)
    self_query_grad, self_key_grad, self_value_grad = attend_backward(
        queries_self,
        keys_self,
        values_self,
        mixed_self_grad,
        logsum_self,
        target_segment,
        target_segment,
    )
    self_query_low = self_query_grad.astype(jnp.bfloat16)
    self_key_low = self_key_grad.astype(jnp.bfloat16)
    self_value_low = self_value_grad.astype(jnp.bfloat16)
    grad_target_query = matmul_first(tokens, self_query_low)
    grad_target_key = matmul_first(tokens, self_key_low)
    grad_target_value = matmul_first(tokens, self_value_low)
    grad_tokens = (
        grad_pre_first
        + matmul_last(self_query_low, target_query)
        + matmul_last(self_key_low, target_key)
        + matmul_last(self_value_low, target_value)
    )
    grad_wide_all = jnp.concatenate(
        [
            grad_target_query,
            grad_target_key,
            grad_target_value,
            grad_target_output,
            grad_source_query,
            grad_source_key,
            grad_source_value,
            grad_source_output,
            grad_up,
        ],
        axis=1,
    )
    bias_front = jnp.stack(
        [
            jnp.sum(self_query_grad, axis=0),
            jnp.sum(self_value_grad, axis=0),
            jnp.sum(grad_pre_first, axis=0),
            jnp.sum(cross_query_grad, axis=0),
            jnp.sum(cross_value_grad, axis=0),
            jnp.sum(grad_pre_second, axis=0),
        ],
        axis=1,
    )
    bias_middle = jnp.sum(grad_hidden, axis=0).reshape(spread, D).T
    bias_back = jnp.stack(
        [
            jnp.sum(grad_pre_third, axis=0),
            grad_slot_bias,
            grad_gain_first,
            grad_shift_first,
            grad_gain_second,
            grad_shift_second,
            grad_gain_third,
            grad_shift_third,
        ],
        axis=1,
    )
    grad_vector_all = jnp.concatenate([bias_front, bias_middle, bias_back], axis=1)
    grad_wide, grad_tall, grad_vecs = (
        lax.psum_scatter(grad_wide_all, ("wide", "narrow"), scatter_dimension=0, tiled=True),
        lax.psum_scatter(grad_tall_all, ("wide", "narrow"), scatter_dimension=0, tiled=True),
        lax.psum_scatter(grad_vector_all, ("wide", "narrow"), scatter_dimension=0, tiled=True),
    )
    new_avg_wide = avg_wide + (w_wide.astype(jnp.float32) - avg_wide) / AVG_STEPS
    new_avg_tall = avg_tall + (w_tall.astype(jnp.float32) - avg_tall) / AVG_STEPS
    new_avg_vecs = avg_vecs + (vecs.astype(jnp.float32) - avg_vecs) / AVG_STEPS
    return (
        slots,
        grad_tokens,
        grad_memory,
        grad_wide,
        grad_tall,
        grad_vecs,
        new_avg_wide,
        new_avg_tall,
        new_avg_vecs,
    )


BF16 = jnp.bfloat16
F32 = jnp.float32
AUG = 80
BIG = 1e30
TILE = 256
MESH_IDS = pl.DeviceIdType.MESH
BIAS_OUT, GAIN = 10, 12
TALL_CUT = 3
OUT_SEMAPHORES = 24
PAIR = 6 * HEAD_DIM
PAIR_GROUPS = ((0,), (1,), (2, 3))
GATHER_STEPS = {
    0: ((0, 0),),
    1: ((1, 0), (0, 2), (1, 1), (2, 0), (0, 3),),
    2: ((9, 0),),
    4: ((3, 0),),
    5: ((1, 2), (2, 1), (1, 3),),
    7: ((4, 0),),
    9: ((3, 1), (5, 0), (2, 2), (2, 3),),
    11: ((4, 1),),
    12: ((6, 0), (9, 1), (3, 2),),
    13: ((5, 1), (7, 0),),
    14: ((3, 3),),
    16: ((4, 2),),
    19: ((6, 1),),
    20: ((4, 3),),
    21: ((8, 0),),
    23: ((5, 2),),
    25: ((7, 1),),
    26: ((5, 3),),
    28: ((6, 2),),
    30: ((8, 1), (6, 3),),
    32: ((9, 2),),
    33: ((7, 2),),
    35: ((9, 3), (8, 2), (7, 3), (8, 3),),
}
SUM_STEPS = {
    5: ((0, 0),),
    10: ((1, 0),),
    12: ((0, 1),),
    20: ((1, 1),),
    24: ((2, 0), (0, 2),),
    25: ((3, 0), (1, 2),),
    27: ((4, 0), (2, 1),),
    29: ((3, 1), (5, 0),),
    30: ((4, 1), (0, 3),),
    37: ((2, 2), (6, 0),),
    38: ((7, 0), (3, 2),),
    39: ((5, 1),),
    40: ((1, 3), (4, 2),),
    44: ((6, 1), (7, 1), (5, 2), (6, 2), (7, 2), (2, 3), (3, 3), (4, 3), (5, 3), (6, 3), (7, 3),),
}


def dot(left, right, left_dim, right_dim):
    return lax.dot_general(
        left, right, (((left_dim,), (right_dim,)), ((), ())), preferred_element_type=F32
    )


def bands(query_rows, key_rows, longest, tile=TILE):
    found = []
    for start in range(0, query_rows, tile):
        if longest is None:
            found.append((0, key_rows))
            continue
        low = max(0, (start - longest + 1) // TILE * TILE)
        high = min(key_rows, -(-(start + TILE + longest - 1) // TILE) * TILE)
        found.append((low, high))
    return found


def column_max(scores):
    rows, columns = scores.shape
    return jnp.max(
        jnp.max(scores.reshape(rows // 64, 64, columns), axis=0), axis=0, keepdims=True
    )


def split_three(value):
    high = value.astype(BF16).astype(F32)
    middle = (value - high).astype(BF16).astype(F32)
    low = (value - high - middle).astype(BF16).astype(F32)
    return high, middle, low


def feature_rows(base, first, parts):
    place = lax.broadcasted_iota(jnp.int32, base.shape, 0)
    for step, part in enumerate(parts):
        base = jnp.where(place == first + step, part, base)
    return base


def gelu_pair(u):
    scale = 0.7978845608028654
    inner = jnp.tanh(scale * (u + 0.044715 * (u * u * u)))
    half = 0.5 * (1.0 + inner)
    slope = half + 0.5 * u * (1.0 - inner * inner) * (scale * (1.0 + 3 * 0.044715 * (u * u)))
    return u * half, slope


def normalize(before, gain, shift):
    centred = before - jnp.mean(before, axis=-1, keepdims=True)
    inverse = lax.rsqrt(jnp.mean(centred * centred, axis=-1, keepdims=True) + EPSILON)
    normed = centred * inverse
    return normed * gain + shift, normed, inverse


def attention_forward(queries, keys, values, mixed, scores, ranges, heads, hooks):
    tiles = len(ranges)
    width = queries.shape[2] // tiles

    def put(head, tile):
        low, high = ranges[tile]
        scores[tile % 2][0 : high - low, :] = dot(
            keys[head, :, low:high], queries[head, :, tile * width : (tile + 1) * width], 0, 0
        )

    put(heads[0], 0)

    def one_head(head, carried):
        for tile, (low, high) in enumerate(ranges):
            if tile + 1 < tiles:
                put(head, tile + 1)
            else:
                put(jnp.minimum(head + 1, heads[1] - 1), 0)
            span = slice(tile * width, (tile + 1) * width)
            current = scores[tile % 2][0 : high - low, :]
            highest = column_max(current)
            shares = jnp.exp(current - highest).astype(BF16)
            gathered = dot(values[head, :, low:high], shares, 1, 0)
            total = gathered[HEAD_DIM : HEAD_DIM + 1]
            rows = pl.ds(pl.multiple_of(head * HEAD_DIM, HEAD_DIM), HEAD_DIM)
            mixed[rows, span] = (gathered[:HEAD_DIM] * (1.0 / total)).astype(BF16)
            queries[head, HEAD_DIM:, span] = feature_rows(
                queries[head, HEAD_DIM:, span].astype(F32),
                SEGS,
                split_three(-(highest + jnp.log(total))),
            ).astype(BF16)
        for at, hook in hooks.items():
            pl.when(head == at)(hook)
        return carried

    lax.fori_loop(heads[0], heads[1], one_head, 0)


def attention_backward(queries, keys, values, grads, outs, sums, shares, score_grads, ranges, hooks):
    key_rows = keys.shape[2]
    key_sum, value_sum = sums
    tiles = len(ranges)

    def put(head, tile):
        low, high = ranges[tile]
        span = slice(tile * TILE, (tile + 1) * TILE)
        share = jnp.exp(dot(queries[head, :, span], keys[head, :, low:high], 0, 0))
        share_grad = dot(grads[head, :, span], values[head, :, low:high], 0, 0)
        shares[tile % 2][:, 0 : high - low] = share.astype(BF16)
        score_grads[tile % 2][:, 0 : high - low] = (share * share_grad).astype(BF16)

    put(0, 0)

    def one_head(head, carried):
        key_sum[:, 0:key_rows] = jnp.zeros((HEAD_DIM, key_rows), F32)
        value_sum[:, 0:key_rows] = jnp.zeros((HEAD_DIM, key_rows), F32)
        query_out, key_out, value_out = [out(head) for out in outs]
        for tile, (low, high) in enumerate(ranges):
            if tile + 1 < tiles:
                put(head, tile + 1)
            else:
                put(jnp.minimum(head + 1, HEADS - 1), 0)
            span = slice(tile * TILE, (tile + 1) * TILE)
            share = shares[tile % 2][:, 0 : high - low]
            score_grad = score_grads[tile % 2][:, 0 : high - low]
            query_out[:, span] = (
                dot(keys[head, 0:HEAD_DIM, low:high], score_grad, 1, 1) * SCORE_SCALE
            ).astype(BF16)
            key_sum[:, low:high] += dot(queries[head, 0:HEAD_DIM, span], score_grad, 1, 0)
            value_sum[:, low:high] += dot(grads[head, 0:HEAD_DIM, span], share, 1, 0)
        key_out[...] = key_sum[:, 0:key_rows].astype(BF16)
        value_out[...] = value_sum[:, 0:key_rows].astype(BF16)
        for at, hook in hooks.items():
            pl.when(head == at)(hook)
        return carried

    lax.fori_loop(0, HEADS, one_head, 0)


class Exchange:
    def __init__(self, wide, narrow):
        self.narrow_bits = narrow.bit_length() - 1
        self.count = (wide * narrow).bit_length() - 1
        self.line = 1 << (self.count - 3)
        self.place = (lax.axis_index("wide"), lax.axis_index("narrow"))
        number = self.place[0] * narrow + self.place[1]
        self.bits = [(number >> bit) & 1 for bit in range(self.count)]
        self.own = tuple(self.bits[bit] for bit in reversed(range(self.count)))
        self.far = list(range(3, self.count))
        self.masks = [1, 2, 4, 6] + [other << 3 for other in range(1, self.line)]
        core = self.bits[0]
        self.first, self.second, self.both = {1: 1 - core, 2: core}, {1: core, 2: 1 - core}, {1: 1, 2: 1}

    def device(self, mask):
        wide, narrow = self.place
        return (wide ^ (mask >> self.narrow_bits), narrow ^ (mask & ((1 << self.narrow_bits) - 1)))

    def greet(self):
        barrier = pltpu.get_barrier_semaphore()
        for mask in self.masks:
            pl.semaphore_signal(
                barrier, inc=1, device_id=self.device(mask), device_id_type=MESH_IDS
            )

    def meet(self):
        pl.semaphore_wait(pltpu.get_barrier_semaphore(), len(self.masks))

    def neighbour(self, second):
        core = self.bits[0]
        take = core if not second else 1 - core
        one, other = self.device(2), self.device(4)
        return tuple(a + (b - a) * take for a, b in zip(one, other))

    def view(self, part, open_bits, flips=None):
        index = tuple(
            slice(None) if bit in open_bits else self.turned(bit, flips)
            for bit in reversed(range(self.count))
        )
        return part.ref.at[index + part.where]

    def turned(self, bit, flips):
        flip = (flips or {}).get(bit, 0)
        return self.bits[bit] + flip - 2 * self.bits[bit] * flip


class Part:
    def __init__(self, ref, rows=None, columns=None, buffers=(), outs=()):
        cut = lambda ends: slice(None) if ends is None else pl.ds(ends[0], ends[1] - ends[0])
        self.ref, self.where, self.buffers, self.outs = ref, (cut(rows), cut(columns)), buffers, outs


class Transfer:
    def __init__(self, net, pieces, send, receive):
        self.net, self.pieces, self.send, self.receive = net, pieces, send, receive
        self.line = tuple(range(4, 3 + net.line))

    def copy(self, piece, part, slot, source, target, device):
        return pltpu.make_async_remote_copy(
            source,
            target,
            self.send.at[piece, slot, part],
            self.receive.at[piece, slot, part],
            device_id=device,
            device_id_type=MESH_IDS,
        )

    def each(self, piece, stage, act):
        for number in range(len(self.pieces[piece])):
            for slot in self.slots(piece, stage):
                act(self.one(piece, number, slot))

    def begin(self, piece, slot):
        for number in range(len(self.pieces[piece])):
            self.one(piece, number, slot).start()

    def finish(self, pieces=None):
        for piece in range(len(self.pieces)) if pieces is None else pieces:
            for stage in range(4):
                self.each(piece, stage, lambda copy: copy.wait_send())


class Gather(Transfer):
    def __init__(self, net, pieces, send, receive):
        super().__init__(net, pieces, send, receive)
        self.last = len(pieces) - 1

    def slots(self, piece, stage):
        if piece == 0:
            return (self.line, (), (0, 1, 2), (3,))[stage]
        if piece == self.last:
            return ((0, 1), (2,), self.line, (3,))[stage]
        return (self.line, (0,), (1, 2), (3,))[stage]

    def one(self, piece, number, slot):
        net, part = self.net, self.pieces[piece][number]
        lines = [] if piece == self.last else net.far
        if slot == 3:
            view, device = net.view(part, net.far + [1, 2]), net.device(1)
        elif slot > 3:
            near = [1, 2] if piece == self.last else []
            view, device = net.view(part, near), net.device((slot - 3) << 3)
        elif slot == 2 and piece == 0:
            view, device = net.view(part, lines), net.device(6)
        else:
            view = net.view(part, lines, net.first if slot == 2 else None)
            device = net.neighbour(slot > 0)
        return self.copy(piece, number, slot, view, view, device)

    def start(self, piece):
        if piece == self.last:
            self.begin(piece, 0)
            self.begin(piece, 1)
        else:
            self.each(piece, 0, lambda copy: copy.start())

    def step(self, piece, stage):
        self.each(piece, stage, lambda copy: copy.wait_recv())
        if piece == self.last and stage < 2:
            self.each(piece, stage + 1, lambda copy: copy.start())
        elif stage == 0:
            self.begin(piece, 0)
            self.begin(piece, 1)
            if piece == 0:
                self.begin(0, 2)
                self.start(1)
            if piece + 2 < self.last:
                self.start(piece + 2)
        elif stage == 1 and piece:
            self.begin(piece, 2)
        elif stage == 2:
            self.begin(piece, 3)


class Sum(Transfer):
    def slots(self, piece, stage):
        return ((0,), (1,), (2, 3), self.line)[stage]

    def one(self, piece, number, slot):
        net, part = self.net, self.pieces[piece][number]
        if slot == 0:
            view, device = net.view(part, net.far + [1, 2], {0: 1}), net.device(1)
        elif slot > 3:
            mask = (slot - 3) << 3
            view, device = net.view(part, [], {bit: mask >> bit & 1 for bit in net.far}), net.device(mask)
        else:
            view = net.view(part, net.far, (None, net.both, net.second, net.first)[slot])
            device = net.neighbour(slot < 3)
        target = part.buffers[4].at[slot - 4] if slot > 3 else part.buffers[slot]
        return self.copy(piece, number, slot, view, target, device)

    def start(self, piece):
        self.begin(piece, 0)

    def add(self, piece, stage):
        net = self.net
        if stage == 3:
            for part in self.pieces[piece]:
                value = part.ref[net.own + part.where].astype(F32)
                for other in range(1, net.line):
                    value = value + part.buffers[4][other - 1].astype(F32)
                for low, high, staged, out, semaphore in part.outs:
                    staged[...] = value[:, low:high]
                    pltpu.make_async_copy(staged, out, semaphore).start()
            return
        rest = net.far + ([1, 2] if stage == 0 else [])
        rest.sort()

        def one_shard(step, carried):
            place = {bit: (step >> at) & 1 for at, bit in enumerate(rest)}
            index = tuple(
                place[bit] if bit in place else net.turned(bit, net.first if stage == 1 else None)
                for bit in reversed(range(net.count))
            )
            arrived = tuple(place[bit] for bit in reversed(rest)) + (slice(None), slice(None))
            for part in self.pieces[piece]:
                where = index + part.where
                if stage == 2:
                    value = (
                        part.ref[where].astype(F32)
                        + part.buffers[2][arrived].astype(F32)
                        + part.buffers[3][arrived].astype(F32)
                    )
                else:
                    value = part.ref[where] + part.buffers[stage][arrived]
                part.ref[where] = value.astype(part.ref.dtype)
            return carried

        lax.fori_loop(0, 1 << len(rest), one_shard, 0, unroll=True)

    def step(self, piece, stage):
        self.each(piece, stage, lambda copy: copy.wait_recv())
        self.add(piece, stage)
        if stage == 0:
            self.begin(piece, 1)
            self.begin(piece, 2)
        elif stage == 1:
            self.begin(piece, 3)
        elif stage == 2:
            self.each(piece, 3, lambda copy: copy.start())

    def finish(self):
        super().finish()
        for piece in self.pieces:
            for part in piece:
                for _, _, staged, out, semaphore in part.outs:
                    pltpu.make_async_copy(staged, out, semaphore).wait()


class Plan:
    def __init__(self, transfer, table):
        self.transfer, self.table, self.stop = transfer, table, 0

    def next(self):
        taken = self.table.get(self.stop, ())
        self.stop += 1

        def act():
            for piece, stage in taken:
                self.transfer.step(piece, stage)

        return act if taken else None

    def now(self):
        act = self.next()
        if act:
            act()

    def loop(self, places):
        found = {place: self.next() for place in places}
        return {place: act for place, act in found.items() if act}


def layer_kernel(r, wide_size, narrow_size):
    net = Exchange(wide_size, narrow_size)
    net.greet()
    devices = wide_size * narrow_size
    wide7, tall7, vec7, gvec7 = r.wide, r.tall, r.vec, r.grad_vec
    wide = wide7.reshape(devices * wide7.shape[-2], wide7.shape[-1])
    tall = tall7.reshape(devices * tall7.shape[-2], tall7.shape[-1])
    slope7 = r.slope
    slope = slope7.reshape(devices * slope7.shape[-2], slope7.shape[-1])
    own_rows = (0, wide7.shape[-2])
    tokens, memory, seed, seed_next = r.tokens, r.memory, r.seed, r.seed_next
    rows, sources = tokens.shape[0], memory.shape[0]
    tiles = rows // TILE
    local = r.local

    wide_moves = [
        (block * D + pair * PAIR // 3, pair * PAIR + block * PAIR // 3, PAIR // 3)
        for pair in range(HEADS // 2)
        for block in range(3)
    ] + [(3 * D, 3 * D, wide7.shape[-1] - 3 * D)]
    loads = [
        pltpu.make_async_copy(
            r.w_wide.at[:, pl.ds(low, width)],
            wide7.at[net.own + (slice(None), pl.ds(high, width))],
            r.own_done.at[number],
        )
        for number, (low, high, width) in enumerate(wide_moves)
    ] + [
        pltpu.make_async_copy(r.w_tall, tall7.at[net.own], local.at[1]),
        pltpu.make_async_copy(r.vecs, vec7.at[net.own], local.at[2]),
        pltpu.make_async_copy(r.tokens_in, tokens, local.at[3]),
        pltpu.make_async_copy(r.memory_in, memory, local.at[4]),
        pltpu.make_async_copy(r.cotangent, seed, local.at[5]),
    ]
    for copy in loads:
        copy.start()

    tall_rows = tall7.shape[-2]
    tall_cuts = [(low, low + tall_rows // TALL_CUT) for low in range(0, tall_rows, tall_rows // TALL_CUT)]

    def wide_part(low, high):
        return [Part(wide7, None, (low, high))]

    gather = Gather(
        net,
        [
            wide_part(0, PAIR) + [Part(vec7)],
            wide_part(PAIR, 2 * PAIR),
            wide_part(2 * PAIR, 4 * PAIR),
            wide_part(3 * D, 5 * D),
            wide_part(5 * D, 7 * D),
            wide_part(7 * D, 9 * D),
            wide_part(9 * D, 12 * D),
        ]
        + [[Part(tall7, cut)] for cut in tall_cuts],
        r.gather_send,
        r.gather_receive,
    )
    plan = Plan(gather, GATHER_STEPS)
    out_semaphores = iter(range(OUT_SEMAPHORES))

    def out_of(low, high, staged, out):
        return (low, high, staged, out, r.out_done.at[next(out_semaphores)])

    def wide_out(low, high, start):
        columns = pl.ds(start, high - low)
        return out_of(low, high, r.out_wide.at[:, columns], r.grad_wide.at[:, columns])

    def wide_sum(low, high, buffers):
        return [Part(wide7, None, (low, high), buffers, [wide_out(0, high - low, low)])]

    def self_sum(pair):
        third = PAIR // 3
        outs = [
            wide_out(block * third, (block + 1) * third, block * D + pair * third)
            for block in range(3)
        ]
        columns = (pair * PAIR, (pair + 1) * PAIR)
        return [Part(slope7, own_rows, columns, r.in_self[pair], outs)]

    vec_out = out_of(0, 128, r.out_vec, r.grad_vecs)
    total = Sum(
        net,
        [
            [Part(tall7, None, None, r.in_tall, [out_of(0, D, r.out_tall, r.grad_tall)])],
            wide_sum(8 * D, 12 * D, r.in_up),
            wide_sum(3 * D, 8 * D, r.in_mid),
        ]
        + [self_sum(pair) for pair in range(HEADS // 2)]
        + [[Part(gvec7, None, None, r.in_vec, [vec_out])]],
        r.sum_send,
        r.sum_receive,
    )
    TALL, UP, MID, SELF = range(4)
    VECTORS = SELF + HEADS // 2
    sum_plan = Plan(total, SUM_STEPS)

    for copy in loads[:-3]:
        copy.wait()
    net.meet()
    gather.start(0)
    gather.start(gather.last)

    def endings(lengths):
        found, running = [], 0
        for index in range(SEGS):
            running = running + lengths[0, index]
            found.append(running)
        return found

    target_ends = endings(r.tgt_lengths)
    source_ends = endings(r.src_lengths)

    def chosen(ends, count):
        place = lax.broadcasted_iota(jnp.int32, (16, count), 1)
        segment = jnp.zeros((16, count), jnp.int32)
        for end in ends:
            segment = segment + (place >= end).astype(jnp.int32)
        return segment == lax.broadcasted_iota(jnp.int32, (16, count), 0)

    def query_features(ends, count):
        return jnp.where(chosen(ends, count), 1.0, 0.0).astype(BF16)

    def key_features(ends, count):
        row = lax.broadcasted_iota(jnp.int32, (16, count), 0)
        masked = jnp.where(chosen(ends, count), 0.0, -BIG)
        return jnp.where(row < SEGS, masked, jnp.where(row < SEGS + 3, 1.0, 0.0)).astype(BF16)

    def value_features(count):
        row = lax.broadcasted_iota(jnp.int32, (16, count), 0)
        return jnp.where(row < 3, 1.0, 0.0).astype(BF16)

    def every_head(ref, features):
        ref[:, HEAD_DIM:, :] = jnp.broadcast_to(features[None], (HEADS,) + features.shape)

    q, k, v, q2, k2, v2 = r.q, r.k, r.v, r.q2, r.k2, r.v2
    every_head(q, query_features(target_ends, rows))
    every_head(q2, query_features(target_ends, rows))
    every_head(k, key_features(target_ends, rows))
    every_head(k2, key_features(source_ends, sources))
    every_head(v, value_features(rows))
    every_head(v2, value_features(sources))
    plan.now()

    def position(tile):
        return tile * TILE + lax.broadcasted_iota(jnp.int32, (TILE, 1), 0)

    def valid(tile):
        return jnp.where(position(tile) < target_ends[SEGS - 2], 1.0, 0.0)

    def follow(tile):
        after = position(tile) + 1
        ended = after == target_ends[0]
        for end in target_ends[1:]:
            ended = ended | (after == end)
        return jnp.where(ended, 0.0, 1.0)

    def span(tile):
        return pl.ds(tile * TILE, TILE)

    shift, res = r.shift, r.res
    loads[-1].wait()
    shift[0:8, :] = jnp.zeros((8, D), F32)
    for tile in range(tiles):
        masked = seed[span(tile), :].astype(F32) * valid(tile)
        seed[span(tile), :] = masked.astype(BF16)
        shift[pl.ds(tile * TILE + 8, TILE), :] = masked * follow(tile)
    for tile in range(tiles):
        seed_next[span(tile), :] = shift[pl.ds(tile * TILE + 7, TILE), :].astype(BF16)
    r.grad_rows[...] = jnp.zeros_like(r.grad_rows)
    r.grad_columns[...] = jnp.zeros_like(r.grad_columns)
    loads[-3].wait()
    loads[-2].wait()

    def row(index):
        return r.row_vectors[index : index + 1, :]

    def column(index):
        return vec7[...].reshape(D, vec7.shape[-1])[:, index : index + 1].astype(F32)

    def heads_of(value):
        return value.reshape(value.shape[0] // HEAD_DIM, HEAD_DIM, value.shape[1])

    def scaled(value):
        return (value.astype(BF16).astype(F32) * SCORE_SCALE).astype(BF16)

    def wide_column(index):
        return wide[:, index * D : (index + 1) * D]

    self_ranges = bands(rows, rows, 512)
    cross_ranges = bands(rows, sources, None)
    cross_wide = bands(rows, sources, None, 2 * TILE)
    cross_scores = [shift.at[pl.ds(start, sources), :] for start in (0, sources)]
    a, a2 = r.mixed, r.mixed2
    bias_rows = PAIR // 3
    identity = lax.broadcasted_iota(jnp.int32, (D, D), 0) == lax.broadcasted_iota(
        jnp.int32, (D, D), 1
    )
    identity = jnp.where(identity, 1.0, 0.0).astype(BF16)
    for index, pairs in enumerate(PAIR_GROUPS):
        plan.now()
        if index == 0:
            r.row_vectors[0 : vec7.shape[-1], :] = dot(
                vec7[...].reshape(D, vec7.shape[-1]), identity, 0, 0
            )
        biases = []
        for pair in pairs:
            place = slice(pair * bias_rows, (pair + 1) * bias_rows)
            biases += [column(0)[place], jnp.zeros((bias_rows, 1), F32), column(1)[place]]
        bias = jnp.concatenate(biases, axis=0)
        for tile in range(tiles):
            both = dot(
                wide[:, pairs[0] * PAIR : (pairs[-1] + 1) * PAIR], tokens[span(tile), :], 0, 1
            )
            both = (both + bias).astype(BF16)
            for place, pair in enumerate(pairs):
                for block, ref in enumerate((q, k, v)):
                    start = place * PAIR + block * bias_rows
                    value = both[start : start + bias_rows]
                    if block == 0:
                        value = (value.astype(F32) * SCORE_SCALE).astype(BF16)
                    ref[2 * pair : 2 * pair + 2, 0:HEAD_DIM, span(tile)] = heads_of(value)
        plan.now()
        heads = (2 * pairs[0], 2 * pairs[-1] + 2)
        attention_forward(
            q,
            k,
            v,
            a,
            r.scores,
            self_ranges,
            heads,
            plan.loop(range(*heads)),
        )

    normed, low, inverse = r.normed, r.low, r.inverse

    def norm_tile(index, tile, before):
        out, unit, rho = normalize(before, row(GAIN + 2 * index), row(GAIN + 2 * index + 1))
        normed[index][span(tile), :] = unit.astype(BF16)
        inverse[span(tile), index : index + 1] = rho
        low[index][span(tile), :] = out.astype(BF16)
        return out

    plan.now()
    for tile in range(tiles):
        before = (
            tokens[span(tile), :].astype(F32) + dot(a[:, span(tile)], wide_column(3), 0, 0) + row(2)
        )
        out = norm_tile(0, tile, before)
        res[span(tile), :] = out
        q2[:, 0:HEAD_DIM, span(tile)] = heads_of(
            scaled(dot(wide_column(4), out.astype(BF16), 0, 1) + column(3))
        )
        plan.now()
    plan.now()
    for tile in range(sources // TILE):
        part = memory[span(tile), :]
        k2[:, 0:HEAD_DIM, span(tile)] = heads_of(dot(wide_column(5), part, 0, 1).astype(BF16))
        v2[:, 0:HEAD_DIM, span(tile)] = heads_of(
            (dot(wide_column(6), part, 0, 1) + column(4)).astype(BF16)
        )
    attention_forward(
        q2,
        k2,
        v2,
        a2,
        cross_scores,
        cross_wide,
        (0, HEADS),
        plan.loop(range(HEADS)),
    )
    active = r.active
    plan.now()
    for tile in range(tiles):
        before = res[span(tile), :] + dot(a2[:, span(tile)], wide_column(7), 0, 0) + row(5)
        out = norm_tile(1, tile, before)
        res[span(tile), :] = out
        for block in range(FF // D):
            if tile == 0 and block == 1:
                plan.now()
            columns = slice(block * D, (block + 1) * D)
            u = dot(out.astype(BF16), wide_column(8 + block), 1, 0) + row(6 + block)
            value, derivative = gelu_pair(u)
            active[span(tile), columns] = value.astype(BF16)
            slope[span(tile), columns] = derivative.astype(BF16)
        plan.now()
    early = range(gather.last - 2)
    gather.finish(early)
    plan.now()
    slot_left = tall.at[pl.ds(FF, D), :]
    slot_right = tall.at[pl.ds(FF + D, D), :]
    for tile in range(tiles):
        before = (
            res[span(tile), :] + dot(active[span(tile), :], tall[0:FF, :], 1, 0) + row(BIAS_OUT)
        )
        norm_tile(2, tile, before)
    low_grad = r.low_grad
    gather.finish(range(len(early), gather.last + 1))

    grad_rows, grad_columns = r.grad_rows, r.grad_columns

    def add_row(index, value):
        grad_rows[index : index + 1, :] += jnp.sum(value, axis=0, keepdims=True)

    def norm_back(index, tile, gradient, bias_row):
        gain = row(GAIN + 2 * index)
        unit = normed[index][span(tile), :].astype(F32)
        scaled_grad = gradient * gain
        inner = jnp.mean(scaled_grad * unit, axis=-1, keepdims=True)
        before = inverse[span(tile), index : index + 1] * (
            scaled_grad - jnp.mean(scaled_grad, axis=-1, keepdims=True) - unit * inner
        )
        add_row(GAIN + 2 * index, gradient * unit)
        add_row(GAIN + 2 * index + 1, gradient)
        add_row(bias_row, before)
        res[span(tile), :] = before
        low_grad[span(tile), :] = before.astype(BF16)

    for tile in range(tiles):
        part = seed[span(tile), :]
        add_row(BIAS_OUT + 1, part.astype(F32))
        gradient = dot(part, slot_left[...], 1, 1) + dot(
            seed_next[span(tile), :], slot_right[...], 1, 1
        )
        norm_back(2, tile, gradient, BIAS_OUT)
    grad_left = dot(low[2][...], seed[...], 0, 0).astype(BF16)
    seed[0:D, :] = slot_left[...]
    slot_left[...] = grad_left
    grad_right = dot(low[2][...], seed_next[...], 0, 0).astype(BF16)
    seed[D : 2 * D, :] = slot_right[...]
    slot_right[...] = grad_right
    for block in range(FF // D):
        columns = slice(block * D, (block + 1) * D)
        for tile in range(tiles):
            grad = dot(low_grad[span(tile), :], tall[columns, :], 1, 1) * slope[
                span(tile), columns
            ].astype(F32)
            add_row(6 + block, grad)
            slope[span(tile), columns] = grad.astype(BF16)
        tall[columns, :] = dot(active[:, columns], low_grad[...], 0, 0).astype(BF16)
    total.start(TALL)
    for tile in range(tiles):
        gradient = res[span(tile), :] + dot(
            slope[span(tile), :], wide[:, 8 * D : 8 * D + FF], 1, 1
        )
        norm_back(1, tile, gradient, 5)
        sum_plan.now()
    for block in range(FF // D):
        columns = slice(block * D, (block + 1) * D)
        wide[:, 8 * D + block * D : 8 * D + (block + 1) * D] = dot(
            low[1][...], slope[:, columns], 0, 0
        ).astype(BF16)
        if block == FF // D - 1:
            total.start(UP)
        sum_plan.now()
    grads = r.mixed_grad

    def mixed_back(weight_index, mixed):
        for tile in range(tiles):
            grad = dot(wide_column(weight_index), low_grad[span(tile), :], 1, 1).astype(BF16)
            grads[:, 0:HEAD_DIM, span(tile)] = heads_of(grad)
            inner = jnp.sum(
                heads_of(grad.astype(F32) * mixed[:, span(tile)].astype(F32)),
                axis=1,
                keepdims=True,
            )
            place = lax.broadcasted_iota(jnp.int32, (HEADS, 16, TILE), 1)
            features = jnp.zeros((HEADS, 16, TILE), F32)
            for step, part in enumerate(split_three(-inner)):
                features = jnp.where(place == step, part, features)
            grads[:, HEAD_DIM:, span(tile)] = features.astype(BF16)
        wide[:, weight_index * D : (weight_index + 1) * D] = dot(
            mixed[...], low_grad[...], 1, 0
        ).astype(BF16)

    mixed_back(7, a2)
    sum_plan.now()
    dq2 = active.at[pl.ds(0, D), pl.ds(0, rows)]
    dk2 = active.at[pl.ds(D, D), pl.ds(0, sources)]
    dv2 = active.at[pl.ds(D, D), pl.ds(rows, sources)]

    def head_rows(ref):
        def of(head):
            return ref.at[pl.ds(pl.multiple_of(head * HEAD_DIM, HEAD_DIM), HEAD_DIM), :]

        return of

    sums = (r.key_sum, r.value_sum)
    attention_backward(
        q2,
        k2,
        v2,
        grads,
        [head_rows(ref) for ref in (dq2, dk2, dv2)],
        sums,
        r.shares,
        r.score_grads,
        cross_ranges,
        sum_plan.loop(range(HEADS)),
    )

    def column_sum(index, value):
        grad_columns[:, index : index + 1] += jnp.sum(value.astype(F32), axis=1, keepdims=True)

    for tile in range(tiles):
        gradient = res[span(tile), :] + dot(dq2[:, span(tile)], wide_column(4), 0, 1)
        norm_back(0, tile, gradient, 2)
        sum_plan.now()
    shift[0:sources, :] = dot(dk2[...], wide_column(5), 0, 1) + dot(dv2[...], wide_column(6), 0, 1)
    memory_copy = pltpu.make_async_copy(
        shift.at[pl.ds(0, sources), :], r.grad_memory, local.at[10]
    )
    memory_copy.start()
    wide[:, 5 * D : 6 * D] = dot(memory[...], dk2[...], 0, 1).astype(BF16)
    wide[:, 6 * D : 7 * D] = dot(memory[...], dv2[...], 0, 1).astype(BF16)
    sum_plan.now()
    wide[:, 4 * D : 5 * D] = dot(low[0][...], dq2[...], 0, 1).astype(BF16)
    column_sum(3, dq2[...])
    column_sum(4, dv2[...])
    mixed_back(3, a)
    total.start(MID)
    sum_plan.now()

    def pair_rows(block):
        def of(head):
            pair = head // 2
            row = pair % 2 * PAIR + block * (PAIR // 3) + head % 2 * HEAD_DIM
            start = pl.multiple_of(pair // 2 * rows, rows)
            return active.at[pl.ds(pl.multiple_of(row, HEAD_DIM), HEAD_DIM), pl.ds(start, rows)]

        return of

    def pair_grad(pair):
        return active[pair % 2 * PAIR : (pair % 2 + 1) * PAIR, pair // 2 * rows : (pair // 2 + 1) * rows]

    def start_pair(pair):
        where = (slice(None),) * net.count + (
            slice(0, own_rows[1]),
            slice(pair * PAIR, (pair + 1) * PAIR),
        )
        slope7[where] = (
            dot(tokens[...], pair_grad(pair), 0, 1)
            .astype(BF16)
            .reshape(slope7.shape[: net.count] + (own_rows[1], PAIR))
        )
        total.start(SELF + pair)

    def start_vectors():
        for pair in range(HEADS // 2):
            place = slice(pair * bias_rows, (pair + 1) * bias_rows)
            grad = pair_grad(pair).astype(F32)
            for index, block in ((0, 0), (1, 2)):
                grad_columns[place, index : index + 1] = jnp.sum(
                    grad[block * bias_rows : (block + 1) * bias_rows], axis=1, keepdims=True
                )
        turned = jnp.transpose(r.grad_rows[...]) + grad_columns[...]
        gvec7[...] = turned.reshape(gvec7.shape)
        total.start(VECTORS)

    hooks = {}
    for head in range(HEADS):
        act = sum_plan.next()

        def hook(head=head, act=act):
            if head % 2 and head < HEADS - 1:
                start_pair(head // 2)
            if act:
                act()

        if act or (head % 2 and head < HEADS - 1):
            hooks[head] = hook
    attention_backward(
        q,
        k,
        v,
        grads,
        [pair_rows(block) for block in range(3)],
        sums,
        r.shares,
        r.score_grads,
        self_ranges,
        hooks,
    )
    start_pair(HEADS // 2 - 1)
    start_vectors()
    sum_plan.now()

    memory_copy.wait()
    shift[rows : rows + 8, :] = jnp.zeros((8, D), F32)
    for tile in range(tiles):
        shift[span(tile), :] = dot(low[2][span(tile), :], seed[D : 2 * D, :], 1, 0)
        sum_plan.now()
    token_copies = []
    for tile in range(tiles):
        low_grad[span(tile), :] = (
            (
                dot(low[2][span(tile), :], seed[0:D, :], 1, 0)
                + follow(tile) * shift[pl.ds(tile * TILE + 1, TILE), :]
                + row(BIAS_OUT + 1)
            )
            * valid(tile)
        ).astype(BF16)
        copy = pltpu.make_async_copy(
            low_grad.at[span(tile), :], r.slots.at[span(tile), :], local.at[6 + tile]
        )
        copy.start()
        token_copies.append(copy)
        sum_plan.now()
    for tile in range(tiles):
        value = res[span(tile), :]
        for side in range(2):
            value = value + dot(
                active[0 : 2 * PAIR, pl.ds(side * rows + tile * TILE, TILE)],
                wide[:, 2 * side * PAIR : 2 * (side + 1) * PAIR],
                0,
                1,
            )
        res[span(tile), :] = value
        copy = pltpu.make_async_copy(
            res.at[span(tile), :], r.grad_tokens.at[span(tile), :], local.at[12 + tile]
        )
        copy.start()
        token_copies.append(copy)
        sum_plan.now()
    sum_plan.now()
    total.finish()
    for copy in token_copies:
        copy.wait()


def finish_kernel(*refs):
    given, results, held = refs[:12], refs[12:21], refs[21:33]
    vec_out, semaphores = refs[33], refs[34]
    loads = [
        pltpu.make_async_copy(source, target, semaphores.at[index])
        for index, (source, target) in enumerate(zip(given, held))
    ]
    for copy in loads:
        copy.start()
    stores = []

    def store(index, source):
        copy = pltpu.make_async_copy(source, results[index], semaphores.at[12 + index])
        copy.start()
        stores.append(copy)

    for index in range(12):
        loads[index].wait()
        if index < 5:
            store(index, held[index])
        elif index == 5:
            vec_out[...] = held[5][:, : vec_out.shape[1]]
            store(5, vec_out)
        elif index >= 9:
            average = held[index - 3]
            average[...] += (held[index][...].astype(F32) - average[...]) / AVG_STEPS
            store(index - 3, average)
    for copy in stores:
        copy.wait()


def fused_body(
    wide_size,
    narrow_size,
    tokens,
    memory,
    w_wide,
    w_tall,
    vecs,
    avg_wide,
    avg_tall,
    avg_vecs,
    tgt_lengths,
    src_lengths,
    cotangent,
):
    count = (wide_size * narrow_size).bit_length() - 1
    rows, sources = tokens.shape[0], memory.shape[0]
    wide_rows, wide_columns = w_wide.shape
    tall_rows = w_tall.shape[0]
    vec_rows = vecs.shape[0]
    bits = (2,) * count
    hbm = pl.BlockSpec(memory_space=pl.ANY)
    smem = pl.BlockSpec(memory_space=pltpu.SMEM)
    inputs = dict(
        tgt_lengths=tgt_lengths,
        src_lengths=src_lengths,
        tokens_in=tokens,
        memory_in=memory,
        cotangent=cotangent,
        w_wide=w_wide,
        w_tall=w_tall,
        vecs=vecs,
    )
    outputs = dict(
        slots=jax.ShapeDtypeStruct((rows, D), BF16),
        grad_tokens=jax.ShapeDtypeStruct((rows, D), F32),
        grad_memory=jax.ShapeDtypeStruct((sources, D), F32),
        grad_wide=jax.ShapeDtypeStruct((wide_rows, wide_columns), F32),
        grad_tall=jax.ShapeDtypeStruct((tall_rows, D), F32),
        grad_vecs=jax.ShapeDtypeStruct((vec_rows, 128), F32),
    )

    def arrivals(shape, dtype=BF16):
        line = (1 << (count - 3)) - 1
        far = bits[3:]
        return [
            pltpu.VMEM(lead + shape, dtype) for lead in (bits[1:], far, far, far, (line,))
        ]

    scratch = dict(
        wide=pltpu.VMEM(bits + (wide_rows, wide_columns), BF16),
        tall=pltpu.VMEM(bits + (tall_rows, D), BF16),
        vec=pltpu.VMEM(bits + vecs.shape, BF16),
        grad_vec=pltpu.VMEM(bits + (vec_rows, 128), F32),
        tokens=pltpu.VMEM((rows, D), BF16),
        memory=pltpu.VMEM((sources, D), BF16),
        seed=pltpu.VMEM((rows, D), BF16),
        seed_next=pltpu.VMEM((rows, D), BF16),
        q=pltpu.VMEM((HEADS, AUG, rows), BF16),
        k=pltpu.VMEM((HEADS, AUG, rows), BF16),
        v=pltpu.VMEM((HEADS, AUG, rows), BF16),
        q2=pltpu.VMEM((HEADS, AUG, rows), BF16),
        k2=pltpu.VMEM((HEADS, AUG, sources), BF16),
        v2=pltpu.VMEM((HEADS, AUG, sources), BF16),
        mixed_grad=pltpu.VMEM((HEADS, AUG, rows), BF16),
        mixed=pltpu.VMEM((D, rows), BF16),
        mixed2=pltpu.VMEM((D, rows), BF16),
        active=pltpu.VMEM((rows, FF), BF16),
        slope=pltpu.VMEM(bits + (rows >> count, FF), BF16),
        res=pltpu.VMEM((rows, D), F32),
        low_grad=pltpu.VMEM((rows, D), BF16),
        shift=pltpu.VMEM((rows + 8, D), F32),
        key_sum=pltpu.VMEM((HEAD_DIM, rows), F32),
        value_sum=pltpu.VMEM((HEAD_DIM, rows), F32),
        inverse=pltpu.VMEM((rows, 128), F32),
        row_vectors=pltpu.VMEM((24, D), F32),
        grad_rows=pltpu.VMEM((128, D), F32),
        grad_columns=pltpu.VMEM((D, 128), F32),
        out_wide=pltpu.VMEM((wide_rows, wide_columns), F32),
        out_tall=pltpu.VMEM((tall_rows, D), F32),
        out_vec=pltpu.VMEM((vec_rows, 128), F32),
        normed=[pltpu.VMEM((rows, D), BF16) for _ in range(3)],
        low=[pltpu.VMEM((rows, D), BF16) for _ in range(3)],
        scores=[
            pltpu.VMEM((max(high - low for low, high in bands(rows, rows, 512)), TILE), F32)
            for _ in range(2)
        ],
        shares=[pltpu.VMEM((TILE, rows), BF16) for _ in range(2)],
        score_grads=[pltpu.VMEM((TILE, rows), BF16) for _ in range(2)],
        in_tall=arrivals((tall_rows, D)),
        in_up=arrivals((wide_rows, FF)),
        in_mid=arrivals((wide_rows, 5 * D)),
        in_self=[arrivals((wide_rows, PAIR)) for _ in range(HEADS // 2)],
        in_vec=arrivals((vec_rows, 128), F32),
        local=pltpu.SemaphoreType.DMA((20,)),
        own_done=pltpu.SemaphoreType.DMA((3 * HEADS // 2 + 1,)),
        out_done=pltpu.SemaphoreType.DMA((OUT_SEMAPHORES,)),
        gather_send=pltpu.SemaphoreType.DMA((7 + TALL_CUT, 3 + (1 << (count - 3)), 2)),
        gather_receive=pltpu.SemaphoreType.DMA((7 + TALL_CUT, 3 + (1 << (count - 3)), 2)),
        sum_send=pltpu.SemaphoreType.DMA((4 + HEADS // 2, 3 + (1 << (count - 3)), 1)),
        sum_receive=pltpu.SemaphoreType.DMA((4 + HEADS // 2, 3 + (1 << (count - 3)), 1)),
    )
    scratch_leaves, scratch_tree = jax.tree.flatten(scratch)
    input_leaves, output_leaves = list(inputs.values()), list(outputs.values())
    names = list(inputs) + list(outputs)
    spec = [smem if value.dtype == jnp.int32 else hbm for value in input_leaves]

    def kernel(*refs):
        held = dict(zip(names, refs))
        held.update(jax.tree.unflatten(scratch_tree, refs[len(names) :]))
        layer_kernel(types.SimpleNamespace(**held), wide_size, narrow_size)

    slots, grad_tokens, grad_memory, grad_wide, grad_tall, grad_vecs = pl.pallas_call(
        kernel,
        out_shape=output_leaves,
        in_specs=spec,
        out_specs=[hbm] * len(outputs),
        scratch_shapes=scratch_leaves,
        compiler_params=pltpu.CompilerParams(
            collective_id=0, has_side_effects=True, vmem_limit_bytes=67_000_000
        ),
    )(*input_leaves)
    done = [slots, grad_tokens, grad_memory, grad_wide, grad_tall, grad_vecs]
    done += [avg_wide, avg_tall, avg_vecs, w_wide, w_tall, vecs]
    shapes = outputs | dict(grad_vecs=jax.ShapeDtypeStruct(vecs.shape, F32))
    return pl.pallas_call(
        finish_kernel,
        out_shape=list(shapes.values())
        + [jax.ShapeDtypeStruct(value.shape, F32) for value in (avg_wide, avg_tall, avg_vecs)],
        in_specs=[hbm] * len(done),
        out_specs=[hbm] * 9,
        scratch_shapes=[pltpu.VMEM(value.shape, value.dtype) for value in done]
        + [pltpu.VMEM(vecs.shape, F32), pltpu.SemaphoreType.DMA((21,))],
    )(*done)


def solution(mesh):
    in_specs = (
        P(("wide", "narrow"), None),
        P(("wide", "narrow"), None),
        P(("wide", "narrow"), None),
        P(("wide", "narrow"), None),
        P(("wide", "narrow"), None),
        P(("wide", "narrow"), None),
        P(("wide", "narrow"), None),
        P(("wide", "narrow"), None),
        P(("wide", "narrow"), None),
        P(("wide", "narrow"), None),
        P(("wide", "narrow"), None),
    )
    out_specs = (
        P(("wide", "narrow"), None),
        P(("wide", "narrow"), None),
        P(("wide", "narrow"), None),
        P(("wide", "narrow"), None),
        P(("wide", "narrow"), None),
        P(("wide", "narrow"), None),
        P(("wide", "narrow"), None),
        P(("wide", "narrow"), None),
        P(("wide", "narrow"), None),
    )
    devices = mesh.shape["wide"] * mesh.shape["narrow"]
    bits = devices.bit_length() - 1

    def body(*args):
        if args[2].shape[0] % 16 or args[3].shape[0] % 16 or devices != 1 << bits or bits < 3:
            return plain_body(*args)
        return fused_body(mesh.shape["wide"], mesh.shape["narrow"], *args)

    return jax.shard_map(body, mesh=mesh, in_specs=in_specs, out_specs=out_specs, check_vma=False)
```

```python
import types

import jax
import jax.numpy as jnp
from jax import lax
from jax.experimental import pallas as pl
from jax.experimental.pallas import tpu as pltpu
from jax.sharding import PartitionSpec as P

D = 512
HEADS = 8
HEAD_DIM = 64
FF = 2048
SEGS = 6
AVG_STEPS = 4


SCORE_SCALE = 0.125
EPSILON = 1e-05
MASKED = -1e30


def matmul(left, right):
    return jnp.dot(left, right, preferred_element_type=jnp.float32)


def matmul_first(left, right):
    return lax.dot_general(
        left, right, (((0,), (0,)), ((), ())), preferred_element_type=jnp.float32
    )


def matmul_last(left, right):
    return lax.dot_general(
        left, right, (((1,), (1,)), ((), ())), preferred_element_type=jnp.float32
    )


def segment_numbers(lengths, count):
    endings = jnp.cumsum(lengths)
    places = jnp.arange(count, dtype=jnp.int32)
    return jnp.sum((places[:, None] >= endings[None, :]).astype(jnp.int32), axis=1)


def norm_forward(before, norm_gain, norm_shift):
    centred = before - jnp.mean(before, axis=-1, keepdims=True)
    inverse = lax.rsqrt(jnp.mean(centred * centred, axis=-1, keepdims=True) + EPSILON)
    normed = centred * inverse
    return (normed * norm_gain + norm_shift, normed, inverse)


def norm_backward(gradient, normed, inverse, norm_gain):
    scaled = gradient * norm_gain
    inner_sum = jnp.mean(scaled * normed, axis=-1, keepdims=True)
    before_grad = inverse * (scaled - jnp.mean(scaled, axis=-1, keepdims=True) - normed * inner_sum)
    return (before_grad, jnp.sum(gradient * normed, axis=0), jnp.sum(gradient, axis=0))


def split_heads(matrix):
    return matrix.reshape(matrix.shape[0], HEADS, HEAD_DIM)


def masked_scores(query_block, key_heads, segment_block, key_segment):
    scores = (
        jnp.einsum(
            "qhe,khe->hqk", split_heads(query_block), key_heads, preferred_element_type=jnp.float32
        )
        * SCORE_SCALE
    )
    allowed = segment_block[:, None] == key_segment[None, :]
    return jnp.where(allowed[None], scores, MASKED)


def attend_forward(queries, keys_in, values_in, query_segment, key_segment):
    row_count = queries.shape[0]
    block_rows = min(512, row_count)
    blocks = row_count // block_rows
    key_heads = split_heads(keys_in)
    value_heads = split_heads(values_in)

    def attend_block(pieces):
        query_block, segment_block = pieces
        scores = masked_scores(query_block, key_heads, segment_block, key_segment)
        highest = jnp.max(scores, axis=-1, keepdims=True)
        exponent = jnp.exp(scores - highest)
        totals = jnp.sum(exponent, axis=-1, keepdims=True)
        shares = (exponent / totals).astype(jnp.bfloat16)
        mixed = jnp.einsum("hqk,khe->qhe", shares, value_heads, preferred_element_type=jnp.float32)
        return (
            mixed.reshape(block_rows, HEADS * HEAD_DIM).astype(jnp.bfloat16),
            (highest + jnp.log(totals))[..., 0],
        )

    mixed, logsum = lax.map(
        attend_block,
        (queries.reshape(blocks, block_rows, -1), query_segment.reshape(blocks, block_rows)),
    )
    return (mixed.reshape(row_count, -1), logsum)


def attend_backward(queries, keys_in, values_in, mixed_grad, logsum, query_segment, key_segment):
    row_count = queries.shape[0]
    block_rows = min(512, row_count)
    blocks = row_count // block_rows
    key_heads = split_heads(keys_in)
    value_heads = split_heads(values_in)

    def backward_block(carried, pieces):
        key_sum, value_sum = carried
        query_block, grad_block, logsum_block, segment_block = pieces
        scores = masked_scores(query_block, key_heads, segment_block, key_segment)
        shares = jnp.exp(scores - logsum_block[..., None])
        grad_heads = split_heads(grad_block)
        share_grad = jnp.einsum(
            "qhe,khe->hqk", grad_heads, value_heads, preferred_element_type=jnp.float32
        )
        inner_sum = jnp.sum(shares * share_grad, axis=-1, keepdims=True)
        score_grad = (shares * (share_grad - inner_sum)).astype(jnp.bfloat16)
        query_grad = (
            jnp.einsum("hqk,khe->qhe", score_grad, key_heads, preferred_element_type=jnp.float32)
            * SCORE_SCALE
        )
        key_sum = (
            key_sum
            + jnp.einsum(
                "hqk,qhe->khe",
                score_grad,
                split_heads(query_block),
                preferred_element_type=jnp.float32,
            )
            * SCORE_SCALE
        )
        value_sum = value_sum + jnp.einsum(
            "hqk,qhe->khe",
            shares.astype(jnp.bfloat16),
            grad_heads,
            preferred_element_type=jnp.float32,
        )
        return ((key_sum, value_sum), query_grad.reshape(block_rows, HEADS * HEAD_DIM))

    zeros_init = jnp.zeros((keys_in.shape[0], HEADS, HEAD_DIM), jnp.float32)
    pieces = (
        queries.reshape(blocks, block_rows, -1),
        mixed_grad.reshape(blocks, block_rows, -1),
        logsum,
        query_segment.reshape(blocks, block_rows),
    )
    (key_sum, value_sum), query_grad = lax.scan(backward_block, (zeros_init, zeros_init), pieces)
    return (
        query_grad.reshape(row_count, -1),
        key_sum.reshape(keys_in.shape[0], -1),
        value_sum.reshape(values_in.shape[0], -1),
    )


def plain_body(
    tokens,
    memory,
    w_wide,
    w_tall,
    vecs,
    avg_wide,
    avg_tall,
    avg_vecs,
    tgt_lengths,
    src_lengths,
    cotangent,
):
    wide_all, tall_all, vector_all = (
        lax.all_gather(w_wide, ("wide", "narrow"), axis=0, tiled=True),
        lax.all_gather(w_tall, ("wide", "narrow"), axis=0, tiled=True),
        lax.all_gather(vecs, ("wide", "narrow"), axis=0, tiled=True),
    )
    vectors = vector_all.astype(jnp.float32)
    spread = FF // D
    offset = 6 + spread
    columns = [wide_all[:, index * D : (index + 1) * D] for index in range(8)]
    target_query, target_key, target_value, target_output = (
        columns[0],
        columns[1],
        columns[2],
        columns[3],
    )
    source_query, source_key, source_value, source_output = (
        columns[4],
        columns[5],
        columns[6],
        columns[7],
    )
    up_weight = wide_all[:, 8 * D :]
    down_weight = tall_all[:FF]
    slot_left = tall_all[FF : FF + D]
    slot_right = tall_all[FF + D :]
    up_bias = vectors[:, 6:offset].T.reshape(FF)
    row_count = tokens.shape[0]
    target_segment = segment_numbers(tgt_lengths[0], row_count)
    source_segment = segment_numbers(src_lengths[0], memory.shape[0])
    valid_rows = (target_segment < SEGS - 1).astype(jnp.float32)[:, None]
    follow = (
        jnp.concatenate([target_segment[1:], jnp.full((1,), -1, jnp.int32)]) == target_segment
    ).astype(jnp.float32)[:, None]
    queries_self = (matmul(tokens, target_query) + vectors[:, 0]).astype(jnp.bfloat16)
    keys_self = matmul(tokens, target_key).astype(jnp.bfloat16)
    values_self = (matmul(tokens, target_value) + vectors[:, 1]).astype(jnp.bfloat16)
    mixed_self, logsum_self = attend_forward(
        queries_self, keys_self, values_self, target_segment, target_segment
    )
    first, normed_first, inverse_first = norm_forward(
        tokens.astype(jnp.float32) + matmul(mixed_self, target_output) + vectors[:, 2],
        vectors[:, offset + 2],
        vectors[:, offset + 3],
    )
    first_low = first.astype(jnp.bfloat16)
    queries_cross = (matmul(first_low, source_query) + vectors[:, 3]).astype(jnp.bfloat16)
    keys_cross = matmul(memory, source_key).astype(jnp.bfloat16)
    values_cross = (matmul(memory, source_value) + vectors[:, 4]).astype(jnp.bfloat16)
    mixed_cross, logsum_cross = attend_forward(
        queries_cross, keys_cross, values_cross, target_segment, source_segment
    )
    second, normed_second, inverse_second = norm_forward(
        first + matmul(mixed_cross, source_output) + vectors[:, 5],
        vectors[:, offset + 4],
        vectors[:, offset + 5],
    )
    second_low = second.astype(jnp.bfloat16)
    hidden = matmul(second_low, up_weight) + up_bias
    active = jax.nn.gelu(hidden).astype(jnp.bfloat16)
    third, normed_third, inverse_third = norm_forward(
        second + matmul(active, down_weight) + vectors[:, offset],
        vectors[:, offset + 6],
        vectors[:, offset + 7],
    )
    third_low = third.astype(jnp.bfloat16)
    right_half = jnp.concatenate([third_low[1:], jnp.zeros((1, D), jnp.bfloat16)]) * follow.astype(
        jnp.bfloat16
    )
    slots = (
        (matmul(third_low, slot_left) + matmul(right_half, slot_right) + vectors[:, offset + 1])
        * valid_rows
    ).astype(jnp.bfloat16)
    seed_grad = cotangent * valid_rows.astype(jnp.bfloat16)
    grad_slot_bias = jnp.sum(seed_grad.astype(jnp.float32), axis=0)
    grad_left = matmul_first(third_low, seed_grad)
    grad_right = matmul_first(right_half, seed_grad)
    right_back = matmul_last(seed_grad, slot_right) * follow
    grad_third = matmul_last(seed_grad, slot_left) + jnp.concatenate(
        [jnp.zeros((1, D), jnp.float32), right_back[:-1]]
    )
    grad_pre_third, grad_gain_third, grad_shift_third = norm_backward(
        grad_third, normed_third, inverse_third, vectors[:, offset + 6]
    )
    pre_third_low = grad_pre_third.astype(jnp.bfloat16)
    grad_down = matmul_first(active, pre_third_low)
    grad_tall_all = jnp.concatenate([grad_down, grad_left, grad_right], axis=0)
    gelu_value, gelu_pull = jax.vjp(jax.nn.gelu, hidden)
    grad_hidden = gelu_pull(matmul_last(pre_third_low, down_weight))[0]
    hidden_low = grad_hidden.astype(jnp.bfloat16)
    grad_up = matmul_first(second_low, hidden_low)
    grad_second = grad_pre_third + matmul_last(hidden_low, up_weight)
    grad_pre_second, grad_gain_second, grad_shift_second = norm_backward(
        grad_second, normed_second, inverse_second, vectors[:, offset + 4]
    )
    pre_second_low = grad_pre_second.astype(jnp.bfloat16)
    grad_source_output = matmul_first(mixed_cross, pre_second_low)
    mixed_cross_grad = matmul_last(pre_second_low, source_output).astype(jnp.bfloat16)
    cross_query_grad, cross_key_grad, cross_value_grad = attend_backward(
        queries_cross,
        keys_cross,
        values_cross,
        mixed_cross_grad,
        logsum_cross,
        target_segment,
        source_segment,
    )
    cross_query_low = cross_query_grad.astype(jnp.bfloat16)
    cross_key_low = cross_key_grad.astype(jnp.bfloat16)
    cross_value_low = cross_value_grad.astype(jnp.bfloat16)
    grad_source_query = matmul_first(first_low, cross_query_low)
    grad_source_key = matmul_first(memory, cross_key_low)
    grad_source_value = matmul_first(memory, cross_value_low)
    grad_memory = matmul_last(cross_key_low, source_key) + matmul_last(
        cross_value_low, source_value
    )
    grad_first = grad_pre_second + matmul_last(cross_query_low, source_query)
    grad_pre_first, grad_gain_first, grad_shift_first = norm_backward(
        grad_first, normed_first, inverse_first, vectors[:, offset + 2]
    )
    pre_first_low = grad_pre_first.astype(jnp.bfloat16)
    grad_target_output = matmul_first(mixed_self, pre_first_low)
    mixed_self_grad = matmul_last(pre_first_low, target_output).astype(jnp.bfloat16)
    self_query_grad, self_key_grad, self_value_grad = attend_backward(
        queries_self,
        keys_self,
        values_self,
        mixed_self_grad,
        logsum_self,
        target_segment,
        target_segment,
    )
    self_query_low = self_query_grad.astype(jnp.bfloat16)
    self_key_low = self_key_grad.astype(jnp.bfloat16)
    self_value_low = self_value_grad.astype(jnp.bfloat16)
    grad_target_query = matmul_first(tokens, self_query_low)
    grad_target_key = matmul_first(tokens, self_key_low)
    grad_target_value = matmul_first(tokens, self_value_low)
    grad_tokens = (
        grad_pre_first
        + matmul_last(self_query_low, target_query)
        + matmul_last(self_key_low, target_key)
        + matmul_last(self_value_low, target_value)
    )
    grad_wide_all = jnp.concatenate(
        [
            grad_target_query,
            grad_target_key,
            grad_target_value,
            grad_target_output,
            grad_source_query,
            grad_source_key,
            grad_source_value,
            grad_source_output,
            grad_up,
        ],
        axis=1,
    )
    bias_front = jnp.stack(
        [
            jnp.sum(self_query_grad, axis=0),
            jnp.sum(self_value_grad, axis=0),
            jnp.sum(grad_pre_first, axis=0),
            jnp.sum(cross_query_grad, axis=0),
            jnp.sum(cross_value_grad, axis=0),
            jnp.sum(grad_pre_second, axis=0),
        ],
        axis=1,
    )
    bias_middle = jnp.sum(grad_hidden, axis=0).reshape(spread, D).T
    bias_back = jnp.stack(
        [
            jnp.sum(grad_pre_third, axis=0),
            grad_slot_bias,
            grad_gain_first,
            grad_shift_first,
            grad_gain_second,
            grad_shift_second,
            grad_gain_third,
            grad_shift_third,
        ],
        axis=1,
    )
    grad_vector_all = jnp.concatenate([bias_front, bias_middle, bias_back], axis=1)
    grad_wide, grad_tall, grad_vecs = (
        lax.psum_scatter(grad_wide_all, ("wide", "narrow"), scatter_dimension=0, tiled=True),
        lax.psum_scatter(grad_tall_all, ("wide", "narrow"), scatter_dimension=0, tiled=True),
        lax.psum_scatter(grad_vector_all, ("wide", "narrow"), scatter_dimension=0, tiled=True),
    )
    new_avg_wide = avg_wide + (w_wide.astype(jnp.float32) - avg_wide) / AVG_STEPS
    new_avg_tall = avg_tall + (w_tall.astype(jnp.float32) - avg_tall) / AVG_STEPS
    new_avg_vecs = avg_vecs + (vecs.astype(jnp.float32) - avg_vecs) / AVG_STEPS
    return (
        slots,
        grad_tokens,
        grad_memory,
        grad_wide,
        grad_tall,
        grad_vecs,
        new_avg_wide,
        new_avg_tall,
        new_avg_vecs,
    )


BF16 = jnp.bfloat16
F32 = jnp.float32
AUG = 80
BIG = 1e30
TILE = 256
MESH_IDS = pl.DeviceIdType.MESH
BIAS_OUT, GAIN = 10, 12
TALL_CUT = 3
OUT_SEMAPHORES = 24
PAIR = 6 * HEAD_DIM
PAIR_GROUPS = ((0,), (1,), (2, 3))
GATHER_STEPS = {
    0: ((0, 0),),
    1: ((1, 0), (0, 2), (1, 1), (2, 0), (0, 3),),
    2: ((9, 0),),
    4: ((3, 0),),
    5: ((1, 2), (2, 1), (1, 3),),
    7: ((4, 0),),
    9: ((3, 1), (5, 0), (2, 2), (2, 3),),
    11: ((4, 1),),
    12: ((6, 0), (9, 1), (3, 2),),
    13: ((5, 1), (7, 0),),
    14: ((3, 3),),
    16: ((4, 2),),
    19: ((6, 1),),
    20: ((4, 3),),
    21: ((8, 0),),
    23: ((5, 2),),
    25: ((7, 1),),
    26: ((5, 3),),
    28: ((6, 2),),
    30: ((8, 1), (6, 3),),
    32: ((9, 2),),
    33: ((7, 2),),
    35: ((9, 3), (8, 2), (7, 3), (8, 3),),
}
SUM_STEPS = {
    5: ((0, 0),),
    10: ((1, 0),),
    12: ((0, 1),),
    20: ((1, 1),),
    24: ((2, 0), (0, 2),),
    25: ((3, 0), (1, 2),),
    27: ((4, 0), (2, 1),),
    29: ((3, 1), (5, 0),),
    30: ((4, 1), (0, 3),),
    37: ((2, 2), (6, 0),),
    38: ((7, 0), (3, 2),),
    39: ((5, 1),),
    40: ((1, 3), (4, 2),),
    44: ((6, 1), (7, 1), (5, 2), (6, 2), (7, 2), (2, 3), (3, 3), (4, 3), (5, 3), (6, 3), (7, 3),),
}


def dot(left, right, left_dim, right_dim):
    return lax.dot_general(
        left, right, (((left_dim,), (right_dim,)), ((), ())), preferred_element_type=F32
    )


def bands(query_rows, key_rows, longest, tile=TILE):
    found = []
    for start in range(0, query_rows, tile):
        if longest is None:
            found.append((0, key_rows))
            continue
        low = max(0, (start - longest + 1) // TILE * TILE)
        high = min(key_rows, -(-(start + TILE + longest - 1) // TILE) * TILE)
        found.append((low, high))
    return found


def column_max(scores):
    rows, columns = scores.shape
    return jnp.max(
        jnp.max(scores.reshape(rows // 64, 64, columns), axis=0), axis=0, keepdims=True
    )


def split_three(value):
    high = value.astype(BF16).astype(F32)
    middle = (value - high).astype(BF16).astype(F32)
    low = (value - high - middle).astype(BF16).astype(F32)
    return high, middle, low


def feature_rows(base, first, parts):
    place = lax.broadcasted_iota(jnp.int32, base.shape, 0)
    for step, part in enumerate(parts):
        base = jnp.where(place == first + step, part, base)
    return base


def gelu_pair(u):
    scale = 0.7978845608028654
    inner = jnp.tanh(scale * (u + 0.044715 * (u * u * u)))
    half = 0.5 * (1.0 + inner)
    slope = half + 0.5 * u * (1.0 - inner * inner) * (scale * (1.0 + 3 * 0.044715 * (u * u)))
    return u * half, slope


def normalize(before, gain, shift):
    centred = before - jnp.mean(before, axis=-1, keepdims=True)
    inverse = lax.rsqrt(jnp.mean(centred * centred, axis=-1, keepdims=True) + EPSILON)
    normed = centred * inverse
    return normed * gain + shift, normed, inverse


def by_pair(hooks):
    found = {}
    for head, act in hooks.items():
        found.setdefault(head // 2, []).append(act)

    def together(acts):
        def act():
            for one in acts:
                one()

        return act

    return {pair: together(acts) for pair, acts in found.items()}


def attention_forward(queries, keys, values, mixed, scores, ranges, heads, hooks):
    tiles = len(ranges)
    width = queries.shape[2] // tiles

    def put(head, tile):
        low, high = ranges[tile]
        scores[tile % 2][0 : high - low, :] = dot(
            keys[head, :, low:high], queries[head, :, tile * width : (tile + 1) * width], 0, 0
        )

    put(heads[0], 0)

    def one_head(head, carried):
        for tile, (low, high) in enumerate(ranges):
            if tile + 1 < tiles:
                put(head, tile + 1)
            else:
                put(jnp.minimum(head + 1, heads[1] - 1), 0)
            span = slice(tile * width, (tile + 1) * width)
            current = scores[tile % 2][0 : high - low, :]
            highest = column_max(current)
            shares = jnp.exp(current - highest).astype(BF16)
            gathered = dot(values[head, :, low:high], shares, 1, 0)
            total = gathered[HEAD_DIM : HEAD_DIM + 1]
            rows = pl.ds(pl.multiple_of(head * HEAD_DIM, HEAD_DIM), HEAD_DIM)
            mixed[rows, span] = (gathered[:HEAD_DIM] * (1.0 / total)).astype(BF16)
            queries[head, HEAD_DIM:, span] = feature_rows(
                queries[head, HEAD_DIM:, span].astype(F32),
                SEGS,
                split_three(-(highest + jnp.log(total))),
            ).astype(BF16)
        for at, hook in hooks.items():
            pl.when(head == at)(hook)
        return carried

    lax.fori_loop(heads[0], heads[1], one_head, 0)


def attention_backward(queries, keys, values, grads, outs, sums, shares, score_grads, ranges, hooks):
    key_rows = keys.shape[2]
    key_sum, value_sum = sums
    tiles = len(ranges)

    def put(head, tile):
        low, high = ranges[tile]
        span = slice(tile * TILE, (tile + 1) * TILE)
        share = jnp.exp(dot(queries[head, :, span], keys[head, :, low:high], 0, 0))
        share_grad = dot(grads[head, :, span], values[head, :, low:high], 0, 0)
        shares[tile % 2][:, 0 : high - low] = share.astype(BF16)
        score_grads[tile % 2][:, 0 : high - low] = (share * share_grad).astype(BF16)

    put(0, 0)

    def one_head(head):
        key_sum[:, 0:key_rows] = jnp.zeros((HEAD_DIM, key_rows), F32)
        value_sum[:, 0:key_rows] = jnp.zeros((HEAD_DIM, key_rows), F32)
        query_out, key_out, value_out = [out(head) for out in outs]
        for tile, (low, high) in enumerate(ranges):
            if tile + 1 < tiles:
                put(head, tile + 1)
            else:
                put(jnp.minimum(head + 1, HEADS - 1), 0)
            span = slice(tile * TILE, (tile + 1) * TILE)
            share = shares[tile % 2][:, 0 : high - low]
            score_grad = score_grads[tile % 2][:, 0 : high - low]
            query_out[:, span] = (
                dot(keys[head, 0:HEAD_DIM, low:high], score_grad, 1, 1) * SCORE_SCALE
            ).astype(BF16)
            key_sum[:, low:high] += dot(queries[head, 0:HEAD_DIM, span], score_grad, 1, 0)
            value_sum[:, low:high] += dot(grads[head, 0:HEAD_DIM, span], share, 1, 0)
        key_out[...] = key_sum[:, 0:key_rows].astype(BF16)
        value_out[...] = value_sum[:, 0:key_rows].astype(BF16)

    def one_pair(pair, carried):
        one_head(2 * pair)
        one_head(2 * pair + 1)
        for at, hook in by_pair(hooks).items():
            pl.when(pair == at)(hook)
        return carried

    lax.fori_loop(0, HEADS // 2, one_pair, 0)


class Exchange:
    def __init__(self, wide, narrow):
        self.narrow_bits = narrow.bit_length() - 1
        self.count = (wide * narrow).bit_length() - 1
        self.line = 1 << (self.count - 3)
        self.place = (lax.axis_index("wide"), lax.axis_index("narrow"))
        number = self.place[0] * narrow + self.place[1]
        self.bits = [(number >> bit) & 1 for bit in range(self.count)]
        self.own = tuple(self.bits[bit] for bit in reversed(range(self.count)))
        self.far = list(range(3, self.count))
        self.masks = [1, 2, 4, 6] + [other << 3 for other in range(1, self.line)]
        core = self.bits[0]
        self.first, self.second, self.both = {1: 1 - core, 2: core}, {1: core, 2: 1 - core}, {1: 1, 2: 1}

    def device(self, mask):
        wide, narrow = self.place
        return (wide ^ (mask >> self.narrow_bits), narrow ^ (mask & ((1 << self.narrow_bits) - 1)))

    def greet(self):
        barrier = pltpu.get_barrier_semaphore()
        for mask in self.masks:
            pl.semaphore_signal(
                barrier, inc=1, device_id=self.device(mask), device_id_type=MESH_IDS
            )

    def meet(self):
        pl.semaphore_wait(pltpu.get_barrier_semaphore(), len(self.masks))

    def neighbour(self, second):
        core = self.bits[0]
        take = core if not second else 1 - core
        one, other = self.device(2), self.device(4)
        return tuple(a + (b - a) * take for a, b in zip(one, other))

    def view(self, part, open_bits, flips=None):
        index = tuple(
            slice(None) if bit in open_bits else self.turned(bit, flips)
            for bit in reversed(range(self.count))
        )
        return part.ref.at[index + part.where]

    def turned(self, bit, flips):
        flip = (flips or {}).get(bit, 0)
        return self.bits[bit] + flip - 2 * self.bits[bit] * flip


class Part:
    def __init__(self, ref, rows=None, columns=None, buffers=(), outs=()):
        cut = lambda ends: slice(None) if ends is None else pl.ds(ends[0], ends[1] - ends[0])
        self.ref, self.where, self.buffers, self.outs = ref, (cut(rows), cut(columns)), buffers, outs


class Transfer:
    def __init__(self, net, pieces, send, receive):
        self.net, self.pieces, self.send, self.receive = net, pieces, send, receive
        self.line = tuple(range(4, 3 + net.line))

    def copy(self, piece, part, slot, source, target, device):
        return pltpu.make_async_remote_copy(
            source,
            target,
            self.send.at[piece, slot, part],
            self.receive.at[piece, slot, part],
            device_id=device,
            device_id_type=MESH_IDS,
        )

    def each(self, piece, stage, act):
        for number in range(len(self.pieces[piece])):
            for slot in self.slots(piece, stage):
                act(self.one(piece, number, slot))

    def begin(self, piece, slot):
        for number in range(len(self.pieces[piece])):
            self.one(piece, number, slot).start()

    def finish(self, pieces=None):
        for piece in range(len(self.pieces)) if pieces is None else pieces:
            for stage in range(4):
                self.each(piece, stage, lambda copy: copy.wait_send())


class Gather(Transfer):
    def __init__(self, net, pieces, send, receive):
        super().__init__(net, pieces, send, receive)
        self.last = len(pieces) - 1

    def slots(self, piece, stage):
        if piece == 0:
            return (self.line, (), (0, 1, 2), (3,))[stage]
        if piece == self.last:
            return ((0, 1), (2,), self.line, (3,))[stage]
        return (self.line, (0,), (1, 2), (3,))[stage]

    def one(self, piece, number, slot):
        net, part = self.net, self.pieces[piece][number]
        lines = [] if piece == self.last else net.far
        if slot == 3:
            view, device = net.view(part, net.far + [1, 2]), net.device(1)
        elif slot > 3:
            near = [1, 2] if piece == self.last else []
            view, device = net.view(part, near), net.device((slot - 3) << 3)
        elif slot == 2 and piece == 0:
            view, device = net.view(part, lines), net.device(6)
        else:
            view = net.view(part, lines, net.first if slot == 2 else None)
            device = net.neighbour(slot > 0)
        return self.copy(piece, number, slot, view, view, device)

    def start(self, piece):
        if piece == self.last:
            self.begin(piece, 0)
            self.begin(piece, 1)
        else:
            self.each(piece, 0, lambda copy: copy.start())

    def step(self, piece, stage):
        self.each(piece, stage, lambda copy: copy.wait_recv())
        if piece == self.last and stage < 2:
            self.each(piece, stage + 1, lambda copy: copy.start())
        elif stage == 0:
            self.begin(piece, 0)
            self.begin(piece, 1)
            if piece == 0:
                self.begin(0, 2)
                self.start(1)
            if piece + 2 < self.last:
                self.start(piece + 2)
        elif stage == 1 and piece:
            self.begin(piece, 2)
        elif stage == 2:
            self.begin(piece, 3)


class Sum(Transfer):
    def slots(self, piece, stage):
        return ((0,), (1,), (2, 3), self.line)[stage]

    def one(self, piece, number, slot):
        net, part = self.net, self.pieces[piece][number]
        if slot == 0:
            view, device = net.view(part, net.far + [1, 2], {0: 1}), net.device(1)
        elif slot > 3:
            mask = (slot - 3) << 3
            view, device = net.view(part, [], {bit: mask >> bit & 1 for bit in net.far}), net.device(mask)
        else:
            view = net.view(part, net.far, (None, net.both, net.second, net.first)[slot])
            device = net.neighbour(slot < 3)
        target = part.buffers[4].at[slot - 4] if slot > 3 else part.buffers[slot]
        return self.copy(piece, number, slot, view, target, device)

    def start(self, piece):
        self.begin(piece, 0)

    def add(self, piece, stage):
        net = self.net
        if stage == 3:
            for part in self.pieces[piece]:
                value = part.ref[net.own + part.where].astype(F32)
                for other in range(1, net.line):
                    value = value + part.buffers[4][other - 1].astype(F32)
                for low, high, staged, out, semaphore in part.outs:
                    staged[...] = value[:, low:high]
                    pltpu.make_async_copy(staged, out, semaphore).start()
            return
        rest = net.far + ([1, 2] if stage == 0 else [])
        rest.sort()

        def one_shard(step, carried):
            place = {bit: (step >> at) & 1 for at, bit in enumerate(rest)}
            index = tuple(
                place[bit] if bit in place else net.turned(bit, net.first if stage == 1 else None)
                for bit in reversed(range(net.count))
            )
            arrived = tuple(place[bit] for bit in reversed(rest)) + (slice(None), slice(None))
            for part in self.pieces[piece]:
                where = index + part.where
                if stage == 2:
                    value = (
                        part.ref[where].astype(F32)
                        + part.buffers[2][arrived].astype(F32)
                        + part.buffers[3][arrived].astype(F32)
                    )
                else:
                    value = part.ref[where] + part.buffers[stage][arrived]
                part.ref[where] = value.astype(part.ref.dtype)
            return carried

        lax.fori_loop(0, 1 << len(rest), one_shard, 0, unroll=True)

    def step(self, piece, stage):
        self.each(piece, stage, lambda copy: copy.wait_recv())
        self.add(piece, stage)
        if stage == 0:
            self.begin(piece, 1)
            self.begin(piece, 2)
        elif stage == 1:
            self.begin(piece, 3)
        elif stage == 2:
            self.each(piece, 3, lambda copy: copy.start())

    def finish(self):
        super().finish()
        for piece in self.pieces:
            for part in piece:
                for _, _, staged, out, semaphore in part.outs:
                    pltpu.make_async_copy(staged, out, semaphore).wait()


class Plan:
    def __init__(self, transfer, table):
        self.transfer, self.table, self.stop = transfer, table, 0

    def next(self):
        taken = self.table.get(self.stop, ())
        self.stop += 1

        def act():
            for piece, stage in taken:
                self.transfer.step(piece, stage)

        return act if taken else None

    def now(self):
        act = self.next()
        if act:
            act()

    def loop(self, places):
        found = {place: self.next() for place in places}
        return {place: act for place, act in found.items() if act}


def layer_kernel(r, wide_size, narrow_size):
    net = Exchange(wide_size, narrow_size)
    net.greet()
    devices = wide_size * narrow_size
    wide7, tall7, vec7, gvec7 = r.wide, r.tall, r.vec, r.grad_vec
    wide = wide7.reshape(devices * wide7.shape[-2], wide7.shape[-1])
    tall = tall7.reshape(devices * tall7.shape[-2], tall7.shape[-1])
    slope7 = r.slope
    slope = slope7.reshape(devices * slope7.shape[-2], slope7.shape[-1])
    own_rows = (0, wide7.shape[-2])
    tokens, memory, seed, seed_next = r.tokens, r.memory, r.seed, r.seed_next
    rows, sources = tokens.shape[0], memory.shape[0]
    tiles = rows // TILE
    local = r.local

    wide_moves = [
        (block * D + pair * PAIR // 3, pair * PAIR + block * PAIR // 3, PAIR // 3)
        for pair in range(HEADS // 2)
        for block in range(3)
    ] + [(3 * D, 3 * D, wide7.shape[-1] - 3 * D)]
    loads = [
        pltpu.make_async_copy(
            r.w_wide.at[:, pl.ds(low, width)],
            wide7.at[net.own + (slice(None), pl.ds(high, width))],
            r.own_done.at[number],
        )
        for number, (low, high, width) in enumerate(wide_moves)
    ] + [
        pltpu.make_async_copy(r.w_tall, tall7.at[net.own], local.at[1]),
        pltpu.make_async_copy(r.vecs, vec7.at[net.own], local.at[2]),
        pltpu.make_async_copy(r.tokens_in, tokens, local.at[3]),
        pltpu.make_async_copy(r.memory_in, memory, local.at[4]),
        pltpu.make_async_copy(r.cotangent, seed, local.at[5]),
    ]
    for copy in loads:
        copy.start()

    tall_rows = tall7.shape[-2]
    tall_cuts = [(low, low + tall_rows // TALL_CUT) for low in range(0, tall_rows, tall_rows // TALL_CUT)]

    def wide_part(low, high):
        return [Part(wide7, None, (low, high))]

    gather = Gather(
        net,
        [
            wide_part(0, PAIR) + [Part(vec7)],
            wide_part(PAIR, 2 * PAIR),
            wide_part(2 * PAIR, 4 * PAIR),
            wide_part(3 * D, 5 * D),
            wide_part(5 * D, 7 * D),
            wide_part(7 * D, 9 * D),
            wide_part(9 * D, 12 * D),
        ]
        + [[Part(tall7, cut)] for cut in tall_cuts],
        r.gather_send,
        r.gather_receive,
    )
    plan = Plan(gather, GATHER_STEPS)
    out_semaphores = iter(range(OUT_SEMAPHORES))

    def out_of(low, high, staged, out):
        return (low, high, staged, out, r.out_done.at[next(out_semaphores)])

    def wide_out(low, high, start):
        columns = pl.ds(start, high - low)
        return out_of(low, high, r.out_wide.at[:, columns], r.grad_wide.at[:, columns])

    def wide_sum(low, high, buffers):
        return [Part(wide7, None, (low, high), buffers, [wide_out(0, high - low, low)])]

    def self_sum(pair):
        third = PAIR // 3
        outs = [
            wide_out(block * third, (block + 1) * third, block * D + pair * third)
            for block in range(3)
        ]
        columns = (pair * PAIR, (pair + 1) * PAIR)
        return [Part(slope7, own_rows, columns, r.in_self[pair], outs)]

    vec_out = out_of(0, 128, r.out_vec, r.grad_vecs)
    total = Sum(
        net,
        [
            [Part(tall7, None, None, r.in_tall, [out_of(0, D, r.out_tall, r.grad_tall)])],
            wide_sum(8 * D, 12 * D, r.in_up),
            wide_sum(3 * D, 8 * D, r.in_mid),
        ]
        + [self_sum(pair) for pair in range(HEADS // 2)]
        + [[Part(gvec7, None, None, r.in_vec, [vec_out])]],
        r.sum_send,
        r.sum_receive,
    )
    TALL, UP, MID, SELF = range(4)
    VECTORS = SELF + HEADS // 2
    sum_plan = Plan(total, SUM_STEPS)

    for copy in loads[:-3]:
        copy.wait()
    net.meet()
    gather.start(0)
    gather.start(gather.last)

    def endings(lengths):
        found, running = [], 0
        for index in range(SEGS):
            running = running + lengths[0, index]
            found.append(running)
        return found

    target_ends = endings(r.tgt_lengths)
    source_ends = endings(r.src_lengths)

    def chosen(ends, count):
        place = lax.broadcasted_iota(jnp.int32, (16, count), 1)
        segment = jnp.zeros((16, count), jnp.int32)
        for end in ends:
            segment = segment + (place >= end).astype(jnp.int32)
        return segment == lax.broadcasted_iota(jnp.int32, (16, count), 0)

    def query_features(ends, count):
        return jnp.where(chosen(ends, count), 1.0, 0.0).astype(BF16)

    def key_features(ends, count):
        row = lax.broadcasted_iota(jnp.int32, (16, count), 0)
        masked = jnp.where(chosen(ends, count), 0.0, -BIG)
        return jnp.where(row < SEGS, masked, jnp.where(row < SEGS + 3, 1.0, 0.0)).astype(BF16)

    def value_features(count):
        row = lax.broadcasted_iota(jnp.int32, (16, count), 0)
        return jnp.where(row < 3, 1.0, 0.0).astype(BF16)

    def every_head(ref, features):
        ref[:, HEAD_DIM:, :] = jnp.broadcast_to(features[None], (HEADS,) + features.shape)

    q, k, v, q2, k2, v2 = r.q, r.k, r.v, r.q2, r.k2, r.v2
    every_head(q, query_features(target_ends, rows))
    every_head(q2, query_features(target_ends, rows))
    every_head(k, key_features(target_ends, rows))
    every_head(k2, key_features(source_ends, sources))
    every_head(v, value_features(rows))
    every_head(v2, value_features(sources))
    plan.now()

    def position(tile):
        return tile * TILE + lax.broadcasted_iota(jnp.int32, (TILE, 1), 0)

    def valid(tile):
        return jnp.where(position(tile) < target_ends[SEGS - 2], 1.0, 0.0)

    def follow(tile):
        after = position(tile) + 1
        ended = after == target_ends[0]
        for end in target_ends[1:]:
            ended = ended | (after == end)
        return jnp.where(ended, 0.0, 1.0)

    def span(tile):
        return pl.ds(tile * TILE, TILE)

    shift, res = r.shift, r.res
    loads[-1].wait()
    shift[0:8, :] = jnp.zeros((8, D), F32)
    for tile in range(tiles):
        masked = seed[span(tile), :].astype(F32) * valid(tile)
        seed[span(tile), :] = masked.astype(BF16)
        shift[pl.ds(tile * TILE + 8, TILE), :] = masked * follow(tile)
    for tile in range(tiles):
        seed_next[span(tile), :] = shift[pl.ds(tile * TILE + 7, TILE), :].astype(BF16)
    r.grad_rows[...] = jnp.zeros_like(r.grad_rows)
    r.grad_columns[...] = jnp.zeros_like(r.grad_columns)
    loads[-3].wait()
    loads[-2].wait()

    def row(index):
        return r.row_vectors[index : index + 1, :]

    def column(index):
        return vec7[...].reshape(D, vec7.shape[-1])[:, index : index + 1].astype(F32)

    def heads_of(value):
        return value.reshape(value.shape[0] // HEAD_DIM, HEAD_DIM, value.shape[1])

    def scaled(value):
        return (value.astype(BF16).astype(F32) * SCORE_SCALE).astype(BF16)

    def wide_column(index):
        return wide[:, index * D : (index + 1) * D]

    self_ranges = bands(rows, rows, 512)
    cross_ranges = bands(rows, sources, None)
    cross_wide = bands(rows, sources, None, 2 * TILE)
    cross_scores = [shift.at[pl.ds(start, sources), :] for start in (0, sources)]
    a, a2 = r.mixed, r.mixed2
    bias_rows = PAIR // 3
    identity = lax.broadcasted_iota(jnp.int32, (D, D), 0) == lax.broadcasted_iota(
        jnp.int32, (D, D), 1
    )
    identity = jnp.where(identity, 1.0, 0.0).astype(BF16)
    for index, pairs in enumerate(PAIR_GROUPS):
        plan.now()
        if index == 0:
            r.row_vectors[0 : vec7.shape[-1], :] = dot(
                vec7[...].reshape(D, vec7.shape[-1]), identity, 0, 0
            )
        biases = []
        for pair in pairs:
            place = slice(pair * bias_rows, (pair + 1) * bias_rows)
            biases += [column(0)[place], jnp.zeros((bias_rows, 1), F32), column(1)[place]]
        bias = jnp.concatenate(biases, axis=0)
        for tile in range(tiles):
            both = dot(
                wide[:, pairs[0] * PAIR : (pairs[-1] + 1) * PAIR], tokens[span(tile), :], 0, 1
            )
            both = (both + bias).astype(BF16)
            for place, pair in enumerate(pairs):
                for block, ref in enumerate((q, k, v)):
                    start = place * PAIR + block * bias_rows
                    value = both[start : start + bias_rows]
                    if block == 0:
                        value = (value.astype(F32) * SCORE_SCALE).astype(BF16)
                    ref[2 * pair : 2 * pair + 2, 0:HEAD_DIM, span(tile)] = heads_of(value)
        plan.now()
        heads = (2 * pairs[0], 2 * pairs[-1] + 2)
        attention_forward(
            q,
            k,
            v,
            a,
            r.scores,
            self_ranges,
            heads,
            plan.loop(range(*heads)),
        )

    normed, low, inverse = r.normed, r.low, r.inverse

    def norm_tile(index, tile, before):
        out, unit, rho = normalize(before, row(GAIN + 2 * index), row(GAIN + 2 * index + 1))
        normed[index][span(tile), :] = unit.astype(BF16)
        inverse[span(tile), index : index + 1] = rho
        low[index][span(tile), :] = out.astype(BF16)
        return out

    plan.now()
    for tile in range(tiles):
        before = (
            tokens[span(tile), :].astype(F32) + dot(a[:, span(tile)], wide_column(3), 0, 0) + row(2)
        )
        out = norm_tile(0, tile, before)
        res[span(tile), :] = out
        q2[:, 0:HEAD_DIM, span(tile)] = heads_of(
            scaled(dot(wide_column(4), out.astype(BF16), 0, 1) + column(3))
        )
        plan.now()
    plan.now()
    for tile in range(sources // TILE):
        part = memory[span(tile), :]
        k2[:, 0:HEAD_DIM, span(tile)] = heads_of(dot(wide_column(5), part, 0, 1).astype(BF16))
        v2[:, 0:HEAD_DIM, span(tile)] = heads_of(
            (dot(wide_column(6), part, 0, 1) + column(4)).astype(BF16)
        )
    attention_forward(
        q2,
        k2,
        v2,
        a2,
        cross_scores,
        cross_wide,
        (0, HEADS),
        plan.loop(range(HEADS)),
    )
    active = r.active
    plan.now()
    for tile in range(tiles):
        before = res[span(tile), :] + dot(a2[:, span(tile)], wide_column(7), 0, 0) + row(5)
        out = norm_tile(1, tile, before)
        res[span(tile), :] = out
        for block in range(FF // D):
            if tile == 0 and block == 1:
                plan.now()
            columns = slice(block * D, (block + 1) * D)
            u = dot(out.astype(BF16), wide_column(8 + block), 1, 0) + row(6 + block)
            value, derivative = gelu_pair(u)
            active[span(tile), columns] = value.astype(BF16)
            slope[span(tile), columns] = derivative.astype(BF16)
        plan.now()
    early = range(gather.last - 2)
    gather.finish(early)
    plan.now()
    slot_left = tall.at[pl.ds(FF, D), :]
    slot_right = tall.at[pl.ds(FF + D, D), :]
    for tile in range(tiles):
        before = (
            res[span(tile), :] + dot(active[span(tile), :], tall[0:FF, :], 1, 0) + row(BIAS_OUT)
        )
        norm_tile(2, tile, before)
    low_grad = r.low_grad
    gather.finish(range(len(early), gather.last + 1))

    grad_rows, grad_columns = r.grad_rows, r.grad_columns

    def add_row(index, value):
        grad_rows[index : index + 1, :] += jnp.sum(value, axis=0, keepdims=True)

    def norm_back(index, tile, gradient, bias_row):
        gain = row(GAIN + 2 * index)
        unit = normed[index][span(tile), :].astype(F32)
        scaled_grad = gradient * gain
        inner = jnp.mean(scaled_grad * unit, axis=-1, keepdims=True)
        before = inverse[span(tile), index : index + 1] * (
            scaled_grad - jnp.mean(scaled_grad, axis=-1, keepdims=True) - unit * inner
        )
        add_row(GAIN + 2 * index, gradient * unit)
        add_row(GAIN + 2 * index + 1, gradient)
        add_row(bias_row, before)
        res[span(tile), :] = before
        low_grad[span(tile), :] = before.astype(BF16)

    for tile in range(tiles):
        part = seed[span(tile), :]
        add_row(BIAS_OUT + 1, part.astype(F32))
        gradient = dot(part, slot_left[...], 1, 1) + dot(
            seed_next[span(tile), :], slot_right[...], 1, 1
        )
        norm_back(2, tile, gradient, BIAS_OUT)
    grad_left = dot(low[2][...], seed[...], 0, 0).astype(BF16)
    seed[0:D, :] = slot_left[...]
    slot_left[...] = grad_left
    grad_right = dot(low[2][...], seed_next[...], 0, 0).astype(BF16)
    seed[D : 2 * D, :] = slot_right[...]
    slot_right[...] = grad_right
    for block in range(FF // D):
        columns = slice(block * D, (block + 1) * D)
        for tile in range(tiles):
            grad = dot(low_grad[span(tile), :], tall[columns, :], 1, 1) * slope[
                span(tile), columns
            ].astype(F32)
            add_row(6 + block, grad)
            slope[span(tile), columns] = grad.astype(BF16)
        tall[columns, :] = dot(active[:, columns], low_grad[...], 0, 0).astype(BF16)
    total.start(TALL)
    for tile in range(tiles):
        gradient = res[span(tile), :] + dot(
            slope[span(tile), :], wide[:, 8 * D : 8 * D + FF], 1, 1
        )
        norm_back(1, tile, gradient, 5)
        sum_plan.now()
    for block in range(FF // D):
        columns = slice(block * D, (block + 1) * D)
        wide[:, 8 * D + block * D : 8 * D + (block + 1) * D] = dot(
            low[1][...], slope[:, columns], 0, 0
        ).astype(BF16)
        if block == FF // D - 1:
            total.start(UP)
        sum_plan.now()
    grads = r.mixed_grad

    def mixed_back(weight_index, mixed):
        for tile in range(tiles):
            grad = dot(wide_column(weight_index), low_grad[span(tile), :], 1, 1).astype(BF16)
            grads[:, 0:HEAD_DIM, span(tile)] = heads_of(grad)
            inner = jnp.sum(
                heads_of(grad.astype(F32) * mixed[:, span(tile)].astype(F32)),
                axis=1,
                keepdims=True,
            )
            place = lax.broadcasted_iota(jnp.int32, (HEADS, 16, TILE), 1)
            features = jnp.zeros((HEADS, 16, TILE), F32)
            for step, part in enumerate(split_three(-inner)):
                features = jnp.where(place == step, part, features)
            grads[:, HEAD_DIM:, span(tile)] = features.astype(BF16)
        wide[:, weight_index * D : (weight_index + 1) * D] = dot(
            mixed[...], low_grad[...], 1, 0
        ).astype(BF16)

    mixed_back(7, a2)
    sum_plan.now()
    dq2 = active.at[pl.ds(0, D), pl.ds(0, rows)]
    dk2 = active.at[pl.ds(D, D), pl.ds(0, sources)]
    dv2 = active.at[pl.ds(D, D), pl.ds(rows, sources)]

    def head_rows(ref):
        def of(head):
            return ref.at[pl.ds(pl.multiple_of(head * HEAD_DIM, HEAD_DIM), HEAD_DIM), :]

        return of

    sums = (r.key_sum, r.value_sum)
    attention_backward(
        q2,
        k2,
        v2,
        grads,
        [head_rows(ref) for ref in (dq2, dk2, dv2)],
        sums,
        r.shares,
        r.score_grads,
        cross_ranges,
        sum_plan.loop(range(HEADS)),
    )

    def column_sum(index, value):
        grad_columns[:, index : index + 1] += jnp.sum(value.astype(F32), axis=1, keepdims=True)

    for tile in range(tiles):
        gradient = res[span(tile), :] + dot(dq2[:, span(tile)], wide_column(4), 0, 1)
        norm_back(0, tile, gradient, 2)
        sum_plan.now()
    shift[0:sources, :] = dot(dk2[...], wide_column(5), 0, 1) + dot(dv2[...], wide_column(6), 0, 1)
    memory_copy = pltpu.make_async_copy(
        shift.at[pl.ds(0, sources), :], r.grad_memory, local.at[10]
    )
    memory_copy.start()
    wide[:, 5 * D : 6 * D] = dot(memory[...], dk2[...], 0, 1).astype(BF16)
    wide[:, 6 * D : 7 * D] = dot(memory[...], dv2[...], 0, 1).astype(BF16)
    sum_plan.now()
    wide[:, 4 * D : 5 * D] = dot(low[0][...], dq2[...], 0, 1).astype(BF16)
    column_sum(3, dq2[...])
    column_sum(4, dv2[...])
    mixed_back(3, a)
    total.start(MID)
    sum_plan.now()

    def pair_rows(block):
        def of(head):
            pair = head // 2
            row = pair % 2 * PAIR + block * (PAIR // 3) + head % 2 * HEAD_DIM
            start = pl.multiple_of(pair // 2 * rows, rows)
            return active.at[pl.ds(pl.multiple_of(row, HEAD_DIM), HEAD_DIM), pl.ds(start, rows)]

        return of

    def pair_grad(pair):
        return active[pair % 2 * PAIR : (pair % 2 + 1) * PAIR, pair // 2 * rows : (pair // 2 + 1) * rows]

    def start_pair(pair):
        where = (slice(None),) * net.count + (
            slice(0, own_rows[1]),
            slice(pair * PAIR, (pair + 1) * PAIR),
        )
        slope7[where] = (
            dot(tokens[...], pair_grad(pair), 0, 1)
            .astype(BF16)
            .reshape(slope7.shape[: net.count] + (own_rows[1], PAIR))
        )
        total.start(SELF + pair)

    def start_vectors():
        for pair in range(HEADS // 2):
            place = slice(pair * bias_rows, (pair + 1) * bias_rows)
            grad = pair_grad(pair).astype(F32)
            for index, block in ((0, 0), (1, 2)):
                grad_columns[place, index : index + 1] = jnp.sum(
                    grad[block * bias_rows : (block + 1) * bias_rows], axis=1, keepdims=True
                )
        turned = jnp.transpose(r.grad_rows[...]) + grad_columns[...]
        gvec7[...] = turned.reshape(gvec7.shape)
        total.start(VECTORS)

    hooks = {}
    for head in range(HEADS):
        act = sum_plan.next()

        def hook(head=head, act=act):
            if head % 2 and head < HEADS - 1:
                start_pair(head // 2)
            if act:
                act()

        if act or (head % 2 and head < HEADS - 1):
            hooks[head] = hook
    attention_backward(
        q,
        k,
        v,
        grads,
        [pair_rows(block) for block in range(3)],
        sums,
        r.shares,
        r.score_grads,
        self_ranges,
        hooks,
    )
    start_pair(HEADS // 2 - 1)
    start_vectors()
    sum_plan.now()

    memory_copy.wait()
    shift[rows : rows + 8, :] = jnp.zeros((8, D), F32)
    for tile in range(tiles):
        shift[span(tile), :] = dot(low[2][span(tile), :], seed[D : 2 * D, :], 1, 0)
        sum_plan.now()
    token_copies = []
    for tile in range(tiles):
        low_grad[span(tile), :] = (
            (
                dot(low[2][span(tile), :], seed[0:D, :], 1, 0)
                + follow(tile) * shift[pl.ds(tile * TILE + 1, TILE), :]
                + row(BIAS_OUT + 1)
            )
            * valid(tile)
        ).astype(BF16)
        copy = pltpu.make_async_copy(
            low_grad.at[span(tile), :], r.slots.at[span(tile), :], local.at[6 + tile]
        )
        copy.start()
        token_copies.append(copy)
        sum_plan.now()
    for tile in range(tiles):
        value = res[span(tile), :]
        for side in range(2):
            value = value + dot(
                active[0 : 2 * PAIR, pl.ds(side * rows + tile * TILE, TILE)],
                wide[:, 2 * side * PAIR : 2 * (side + 1) * PAIR],
                0,
                1,
            )
        res[span(tile), :] = value
        copy = pltpu.make_async_copy(
            res.at[span(tile), :], r.grad_tokens.at[span(tile), :], local.at[12 + tile]
        )
        copy.start()
        token_copies.append(copy)
        sum_plan.now()
    sum_plan.now()
    total.finish()
    for copy in token_copies:
        copy.wait()


def finish_kernel(*refs):
    given, results, held = refs[:12], refs[12:21], refs[21:33]
    vec_out, semaphores = refs[33], refs[34]
    loads = [
        pltpu.make_async_copy(source, target, semaphores.at[index])
        for index, (source, target) in enumerate(zip(given, held))
    ]
    for copy in loads:
        copy.start()
    stores = []

    def store(index, source):
        copy = pltpu.make_async_copy(source, results[index], semaphores.at[12 + index])
        copy.start()
        stores.append(copy)

    for index in range(12):
        loads[index].wait()
        if index < 5:
            store(index, held[index])
        elif index == 5:
            vec_out[...] = held[5][:, : vec_out.shape[1]]
            store(5, vec_out)
        elif index >= 9:
            average = held[index - 3]
            average[...] += (held[index][...].astype(F32) - average[...]) / AVG_STEPS
            store(index - 3, average)
    for copy in stores:
        copy.wait()


def fused_body(
    wide_size,
    narrow_size,
    tokens,
    memory,
    w_wide,
    w_tall,
    vecs,
    avg_wide,
    avg_tall,
    avg_vecs,
    tgt_lengths,
    src_lengths,
    cotangent,
):
    count = (wide_size * narrow_size).bit_length() - 1
    rows, sources = tokens.shape[0], memory.shape[0]
    wide_rows, wide_columns = w_wide.shape
    tall_rows = w_tall.shape[0]
    vec_rows = vecs.shape[0]
    bits = (2,) * count
    hbm = pl.BlockSpec(memory_space=pl.ANY)
    smem = pl.BlockSpec(memory_space=pltpu.SMEM)
    inputs = dict(
        tgt_lengths=tgt_lengths,
        src_lengths=src_lengths,
        tokens_in=tokens,
        memory_in=memory,
        cotangent=cotangent,
        w_wide=w_wide,
        w_tall=w_tall,
        vecs=vecs,
    )
    outputs = dict(
        slots=jax.ShapeDtypeStruct((rows, D), BF16),
        grad_tokens=jax.ShapeDtypeStruct((rows, D), F32),
        grad_memory=jax.ShapeDtypeStruct((sources, D), F32),
        grad_wide=jax.ShapeDtypeStruct((wide_rows, wide_columns), F32),
        grad_tall=jax.ShapeDtypeStruct((tall_rows, D), F32),
        grad_vecs=jax.ShapeDtypeStruct((vec_rows, 128), F32),
    )

    def arrivals(shape, dtype=BF16):
        line = (1 << (count - 3)) - 1
        far = bits[3:]
        return [
            pltpu.VMEM(lead + shape, dtype) for lead in (bits[1:], far, far, far, (line,))
        ]

    scratch = dict(
        wide=pltpu.VMEM(bits + (wide_rows, wide_columns), BF16),
        tall=pltpu.VMEM(bits + (tall_rows, D), BF16),
        vec=pltpu.VMEM(bits + vecs.shape, BF16),
        grad_vec=pltpu.VMEM(bits + (vec_rows, 128), F32),
        tokens=pltpu.VMEM((rows, D), BF16),
        memory=pltpu.VMEM((sources, D), BF16),
        seed=pltpu.VMEM((rows, D), BF16),
        seed_next=pltpu.VMEM((rows, D), BF16),
        q=pltpu.VMEM((HEADS, AUG, rows), BF16),
        k=pltpu.VMEM((HEADS, AUG, rows), BF16),
        v=pltpu.VMEM((HEADS, AUG, rows), BF16),
        q2=pltpu.VMEM((HEADS, AUG, rows), BF16),
        k2=pltpu.VMEM((HEADS, AUG, sources), BF16),
        v2=pltpu.VMEM((HEADS, AUG, sources), BF16),
        mixed_grad=pltpu.VMEM((HEADS, AUG, rows), BF16),
        mixed=pltpu.VMEM((D, rows), BF16),
        mixed2=pltpu.VMEM((D, rows), BF16),
        active=pltpu.VMEM((rows, FF), BF16),
        slope=pltpu.VMEM(bits + (rows >> count, FF), BF16),
        res=pltpu.VMEM((rows, D), F32),
        low_grad=pltpu.VMEM((rows, D), BF16),
        shift=pltpu.VMEM((rows + 8, D), F32),
        key_sum=pltpu.VMEM((HEAD_DIM, rows), F32),
        value_sum=pltpu.VMEM((HEAD_DIM, rows), F32),
        inverse=pltpu.VMEM((rows, 128), F32),
        row_vectors=pltpu.VMEM((24, D), F32),
        grad_rows=pltpu.VMEM((128, D), F32),
        grad_columns=pltpu.VMEM((D, 128), F32),
        out_wide=pltpu.VMEM((wide_rows, wide_columns), F32),
        out_tall=pltpu.VMEM((tall_rows, D), F32),
        out_vec=pltpu.VMEM((vec_rows, 128), F32),
        normed=[pltpu.VMEM((rows, D), BF16) for _ in range(3)],
        low=[pltpu.VMEM((rows, D), BF16) for _ in range(3)],
        scores=[
            pltpu.VMEM((max(high - low for low, high in bands(rows, rows, 512)), TILE), F32)
            for _ in range(2)
        ],
        shares=[pltpu.VMEM((TILE, rows), BF16) for _ in range(2)],
        score_grads=[pltpu.VMEM((TILE, rows), BF16) for _ in range(2)],
        in_tall=arrivals((tall_rows, D)),
        in_up=arrivals((wide_rows, FF)),
        in_mid=arrivals((wide_rows, 5 * D)),
        in_self=[arrivals((wide_rows, PAIR)) for _ in range(HEADS // 2)],
        in_vec=arrivals((vec_rows, 128), F32),
        local=pltpu.SemaphoreType.DMA((20,)),
        own_done=pltpu.SemaphoreType.DMA((3 * HEADS // 2 + 1,)),
        out_done=pltpu.SemaphoreType.DMA((OUT_SEMAPHORES,)),
        gather_send=pltpu.SemaphoreType.DMA((7 + TALL_CUT, 3 + (1 << (count - 3)), 2)),
        gather_receive=pltpu.SemaphoreType.DMA((7 + TALL_CUT, 3 + (1 << (count - 3)), 2)),
        sum_send=pltpu.SemaphoreType.DMA((4 + HEADS // 2, 3 + (1 << (count - 3)), 1)),
        sum_receive=pltpu.SemaphoreType.DMA((4 + HEADS // 2, 3 + (1 << (count - 3)), 1)),
    )
    scratch_leaves, scratch_tree = jax.tree.flatten(scratch)
    input_leaves, output_leaves = list(inputs.values()), list(outputs.values())
    names = list(inputs) + list(outputs)
    spec = [smem if value.dtype == jnp.int32 else hbm for value in input_leaves]

    def kernel(*refs):
        held = dict(zip(names, refs))
        held.update(jax.tree.unflatten(scratch_tree, refs[len(names) :]))
        layer_kernel(types.SimpleNamespace(**held), wide_size, narrow_size)

    slots, grad_tokens, grad_memory, grad_wide, grad_tall, grad_vecs = pl.pallas_call(
        kernel,
        out_shape=output_leaves,
        in_specs=spec,
        out_specs=[hbm] * len(outputs),
        scratch_shapes=scratch_leaves,
        compiler_params=pltpu.CompilerParams(
            collective_id=0, has_side_effects=True, vmem_limit_bytes=67_000_000
        ),
    )(*input_leaves)
    done = [slots, grad_tokens, grad_memory, grad_wide, grad_tall, grad_vecs]
    done += [avg_wide, avg_tall, avg_vecs, w_wide, w_tall, vecs]
    shapes = outputs | dict(grad_vecs=jax.ShapeDtypeStruct(vecs.shape, F32))
    return pl.pallas_call(
        finish_kernel,
        out_shape=list(shapes.values())
        + [jax.ShapeDtypeStruct(value.shape, F32) for value in (avg_wide, avg_tall, avg_vecs)],
        in_specs=[hbm] * len(done),
        out_specs=[hbm] * 9,
        scratch_shapes=[pltpu.VMEM(value.shape, value.dtype) for value in done]
        + [pltpu.VMEM(vecs.shape, F32), pltpu.SemaphoreType.DMA((21,))],
    )(*done)


def solution(mesh):
    in_specs = (
        P(("wide", "narrow"), None),
        P(("wide", "narrow"), None),
        P(("wide", "narrow"), None),
        P(("wide", "narrow"), None),
        P(("wide", "narrow"), None),
        P(("wide", "narrow"), None),
        P(("wide", "narrow"), None),
        P(("wide", "narrow"), None),
        P(("wide", "narrow"), None),
        P(("wide", "narrow"), None),
        P(("wide", "narrow"), None),
    )
    out_specs = (
        P(("wide", "narrow"), None),
        P(("wide", "narrow"), None),
        P(("wide", "narrow"), None),
        P(("wide", "narrow"), None),
        P(("wide", "narrow"), None),
        P(("wide", "narrow"), None),
        P(("wide", "narrow"), None),
        P(("wide", "narrow"), None),
        P(("wide", "narrow"), None),
    )
    devices = mesh.shape["wide"] * mesh.shape["narrow"]
    bits = devices.bit_length() - 1

    def body(*args):
        if args[2].shape[0] % 16 or args[3].shape[0] % 16 or devices != 1 << bits or bits < 3:
            return plain_body(*args)
        return fused_body(mesh.shape["wide"], mesh.shape["narrow"], *args)

    return jax.shard_map(body, mesh=mesh, in_specs=in_specs, out_specs=out_specs, check_vma=False)
```

```python
import types

import jax
import jax.numpy as jnp
from jax import lax
from jax.experimental import pallas as pl
from jax.experimental.pallas import tpu as pltpu
from jax.sharding import PartitionSpec as P

D = 512
HEADS = 8
HEAD_DIM = 64
FF = 2048
SEGS = 6
AVG_STEPS = 4


SCORE_SCALE = 0.125
EPSILON = 1e-05
MASKED = -1e30


def matmul(left, right):
    return jnp.dot(left, right, preferred_element_type=jnp.float32)


def matmul_first(left, right):
    return lax.dot_general(
        left, right, (((0,), (0,)), ((), ())), preferred_element_type=jnp.float32
    )


def matmul_last(left, right):
    return lax.dot_general(
        left, right, (((1,), (1,)), ((), ())), preferred_element_type=jnp.float32
    )


def segment_numbers(lengths, count):
    endings = jnp.cumsum(lengths)
    places = jnp.arange(count, dtype=jnp.int32)
    return jnp.sum((places[:, None] >= endings[None, :]).astype(jnp.int32), axis=1)


def norm_forward(before, norm_gain, norm_shift):
    centred = before - jnp.mean(before, axis=-1, keepdims=True)
    inverse = lax.rsqrt(jnp.mean(centred * centred, axis=-1, keepdims=True) + EPSILON)
    normed = centred * inverse
    return (normed * norm_gain + norm_shift, normed, inverse)


def norm_backward(gradient, normed, inverse, norm_gain):
    scaled = gradient * norm_gain
    inner_sum = jnp.mean(scaled * normed, axis=-1, keepdims=True)
    before_grad = inverse * (scaled - jnp.mean(scaled, axis=-1, keepdims=True) - normed * inner_sum)
    return (before_grad, jnp.sum(gradient * normed, axis=0), jnp.sum(gradient, axis=0))


def split_heads(matrix):
    return matrix.reshape(matrix.shape[0], HEADS, HEAD_DIM)


def masked_scores(query_block, key_heads, segment_block, key_segment):
    scores = (
        jnp.einsum(
            "qhe,khe->hqk", split_heads(query_block), key_heads, preferred_element_type=jnp.float32
        )
        * SCORE_SCALE
    )
    allowed = segment_block[:, None] == key_segment[None, :]
    return jnp.where(allowed[None], scores, MASKED)


def attend_forward(queries, keys_in, values_in, query_segment, key_segment):
    row_count = queries.shape[0]
    block_rows = min(512, row_count)
    blocks = row_count // block_rows
    key_heads = split_heads(keys_in)
    value_heads = split_heads(values_in)

    def attend_block(pieces):
        query_block, segment_block = pieces
        scores = masked_scores(query_block, key_heads, segment_block, key_segment)
        highest = jnp.max(scores, axis=-1, keepdims=True)
        exponent = jnp.exp(scores - highest)
        totals = jnp.sum(exponent, axis=-1, keepdims=True)
        shares = (exponent / totals).astype(jnp.bfloat16)
        mixed = jnp.einsum("hqk,khe->qhe", shares, value_heads, preferred_element_type=jnp.float32)
        return (
            mixed.reshape(block_rows, HEADS * HEAD_DIM).astype(jnp.bfloat16),
            (highest + jnp.log(totals))[..., 0],
        )

    mixed, logsum = lax.map(
        attend_block,
        (queries.reshape(blocks, block_rows, -1), query_segment.reshape(blocks, block_rows)),
    )
    return (mixed.reshape(row_count, -1), logsum)


def attend_backward(queries, keys_in, values_in, mixed_grad, logsum, query_segment, key_segment):
    row_count = queries.shape[0]
    block_rows = min(512, row_count)
    blocks = row_count // block_rows
    key_heads = split_heads(keys_in)
    value_heads = split_heads(values_in)

    def backward_block(carried, pieces):
        key_sum, value_sum = carried
        query_block, grad_block, logsum_block, segment_block = pieces
        scores = masked_scores(query_block, key_heads, segment_block, key_segment)
        shares = jnp.exp(scores - logsum_block[..., None])
        grad_heads = split_heads(grad_block)
        share_grad = jnp.einsum(
            "qhe,khe->hqk", grad_heads, value_heads, preferred_element_type=jnp.float32
        )
        inner_sum = jnp.sum(shares * share_grad, axis=-1, keepdims=True)
        score_grad = (shares * (share_grad - inner_sum)).astype(jnp.bfloat16)
        query_grad = (
            jnp.einsum("hqk,khe->qhe", score_grad, key_heads, preferred_element_type=jnp.float32)
            * SCORE_SCALE
        )
        key_sum = (
            key_sum
            + jnp.einsum(
                "hqk,qhe->khe",
                score_grad,
                split_heads(query_block),
                preferred_element_type=jnp.float32,
            )
            * SCORE_SCALE
        )
        value_sum = value_sum + jnp.einsum(
            "hqk,qhe->khe",
            shares.astype(jnp.bfloat16),
            grad_heads,
            preferred_element_type=jnp.float32,
        )
        return ((key_sum, value_sum), query_grad.reshape(block_rows, HEADS * HEAD_DIM))

    zeros_init = jnp.zeros((keys_in.shape[0], HEADS, HEAD_DIM), jnp.float32)
    pieces = (
        queries.reshape(blocks, block_rows, -1),
        mixed_grad.reshape(blocks, block_rows, -1),
        logsum,
        query_segment.reshape(blocks, block_rows),
    )
    (key_sum, value_sum), query_grad = lax.scan(backward_block, (zeros_init, zeros_init), pieces)
    return (
        query_grad.reshape(row_count, -1),
        key_sum.reshape(keys_in.shape[0], -1),
        value_sum.reshape(values_in.shape[0], -1),
    )


def plain_body(
    tokens,
    memory,
    w_wide,
    w_tall,
    vecs,
    avg_wide,
    avg_tall,
    avg_vecs,
    tgt_lengths,
    src_lengths,
    cotangent,
):
    wide_all, tall_all, vector_all = (
        lax.all_gather(w_wide, ("wide", "narrow"), axis=0, tiled=True),
        lax.all_gather(w_tall, ("wide", "narrow"), axis=0, tiled=True),
        lax.all_gather(vecs, ("wide", "narrow"), axis=0, tiled=True),
    )
    vectors = vector_all.astype(jnp.float32)
    spread = FF // D
    offset = 6 + spread
    columns = [wide_all[:, index * D : (index + 1) * D] for index in range(8)]
    target_query, target_key, target_value, target_output = (
        columns[0],
        columns[1],
        columns[2],
        columns[3],
    )
    source_query, source_key, source_value, source_output = (
        columns[4],
        columns[5],
        columns[6],
        columns[7],
    )
    up_weight = wide_all[:, 8 * D :]
    down_weight = tall_all[:FF]
    slot_left = tall_all[FF : FF + D]
    slot_right = tall_all[FF + D :]
    up_bias = vectors[:, 6:offset].T.reshape(FF)
    row_count = tokens.shape[0]
    target_segment = segment_numbers(tgt_lengths[0], row_count)
    source_segment = segment_numbers(src_lengths[0], memory.shape[0])
    valid_rows = (target_segment < SEGS - 1).astype(jnp.float32)[:, None]
    follow = (
        jnp.concatenate([target_segment[1:], jnp.full((1,), -1, jnp.int32)]) == target_segment
    ).astype(jnp.float32)[:, None]
    queries_self = (matmul(tokens, target_query) + vectors[:, 0]).astype(jnp.bfloat16)
    keys_self = matmul(tokens, target_key).astype(jnp.bfloat16)
    values_self = (matmul(tokens, target_value) + vectors[:, 1]).astype(jnp.bfloat16)
    mixed_self, logsum_self = attend_forward(
        queries_self, keys_self, values_self, target_segment, target_segment
    )
    first, normed_first, inverse_first = norm_forward(
        tokens.astype(jnp.float32) + matmul(mixed_self, target_output) + vectors[:, 2],
        vectors[:, offset + 2],
        vectors[:, offset + 3],
    )
    first_low = first.astype(jnp.bfloat16)
    queries_cross = (matmul(first_low, source_query) + vectors[:, 3]).astype(jnp.bfloat16)
    keys_cross = matmul(memory, source_key).astype(jnp.bfloat16)
    values_cross = (matmul(memory, source_value) + vectors[:, 4]).astype(jnp.bfloat16)
    mixed_cross, logsum_cross = attend_forward(
        queries_cross, keys_cross, values_cross, target_segment, source_segment
    )
    second, normed_second, inverse_second = norm_forward(
        first + matmul(mixed_cross, source_output) + vectors[:, 5],
        vectors[:, offset + 4],
        vectors[:, offset + 5],
    )
    second_low = second.astype(jnp.bfloat16)
    hidden = matmul(second_low, up_weight) + up_bias
    active = jax.nn.gelu(hidden).astype(jnp.bfloat16)
    third, normed_third, inverse_third = norm_forward(
        second + matmul(active, down_weight) + vectors[:, offset],
        vectors[:, offset + 6],
        vectors[:, offset + 7],
    )
    third_low = third.astype(jnp.bfloat16)
    right_half = jnp.concatenate([third_low[1:], jnp.zeros((1, D), jnp.bfloat16)]) * follow.astype(
        jnp.bfloat16
    )
    slots = (
        (matmul(third_low, slot_left) + matmul(right_half, slot_right) + vectors[:, offset + 1])
        * valid_rows
    ).astype(jnp.bfloat16)
    seed_grad = cotangent * valid_rows.astype(jnp.bfloat16)
    grad_slot_bias = jnp.sum(seed_grad.astype(jnp.float32), axis=0)
    grad_left = matmul_first(third_low, seed_grad)
    grad_right = matmul_first(right_half, seed_grad)
    right_back = matmul_last(seed_grad, slot_right) * follow
    grad_third = matmul_last(seed_grad, slot_left) + jnp.concatenate(
        [jnp.zeros((1, D), jnp.float32), right_back[:-1]]
    )
    grad_pre_third, grad_gain_third, grad_shift_third = norm_backward(
        grad_third, normed_third, inverse_third, vectors[:, offset + 6]
    )
    pre_third_low = grad_pre_third.astype(jnp.bfloat16)
    grad_down = matmul_first(active, pre_third_low)
    grad_tall_all = jnp.concatenate([grad_down, grad_left, grad_right], axis=0)
    gelu_value, gelu_pull = jax.vjp(jax.nn.gelu, hidden)
    grad_hidden = gelu_pull(matmul_last(pre_third_low, down_weight))[0]
    hidden_low = grad_hidden.astype(jnp.bfloat16)
    grad_up = matmul_first(second_low, hidden_low)
    grad_second = grad_pre_third + matmul_last(hidden_low, up_weight)
    grad_pre_second, grad_gain_second, grad_shift_second = norm_backward(
        grad_second, normed_second, inverse_second, vectors[:, offset + 4]
    )
    pre_second_low = grad_pre_second.astype(jnp.bfloat16)
    grad_source_output = matmul_first(mixed_cross, pre_second_low)
    mixed_cross_grad = matmul_last(pre_second_low, source_output).astype(jnp.bfloat16)
    cross_query_grad, cross_key_grad, cross_value_grad = attend_backward(
        queries_cross,
        keys_cross,
        values_cross,
        mixed_cross_grad,
        logsum_cross,
        target_segment,
        source_segment,
    )
    cross_query_low = cross_query_grad.astype(jnp.bfloat16)
    cross_key_low = cross_key_grad.astype(jnp.bfloat16)
    cross_value_low = cross_value_grad.astype(jnp.bfloat16)
    grad_source_query = matmul_first(first_low, cross_query_low)
    grad_source_key = matmul_first(memory, cross_key_low)
    grad_source_value = matmul_first(memory, cross_value_low)
    grad_memory = matmul_last(cross_key_low, source_key) + matmul_last(
        cross_value_low, source_value
    )
    grad_first = grad_pre_second + matmul_last(cross_query_low, source_query)
    grad_pre_first, grad_gain_first, grad_shift_first = norm_backward(
        grad_first, normed_first, inverse_first, vectors[:, offset + 2]
    )
    pre_first_low = grad_pre_first.astype(jnp.bfloat16)
    grad_target_output = matmul_first(mixed_self, pre_first_low)
    mixed_self_grad = matmul_last(pre_first_low, target_output).astype(jnp.bfloat16)
    self_query_grad, self_key_grad, self_value_grad = attend_backward(
        queries_self,
        keys_self,
        values_self,
        mixed_self_grad,
        logsum_self,
        target_segment,
        target_segment,
    )
    self_query_low = self_query_grad.astype(jnp.bfloat16)
    self_key_low = self_key_grad.astype(jnp.bfloat16)
    self_value_low = self_value_grad.astype(jnp.bfloat16)
    grad_target_query = matmul_first(tokens, self_query_low)
    grad_target_key = matmul_first(tokens, self_key_low)
    grad_target_value = matmul_first(tokens, self_value_low)
    grad_tokens = (
        grad_pre_first
        + matmul_last(self_query_low, target_query)
        + matmul_last(self_key_low, target_key)
        + matmul_last(self_value_low, target_value)
    )
    grad_wide_all = jnp.concatenate(
        [
            grad_target_query,
            grad_target_key,
            grad_target_value,
            grad_target_output,
            grad_source_query,
            grad_source_key,
            grad_source_value,
            grad_source_output,
            grad_up,
        ],
        axis=1,
    )
    bias_front = jnp.stack(
        [
            jnp.sum(self_query_grad, axis=0),
            jnp.sum(self_value_grad, axis=0),
            jnp.sum(grad_pre_first, axis=0),
            jnp.sum(cross_query_grad, axis=0),
            jnp.sum(cross_value_grad, axis=0),
            jnp.sum(grad_pre_second, axis=0),
        ],
        axis=1,
    )
    bias_middle = jnp.sum(grad_hidden, axis=0).reshape(spread, D).T
    bias_back = jnp.stack(
        [
            jnp.sum(grad_pre_third, axis=0),
            grad_slot_bias,
            grad_gain_first,
            grad_shift_first,
            grad_gain_second,
            grad_shift_second,
            grad_gain_third,
            grad_shift_third,
        ],
        axis=1,
    )
    grad_vector_all = jnp.concatenate([bias_front, bias_middle, bias_back], axis=1)
    grad_wide, grad_tall, grad_vecs = (
        lax.psum_scatter(grad_wide_all, ("wide", "narrow"), scatter_dimension=0, tiled=True),
        lax.psum_scatter(grad_tall_all, ("wide", "narrow"), scatter_dimension=0, tiled=True),
        lax.psum_scatter(grad_vector_all, ("wide", "narrow"), scatter_dimension=0, tiled=True),
    )
    new_avg_wide = avg_wide + (w_wide.astype(jnp.float32) - avg_wide) / AVG_STEPS
    new_avg_tall = avg_tall + (w_tall.astype(jnp.float32) - avg_tall) / AVG_STEPS
    new_avg_vecs = avg_vecs + (vecs.astype(jnp.float32) - avg_vecs) / AVG_STEPS
    return (
        slots,
        grad_tokens,
        grad_memory,
        grad_wide,
        grad_tall,
        grad_vecs,
        new_avg_wide,
        new_avg_tall,
        new_avg_vecs,
    )


BF16 = jnp.bfloat16
F32 = jnp.float32
AUG = 80
BIG = 1e30
TILE = 256
MESH_IDS = pl.DeviceIdType.MESH
BIAS_OUT, GAIN = 10, 12
TALL_CUT = 3
OUT_SEMAPHORES = 24
PAIR = 6 * HEAD_DIM
PAIR_GROUPS = ((0,), (1,), (2, 3))
GATHER_STEPS = {
    0: ((0, 0),),
    1: ((1, 0), (0, 2), (1, 1), (2, 0), (0, 3),),
    2: ((9, 0),),
    4: ((3, 0),),
    5: ((1, 2), (2, 1), (1, 3),),
    7: ((4, 0),),
    9: ((3, 1), (5, 0), (2, 2), (2, 3),),
    11: ((4, 1),),
    12: ((6, 0), (9, 1), (3, 2),),
    13: ((5, 1), (7, 0),),
    14: ((3, 3),),
    16: ((4, 2),),
    19: ((6, 1),),
    20: ((4, 3),),
    21: ((8, 0),),
    23: ((5, 2),),
    25: ((7, 1),),
    26: ((5, 3),),
    28: ((6, 2),),
    30: ((8, 1), (6, 3),),
    32: ((9, 2),),
    33: ((7, 2),),
    35: ((9, 3), (8, 2), (7, 3), (8, 3),),
}
SUM_STEPS = {
    5: ((0, 0),),
    10: ((1, 0),),
    12: ((0, 1),),
    20: ((1, 1),),
    24: ((2, 0), (0, 2),),
    25: ((3, 0), (1, 2),),
    27: ((4, 0), (2, 1),),
    29: ((3, 1), (5, 0),),
    30: ((4, 1), (0, 3),),
    37: ((2, 2), (6, 0),),
    38: ((7, 0), (3, 2),),
    39: ((5, 1),),
    40: ((1, 3), (4, 2),),
    44: ((6, 1), (7, 1), (5, 2), (6, 2), (7, 2), (2, 3), (3, 3), (4, 3), (5, 3), (6, 3), (7, 3),),
}


def dot(left, right, left_dim, right_dim):
    return lax.dot_general(
        left, right, (((left_dim,), (right_dim,)), ((), ())), preferred_element_type=F32
    )


def bands(query_rows, key_rows, longest, tile=TILE):
    found = []
    for start in range(0, query_rows, tile):
        if longest is None:
            found.append((0, key_rows))
            continue
        low = max(0, (start - longest + 1) // TILE * TILE)
        high = min(key_rows, -(-(start + TILE + longest - 1) // TILE) * TILE)
        found.append((low, high))
    return found


def column_max(scores):
    rows, columns = scores.shape
    return jnp.max(
        jnp.max(scores.reshape(rows // 64, 64, columns), axis=0), axis=0, keepdims=True
    )


def split_three(value):
    high = value.astype(BF16).astype(F32)
    middle = (value - high).astype(BF16).astype(F32)
    low = (value - high - middle).astype(BF16).astype(F32)
    return high, middle, low


def feature_rows(base, first, parts):
    place = lax.broadcasted_iota(jnp.int32, base.shape, 0)
    for step, part in enumerate(parts):
        base = jnp.where(place == first + step, part, base)
    return base


def gelu_pair(u):
    scale = 0.7978845608028654
    inner = jnp.tanh(scale * (u + 0.044715 * (u * u * u)))
    half = 0.5 * (1.0 + inner)
    slope = half + 0.5 * u * (1.0 - inner * inner) * (scale * (1.0 + 3 * 0.044715 * (u * u)))
    return u * half, slope


def normalize(before, gain, shift):
    centred = before - jnp.mean(before, axis=-1, keepdims=True)
    inverse = lax.rsqrt(jnp.mean(centred * centred, axis=-1, keepdims=True) + EPSILON)
    normed = centred * inverse
    return normed * gain + shift, normed, inverse


def by_pair(hooks):
    found = {}
    for head, act in hooks.items():
        found.setdefault(head // 2, []).append(act)

    def together(acts):
        def act():
            for one in acts:
                one()

        return act

    return {pair: together(acts) for pair, acts in found.items()}


def attention_forward(queries, keys, values, mixed, scores, ranges, heads, hooks):
    tiles = len(ranges)
    width = queries.shape[2] // tiles

    def put(head, tile):
        low, high = ranges[tile]
        scores[tile % 2][0 : high - low, :] = dot(
            keys[head, :, low:high], queries[head, :, tile * width : (tile + 1) * width], 0, 0
        )

    put(heads[0], 0)

    def one_head(head):
        for tile, (low, high) in enumerate(ranges):
            if tile + 1 < tiles:
                put(head, tile + 1)
            else:
                put(jnp.minimum(head + 1, heads[1] - 1), 0)
            span = slice(tile * width, (tile + 1) * width)
            current = scores[tile % 2][0 : high - low, :]
            highest = column_max(current)
            shares = jnp.exp(current - highest).astype(BF16)
            gathered = dot(values[head, :, low:high], shares, 1, 0)
            total = gathered[HEAD_DIM : HEAD_DIM + 1]
            rows = pl.ds(pl.multiple_of(head * HEAD_DIM, HEAD_DIM), HEAD_DIM)
            mixed[rows, span] = (gathered[:HEAD_DIM] * (1.0 / total)).astype(BF16)
            queries[head, HEAD_DIM:, span] = feature_rows(
                queries[head, HEAD_DIM:, span].astype(F32),
                SEGS,
                split_three(-(highest + jnp.log(total))),
            ).astype(BF16)

    def one_pair(pair, carried):
        one_head(2 * pair)
        one_head(2 * pair + 1)
        for at, hook in by_pair(hooks).items():
            pl.when(pair == at)(hook)
        return carried

    lax.fori_loop(heads[0] // 2, heads[1] // 2, one_pair, 0)


def attention_backward(queries, keys, values, grads, outs, sums, shares, score_grads, ranges, hooks):
    key_rows = keys.shape[2]
    key_sum, value_sum = sums
    tiles = len(ranges)

    def put(head, tile):
        low, high = ranges[tile]
        span = slice(tile * TILE, (tile + 1) * TILE)
        share = jnp.exp(dot(queries[head, :, span], keys[head, :, low:high], 0, 0))
        share_grad = dot(grads[head, :, span], values[head, :, low:high], 0, 0)
        shares[tile % 2][:, 0 : high - low] = share.astype(BF16)
        score_grads[tile % 2][:, 0 : high - low] = (share * share_grad).astype(BF16)

    put(0, 0)

    def one_head(head):
        key_sum[:, 0:key_rows] = jnp.zeros((HEAD_DIM, key_rows), F32)
        value_sum[:, 0:key_rows] = jnp.zeros((HEAD_DIM, key_rows), F32)
        query_out, key_out, value_out = [out(head) for out in outs]
        for tile, (low, high) in enumerate(ranges):
            if tile + 1 < tiles:
                put(head, tile + 1)
            else:
                put(jnp.minimum(head + 1, HEADS - 1), 0)
            span = slice(tile * TILE, (tile + 1) * TILE)
            share = shares[tile % 2][:, 0 : high - low]
            score_grad = score_grads[tile % 2][:, 0 : high - low]
            query_out[:, span] = (
                dot(keys[head, 0:HEAD_DIM, low:high], score_grad, 1, 1) * SCORE_SCALE
            ).astype(BF16)
            key_sum[:, low:high] += dot(queries[head, 0:HEAD_DIM, span], score_grad, 1, 0)
            value_sum[:, low:high] += dot(grads[head, 0:HEAD_DIM, span], share, 1, 0)
        key_out[...] = key_sum[:, 0:key_rows].astype(BF16)
        value_out[...] = value_sum[:, 0:key_rows].astype(BF16)

    def one_pair(pair, carried):
        one_head(2 * pair)
        one_head(2 * pair + 1)
        for at, hook in by_pair(hooks).items():
            pl.when(pair == at)(hook)
        return carried

    lax.fori_loop(0, HEADS // 2, one_pair, 0)


class Exchange:
    def __init__(self, wide, narrow):
        self.narrow_bits = narrow.bit_length() - 1
        self.count = (wide * narrow).bit_length() - 1
        self.line = 1 << (self.count - 3)
        self.place = (lax.axis_index("wide"), lax.axis_index("narrow"))
        number = self.place[0] * narrow + self.place[1]
        self.bits = [(number >> bit) & 1 for bit in range(self.count)]
        self.own = tuple(self.bits[bit] for bit in reversed(range(self.count)))
        self.far = list(range(3, self.count))
        self.masks = [1, 2, 4, 6] + [other << 3 for other in range(1, self.line)]
        core = self.bits[0]
        self.first, self.second, self.both = {1: 1 - core, 2: core}, {1: core, 2: 1 - core}, {1: 1, 2: 1}

    def device(self, mask):
        wide, narrow = self.place
        return (wide ^ (mask >> self.narrow_bits), narrow ^ (mask & ((1 << self.narrow_bits) - 1)))

    def greet(self):
        barrier = pltpu.get_barrier_semaphore()
        for mask in self.masks:
            pl.semaphore_signal(
                barrier, inc=1, device_id=self.device(mask), device_id_type=MESH_IDS
            )

    def meet(self):
        pl.semaphore_wait(pltpu.get_barrier_semaphore(), len(self.masks))

    def neighbour(self, second):
        core = self.bits[0]
        take = core if not second else 1 - core
        one, other = self.device(2), self.device(4)
        return tuple(a + (b - a) * take for a, b in zip(one, other))

    def view(self, part, open_bits, flips=None):
        index = tuple(
            slice(None) if bit in open_bits else self.turned(bit, flips)
            for bit in reversed(range(self.count))
        )
        return part.ref.at[index + part.where]

    def turned(self, bit, flips):
        flip = (flips or {}).get(bit, 0)
        return self.bits[bit] + flip - 2 * self.bits[bit] * flip


class Part:
    def __init__(self, ref, rows=None, columns=None, buffers=(), outs=()):
        cut = lambda ends: slice(None) if ends is None else pl.ds(ends[0], ends[1] - ends[0])
        self.ref, self.where, self.buffers, self.outs = ref, (cut(rows), cut(columns)), buffers, outs


class Transfer:
    def __init__(self, net, pieces, send, receive):
        self.net, self.pieces, self.send, self.receive = net, pieces, send, receive
        self.line = tuple(range(4, 3 + net.line))

    def copy(self, piece, part, slot, source, target, device):
        return pltpu.make_async_remote_copy(
            source,
            target,
            self.send.at[piece, slot, part],
            self.receive.at[piece, slot, part],
            device_id=device,
            device_id_type=MESH_IDS,
        )

    def each(self, piece, stage, act):
        for number in range(len(self.pieces[piece])):
            for slot in self.slots(piece, stage):
                act(self.one(piece, number, slot))

    def begin(self, piece, slot):
        for number in range(len(self.pieces[piece])):
            self.one(piece, number, slot).start()

    def finish(self, pieces=None):
        for piece in range(len(self.pieces)) if pieces is None else pieces:
            for stage in range(4):
                self.each(piece, stage, lambda copy: copy.wait_send())


class Gather(Transfer):
    def __init__(self, net, pieces, send, receive):
        super().__init__(net, pieces, send, receive)
        self.last = len(pieces) - 1

    def slots(self, piece, stage):
        if piece == 0:
            return (self.line, (), (0, 1, 2), (3,))[stage]
        if piece == self.last:
            return ((0, 1), (2,), self.line, (3,))[stage]
        return (self.line, (0,), (1, 2), (3,))[stage]

    def one(self, piece, number, slot):
        net, part = self.net, self.pieces[piece][number]
        lines = [] if piece == self.last else net.far
        if slot == 3:
            view, device = net.view(part, net.far + [1, 2]), net.device(1)
        elif slot > 3:
            near = [1, 2] if piece == self.last else []
            view, device = net.view(part, near), net.device((slot - 3) << 3)
        elif slot == 2 and piece == 0:
            view, device = net.view(part, lines), net.device(6)
        else:
            view = net.view(part, lines, net.first if slot == 2 else None)
            device = net.neighbour(slot > 0)
        return self.copy(piece, number, slot, view, view, device)

    def start(self, piece):
        if piece == self.last:
            self.begin(piece, 0)
            self.begin(piece, 1)
        else:
            self.each(piece, 0, lambda copy: copy.start())

    def step(self, piece, stage):
        self.each(piece, stage, lambda copy: copy.wait_recv())
        if piece == self.last and stage < 2:
            self.each(piece, stage + 1, lambda copy: copy.start())
        elif stage == 0:
            self.begin(piece, 0)
            self.begin(piece, 1)
            if piece == 0:
                self.begin(0, 2)
                self.start(1)
            if piece + 2 < self.last:
                self.start(piece + 2)
        elif stage == 1 and piece:
            self.begin(piece, 2)
        elif stage == 2:
            self.begin(piece, 3)


class Sum(Transfer):
    def slots(self, piece, stage):
        return ((0,), (1,), (2, 3), self.line)[stage]

    def one(self, piece, number, slot):
        net, part = self.net, self.pieces[piece][number]
        if slot == 0:
            view, device = net.view(part, net.far + [1, 2], {0: 1}), net.device(1)
        elif slot > 3:
            mask = (slot - 3) << 3
            view, device = net.view(part, [], {bit: mask >> bit & 1 for bit in net.far}), net.device(mask)
        else:
            view = net.view(part, net.far, (None, net.both, net.second, net.first)[slot])
            device = net.neighbour(slot < 3)
        target = part.buffers[4].at[slot - 4] if slot > 3 else part.buffers[slot]
        return self.copy(piece, number, slot, view, target, device)

    def start(self, piece):
        self.begin(piece, 0)

    def add(self, piece, stage):
        net = self.net
        if stage == 3:
            for part in self.pieces[piece]:
                value = part.ref[net.own + part.where].astype(F32)
                for other in range(1, net.line):
                    value = value + part.buffers[4][other - 1].astype(F32)
                for low, high, staged, out, semaphore in part.outs:
                    staged[...] = value[:, low:high]
                    pltpu.make_async_copy(staged, out, semaphore).start()
            return
        rest = net.far + ([1, 2] if stage == 0 else [])
        rest.sort()

        def one_shard(step, carried):
            place = {bit: (step >> at) & 1 for at, bit in enumerate(rest)}
            index = tuple(
                place[bit] if bit in place else net.turned(bit, net.first if stage == 1 else None)
                for bit in reversed(range(net.count))
            )
            arrived = tuple(place[bit] for bit in reversed(rest)) + (slice(None), slice(None))
            for part in self.pieces[piece]:
                where = index + part.where
                if stage == 2:
                    value = (
                        part.ref[where].astype(F32)
                        + part.buffers[2][arrived].astype(F32)
                        + part.buffers[3][arrived].astype(F32)
                    )
                else:
                    value = part.ref[where] + part.buffers[stage][arrived]
                part.ref[where] = value.astype(part.ref.dtype)
            return carried

        lax.fori_loop(0, 1 << len(rest), one_shard, 0, unroll=True)

    def step(self, piece, stage):
        self.each(piece, stage, lambda copy: copy.wait_recv())
        self.add(piece, stage)
        if stage == 0:
            self.begin(piece, 1)
            self.begin(piece, 2)
        elif stage == 1:
            self.begin(piece, 3)
        elif stage == 2:
            self.each(piece, 3, lambda copy: copy.start())

    def finish(self):
        super().finish()
        for piece in self.pieces:
            for part in piece:
                for _, _, staged, out, semaphore in part.outs:
                    pltpu.make_async_copy(staged, out, semaphore).wait()


class Plan:
    def __init__(self, transfer, table):
        self.transfer, self.table, self.stop = transfer, table, 0

    def next(self):
        taken = self.table.get(self.stop, ())
        self.stop += 1

        def act():
            for piece, stage in taken:
                self.transfer.step(piece, stage)

        return act if taken else None

    def now(self):
        act = self.next()
        if act:
            act()

    def loop(self, places):
        found = {place: self.next() for place in places}
        return {place: act for place, act in found.items() if act}


def layer_kernel(r, wide_size, narrow_size):
    net = Exchange(wide_size, narrow_size)
    net.greet()
    devices = wide_size * narrow_size
    wide7, tall7, vec7, gvec7 = r.wide, r.tall, r.vec, r.grad_vec
    wide = wide7.reshape(devices * wide7.shape[-2], wide7.shape[-1])
    tall = tall7.reshape(devices * tall7.shape[-2], tall7.shape[-1])
    slope7 = r.slope
    slope = slope7.reshape(devices * slope7.shape[-2], slope7.shape[-1])
    own_rows = (0, wide7.shape[-2])
    tokens, memory, seed, seed_next = r.tokens, r.memory, r.seed, r.seed_next
    rows, sources = tokens.shape[0], memory.shape[0]
    tiles = rows // TILE
    local = r.local

    wide_moves = [
        (block * D + pair * PAIR // 3, pair * PAIR + block * PAIR // 3, PAIR // 3)
        for pair in range(HEADS // 2)
        for block in range(3)
    ] + [(3 * D, 3 * D, wide7.shape[-1] - 3 * D)]
    loads = [
        pltpu.make_async_copy(
            r.w_wide.at[:, pl.ds(low, width)],
            wide7.at[net.own + (slice(None), pl.ds(high, width))],
            r.own_done.at[number],
        )
        for number, (low, high, width) in enumerate(wide_moves)
    ] + [
        pltpu.make_async_copy(r.w_tall, tall7.at[net.own], local.at[1]),
        pltpu.make_async_copy(r.vecs, vec7.at[net.own], local.at[2]),
        pltpu.make_async_copy(r.tokens_in, tokens, local.at[3]),
        pltpu.make_async_copy(r.memory_in, memory, local.at[4]),
        pltpu.make_async_copy(r.cotangent, seed, local.at[5]),
    ]
    for copy in loads:
        copy.start()

    tall_rows = tall7.shape[-2]
    tall_cuts = [(low, low + tall_rows // TALL_CUT) for low in range(0, tall_rows, tall_rows // TALL_CUT)]

    def wide_part(low, high):
        return [Part(wide7, None, (low, high))]

    gather = Gather(
        net,
        [
            wide_part(0, PAIR) + [Part(vec7)],
            wide_part(PAIR, 2 * PAIR),
            wide_part(2 * PAIR, 4 * PAIR),
            wide_part(3 * D, 5 * D),
            wide_part(5 * D, 7 * D),
            wide_part(7 * D, 9 * D),
            wide_part(9 * D, 12 * D),
        ]
        + [[Part(tall7, cut)] for cut in tall_cuts],
        r.gather_send,
        r.gather_receive,
    )
    plan = Plan(gather, GATHER_STEPS)
    out_semaphores = iter(range(OUT_SEMAPHORES))

    def out_of(low, high, staged, out):
        return (low, high, staged, out, r.out_done.at[next(out_semaphores)])

    def wide_out(low, high, start):
        columns = pl.ds(start, high - low)
        return out_of(low, high, r.out_wide.at[:, columns], r.grad_wide.at[:, columns])

    def wide_sum(low, high, buffers):
        return [Part(wide7, None, (low, high), buffers, [wide_out(0, high - low, low)])]

    def self_sum(pair):
        third = PAIR // 3
        outs = [
            wide_out(block * third, (block + 1) * third, block * D + pair * third)
            for block in range(3)
        ]
        columns = (pair * PAIR, (pair + 1) * PAIR)
        return [Part(slope7, own_rows, columns, r.in_self[pair], outs)]

    vec_out = out_of(0, 128, r.out_vec, r.grad_vecs)
    total = Sum(
        net,
        [
            [Part(tall7, None, None, r.in_tall, [out_of(0, D, r.out_tall, r.grad_tall)])],
            wide_sum(8 * D, 12 * D, r.in_up),
            wide_sum(3 * D, 8 * D, r.in_mid),
        ]
        + [self_sum(pair) for pair in range(HEADS // 2)]
        + [[Part(gvec7, None, None, r.in_vec, [vec_out])]],
        r.sum_send,
        r.sum_receive,
    )
    TALL, UP, MID, SELF = range(4)
    VECTORS = SELF + HEADS // 2
    sum_plan = Plan(total, SUM_STEPS)

    for copy in loads[:-3]:
        copy.wait()
    net.meet()
    gather.start(0)
    gather.start(gather.last)

    def endings(lengths):
        found, running = [], 0
        for index in range(SEGS):
            running = running + lengths[0, index]
            found.append(running)
        return found

    target_ends = endings(r.tgt_lengths)
    source_ends = endings(r.src_lengths)

    def chosen(ends, count):
        place = lax.broadcasted_iota(jnp.int32, (16, count), 1)
        segment = jnp.zeros((16, count), jnp.int32)
        for end in ends:
            segment = segment + (place >= end).astype(jnp.int32)
        return segment == lax.broadcasted_iota(jnp.int32, (16, count), 0)

    def query_features(ends, count):
        return jnp.where(chosen(ends, count), 1.0, 0.0).astype(BF16)

    def key_features(ends, count):
        row = lax.broadcasted_iota(jnp.int32, (16, count), 0)
        masked = jnp.where(chosen(ends, count), 0.0, -BIG)
        return jnp.where(row < SEGS, masked, jnp.where(row < SEGS + 3, 1.0, 0.0)).astype(BF16)

    def value_features(count):
        row = lax.broadcasted_iota(jnp.int32, (16, count), 0)
        return jnp.where(row < 3, 1.0, 0.0).astype(BF16)

    def every_head(ref, features):
        ref[:, HEAD_DIM:, :] = jnp.broadcast_to(features[None], (HEADS,) + features.shape)

    q, k, v, q2, k2, v2 = r.q, r.k, r.v, r.q2, r.k2, r.v2
    every_head(q, query_features(target_ends, rows))
    every_head(q2, query_features(target_ends, rows))
    every_head(k, key_features(target_ends, rows))
    every_head(k2, key_features(source_ends, sources))
    every_head(v, value_features(rows))
    every_head(v2, value_features(sources))
    plan.now()

    def position(tile):
        return tile * TILE + lax.broadcasted_iota(jnp.int32, (TILE, 1), 0)

    def valid(tile):
        return jnp.where(position(tile) < target_ends[SEGS - 2], 1.0, 0.0)

    def follow(tile):
        after = position(tile) + 1
        ended = after == target_ends[0]
        for end in target_ends[1:]:
            ended = ended | (after == end)
        return jnp.where(ended, 0.0, 1.0)

    def span(tile):
        return pl.ds(tile * TILE, TILE)

    shift, res = r.shift, r.res
    loads[-1].wait()
    shift[0:8, :] = jnp.zeros((8, D), F32)
    for tile in range(tiles):
        masked = seed[span(tile), :].astype(F32) * valid(tile)
        seed[span(tile), :] = masked.astype(BF16)
        shift[pl.ds(tile * TILE + 8, TILE), :] = masked * follow(tile)
    for tile in range(tiles):
        seed_next[span(tile), :] = shift[pl.ds(tile * TILE + 7, TILE), :].astype(BF16)
    r.grad_rows[...] = jnp.zeros_like(r.grad_rows)
    r.grad_columns[...] = jnp.zeros_like(r.grad_columns)
    loads[-3].wait()
    loads[-2].wait()

    def row(index):
        return r.row_vectors[index : index + 1, :]

    def column(index):
        return vec7[...].reshape(D, vec7.shape[-1])[:, index : index + 1].astype(F32)

    def heads_of(value):
        return value.reshape(value.shape[0] // HEAD_DIM, HEAD_DIM, value.shape[1])

    def scaled(value):
        return (value.astype(BF16).astype(F32) * SCORE_SCALE).astype(BF16)

    def wide_column(index):
        return wide[:, index * D : (index + 1) * D]

    self_ranges = bands(rows, rows, 512)
    cross_ranges = bands(rows, sources, None)
    cross_wide = bands(rows, sources, None, 2 * TILE)
    cross_scores = [shift.at[pl.ds(start, sources), :] for start in (0, sources)]
    a, a2 = r.mixed, r.mixed2
    bias_rows = PAIR // 3
    identity = lax.broadcasted_iota(jnp.int32, (D, D), 0) == lax.broadcasted_iota(
        jnp.int32, (D, D), 1
    )
    identity = jnp.where(identity, 1.0, 0.0).astype(BF16)
    for index, pairs in enumerate(PAIR_GROUPS):
        plan.now()
        if index == 0:
            r.row_vectors[0 : vec7.shape[-1], :] = dot(
                vec7[...].reshape(D, vec7.shape[-1]), identity, 0, 0
            )
        biases = []
        for pair in pairs:
            place = slice(pair * bias_rows, (pair + 1) * bias_rows)
            biases += [column(0)[place], jnp.zeros((bias_rows, 1), F32), column(1)[place]]
        bias = jnp.concatenate(biases, axis=0)
        for tile in range(tiles):
            both = dot(
                wide[:, pairs[0] * PAIR : (pairs[-1] + 1) * PAIR], tokens[span(tile), :], 0, 1
            )
            both = (both + bias).astype(BF16)
            for place, pair in enumerate(pairs):
                for block, ref in enumerate((q, k, v)):
                    start = place * PAIR + block * bias_rows
                    value = both[start : start + bias_rows]
                    if block == 0:
                        value = (value.astype(F32) * SCORE_SCALE).astype(BF16)
                    ref[2 * pair : 2 * pair + 2, 0:HEAD_DIM, span(tile)] = heads_of(value)
        plan.now()
        heads = (2 * pairs[0], 2 * pairs[-1] + 2)
        attention_forward(
            q,
            k,
            v,
            a,
            r.scores,
            self_ranges,
            heads,
            plan.loop(range(*heads)),
        )

    normed, low, inverse = r.normed, r.low, r.inverse

    def norm_tile(index, tile, before):
        out, unit, rho = normalize(before, row(GAIN + 2 * index), row(GAIN + 2 * index + 1))
        normed[index][span(tile), :] = unit.astype(BF16)
        inverse[span(tile), index : index + 1] = rho
        low[index][span(tile), :] = out.astype(BF16)
        return out

    plan.now()
    for tile in range(tiles):
        before = (
            tokens[span(tile), :].astype(F32) + dot(a[:, span(tile)], wide_column(3), 0, 0) + row(2)
        )
        out = norm_tile(0, tile, before)
        res[span(tile), :] = out
        q2[:, 0:HEAD_DIM, span(tile)] = heads_of(
            scaled(dot(wide_column(4), out.astype(BF16), 0, 1) + column(3))
        )
        plan.now()
    plan.now()
    for tile in range(sources // TILE):
        part = memory[span(tile), :]
        k2[:, 0:HEAD_DIM, span(tile)] = heads_of(dot(wide_column(5), part, 0, 1).astype(BF16))
        v2[:, 0:HEAD_DIM, span(tile)] = heads_of(
            (dot(wide_column(6), part, 0, 1) + column(4)).astype(BF16)
        )
    attention_forward(
        q2,
        k2,
        v2,
        a2,
        cross_scores,
        cross_wide,
        (0, HEADS),
        plan.loop(range(HEADS)),
    )
    active = r.active
    plan.now()
    for tile in range(tiles):
        before = res[span(tile), :] + dot(a2[:, span(tile)], wide_column(7), 0, 0) + row(5)
        out = norm_tile(1, tile, before)
        res[span(tile), :] = out
        for block in range(FF // D):
            if tile == 0 and block == 1:
                plan.now()
            columns = slice(block * D, (block + 1) * D)
            u = dot(out.astype(BF16), wide_column(8 + block), 1, 0) + row(6 + block)
            value, derivative = gelu_pair(u)
            active[span(tile), columns] = value.astype(BF16)
            slope[span(tile), columns] = derivative.astype(BF16)
        plan.now()
    early = range(gather.last - 2)
    gather.finish(early)
    plan.now()
    slot_left = tall.at[pl.ds(FF, D), :]
    slot_right = tall.at[pl.ds(FF + D, D), :]
    for tile in range(tiles):
        before = (
            res[span(tile), :] + dot(active[span(tile), :], tall[0:FF, :], 1, 0) + row(BIAS_OUT)
        )
        norm_tile(2, tile, before)
    low_grad = r.low_grad
    gather.finish(range(len(early), gather.last + 1))

    grad_rows, grad_columns = r.grad_rows, r.grad_columns

    def add_row(index, value):
        grad_rows[index : index + 1, :] += jnp.sum(value, axis=0, keepdims=True)

    def norm_back(index, tile, gradient, bias_row):
        gain = row(GAIN + 2 * index)
        unit = normed[index][span(tile), :].astype(F32)
        scaled_grad = gradient * gain
        inner = jnp.mean(scaled_grad * unit, axis=-1, keepdims=True)
        before = inverse[span(tile), index : index + 1] * (
            scaled_grad - jnp.mean(scaled_grad, axis=-1, keepdims=True) - unit * inner
        )
        add_row(GAIN + 2 * index, gradient * unit)
        add_row(GAIN + 2 * index + 1, gradient)
        add_row(bias_row, before)
        res[span(tile), :] = before
        low_grad[span(tile), :] = before.astype(BF16)

    for tile in range(tiles):
        part = seed[span(tile), :]
        add_row(BIAS_OUT + 1, part.astype(F32))
        gradient = dot(part, slot_left[...], 1, 1) + dot(
            seed_next[span(tile), :], slot_right[...], 1, 1
        )
        norm_back(2, tile, gradient, BIAS_OUT)
    grad_left = dot(low[2][...], seed[...], 0, 0).astype(BF16)
    seed[0:D, :] = slot_left[...]
    slot_left[...] = grad_left
    grad_right = dot(low[2][...], seed_next[...], 0, 0).astype(BF16)
    seed[D : 2 * D, :] = slot_right[...]
    slot_right[...] = grad_right
    for block in range(FF // D):
        columns = slice(block * D, (block + 1) * D)
        for tile in range(tiles):
            grad = dot(low_grad[span(tile), :], tall[columns, :], 1, 1) * slope[
                span(tile), columns
            ].astype(F32)
            add_row(6 + block, grad)
            slope[span(tile), columns] = grad.astype(BF16)
        tall[columns, :] = dot(active[:, columns], low_grad[...], 0, 0).astype(BF16)
    total.start(TALL)
    for tile in range(tiles):
        gradient = res[span(tile), :] + dot(
            slope[span(tile), :], wide[:, 8 * D : 8 * D + FF], 1, 1
        )
        norm_back(1, tile, gradient, 5)
        sum_plan.now()
    for block in range(FF // D):
        columns = slice(block * D, (block + 1) * D)
        wide[:, 8 * D + block * D : 8 * D + (block + 1) * D] = dot(
            low[1][...], slope[:, columns], 0, 0
        ).astype(BF16)
        if block == FF // D - 1:
            total.start(UP)
        sum_plan.now()
    grads = r.mixed_grad

    def mixed_back(weight_index, mixed):
        for tile in range(tiles):
            grad = dot(wide_column(weight_index), low_grad[span(tile), :], 1, 1).astype(BF16)
            grads[:, 0:HEAD_DIM, span(tile)] = heads_of(grad)
            inner = jnp.sum(
                heads_of(grad.astype(F32) * mixed[:, span(tile)].astype(F32)),
                axis=1,
                keepdims=True,
            )
            place = lax.broadcasted_iota(jnp.int32, (HEADS, 16, TILE), 1)
            features = jnp.zeros((HEADS, 16, TILE), F32)
            for step, part in enumerate(split_three(-inner)):
                features = jnp.where(place == step, part, features)
            grads[:, HEAD_DIM:, span(tile)] = features.astype(BF16)
        wide[:, weight_index * D : (weight_index + 1) * D] = dot(
            mixed[...], low_grad[...], 1, 0
        ).astype(BF16)

    mixed_back(7, a2)
    sum_plan.now()
    dq2 = active.at[pl.ds(0, D), pl.ds(0, rows)]
    dk2 = active.at[pl.ds(D, D), pl.ds(0, sources)]
    dv2 = active.at[pl.ds(D, D), pl.ds(rows, sources)]

    def head_rows(ref):
        def of(head):
            return ref.at[pl.ds(pl.multiple_of(head * HEAD_DIM, HEAD_DIM), HEAD_DIM), :]

        return of

    sums = (r.key_sum, r.value_sum)
    attention_backward(
        q2,
        k2,
        v2,
        grads,
        [head_rows(ref) for ref in (dq2, dk2, dv2)],
        sums,
        r.shares,
        r.score_grads,
        cross_ranges,
        sum_plan.loop(range(HEADS)),
    )

    def column_sum(index, value):
        grad_columns[:, index : index + 1] += jnp.sum(value.astype(F32), axis=1, keepdims=True)

    for tile in range(tiles):
        gradient = res[span(tile), :] + dot(dq2[:, span(tile)], wide_column(4), 0, 1)
        norm_back(0, tile, gradient, 2)
        sum_plan.now()
    shift[0:sources, :] = dot(dk2[...], wide_column(5), 0, 1) + dot(dv2[...], wide_column(6), 0, 1)
    memory_copy = pltpu.make_async_copy(
        shift.at[pl.ds(0, sources), :], r.grad_memory, local.at[10]
    )
    memory_copy.start()
    wide[:, 5 * D : 6 * D] = dot(memory[...], dk2[...], 0, 1).astype(BF16)
    wide[:, 6 * D : 7 * D] = dot(memory[...], dv2[...], 0, 1).astype(BF16)
    sum_plan.now()
    wide[:, 4 * D : 5 * D] = dot(low[0][...], dq2[...], 0, 1).astype(BF16)
    column_sum(3, dq2[...])
    column_sum(4, dv2[...])
    mixed_back(3, a)
    total.start(MID)
    sum_plan.now()

    def pair_rows(block):
        def of(head):
            pair = head // 2
            row = pair % 2 * PAIR + block * (PAIR // 3) + head % 2 * HEAD_DIM
            start = pl.multiple_of(pair // 2 * rows, rows)
            return active.at[pl.ds(pl.multiple_of(row, HEAD_DIM), HEAD_DIM), pl.ds(start, rows)]

        return of

    def pair_grad(pair):
        return active[pair % 2 * PAIR : (pair % 2 + 1) * PAIR, pair // 2 * rows : (pair // 2 + 1) * rows]

    def start_pair(pair):
        where = (slice(None),) * net.count + (
            slice(0, own_rows[1]),
            slice(pair * PAIR, (pair + 1) * PAIR),
        )
        slope7[where] = (
            dot(tokens[...], pair_grad(pair), 0, 1)
            .astype(BF16)
            .reshape(slope7.shape[: net.count] + (own_rows[1], PAIR))
        )
        total.start(SELF + pair)

    def start_vectors():
        for pair in range(HEADS // 2):
            place = slice(pair * bias_rows, (pair + 1) * bias_rows)
            grad = pair_grad(pair).astype(F32)
            for index, block in ((0, 0), (1, 2)):
                grad_columns[place, index : index + 1] = jnp.sum(
                    grad[block * bias_rows : (block + 1) * bias_rows], axis=1, keepdims=True
                )
        turned = jnp.transpose(r.grad_rows[...]) + grad_columns[...]
        gvec7[...] = turned.reshape(gvec7.shape)
        total.start(VECTORS)

    hooks = {}
    for head in range(HEADS):
        act = sum_plan.next()

        def hook(head=head, act=act):
            if head % 2 and head < HEADS - 1:
                start_pair(head // 2)
            if act:
                act()

        if act or (head % 2 and head < HEADS - 1):
            hooks[head] = hook
    attention_backward(
        q,
        k,
        v,
        grads,
        [pair_rows(block) for block in range(3)],
        sums,
        r.shares,
        r.score_grads,
        self_ranges,
        hooks,
    )
    start_pair(HEADS // 2 - 1)
    start_vectors()
    sum_plan.now()

    memory_copy.wait()
    shift[rows : rows + 8, :] = jnp.zeros((8, D), F32)
    for tile in range(tiles):
        shift[span(tile), :] = dot(low[2][span(tile), :], seed[D : 2 * D, :], 1, 0)
        sum_plan.now()
    token_copies = []
    for tile in range(tiles):
        low_grad[span(tile), :] = (
            (
                dot(low[2][span(tile), :], seed[0:D, :], 1, 0)
                + follow(tile) * shift[pl.ds(tile * TILE + 1, TILE), :]
                + row(BIAS_OUT + 1)
            )
            * valid(tile)
        ).astype(BF16)
        copy = pltpu.make_async_copy(
            low_grad.at[span(tile), :], r.slots.at[span(tile), :], local.at[6 + tile]
        )
        copy.start()
        token_copies.append(copy)
        sum_plan.now()
    for tile in range(tiles):
        value = res[span(tile), :]
        for side in range(2):
            value = value + dot(
                active[0 : 2 * PAIR, pl.ds(side * rows + tile * TILE, TILE)],
                wide[:, 2 * side * PAIR : 2 * (side + 1) * PAIR],
                0,
                1,
            )
        res[span(tile), :] = value
        copy = pltpu.make_async_copy(
            res.at[span(tile), :], r.grad_tokens.at[span(tile), :], local.at[12 + tile]
        )
        copy.start()
        token_copies.append(copy)
        sum_plan.now()
    sum_plan.now()
    total.finish()
    for copy in token_copies:
        copy.wait()


def finish_kernel(*refs):
    given, results, held = refs[:12], refs[12:21], refs[21:33]
    vec_out, semaphores = refs[33], refs[34]
    loads = [
        pltpu.make_async_copy(source, target, semaphores.at[index])
        for index, (source, target) in enumerate(zip(given, held))
    ]
    for copy in loads:
        copy.start()
    stores = []

    def store(index, source):
        copy = pltpu.make_async_copy(source, results[index], semaphores.at[12 + index])
        copy.start()
        stores.append(copy)

    for index in range(12):
        loads[index].wait()
        if index < 5:
            store(index, held[index])
        elif index == 5:
            vec_out[...] = held[5][:, : vec_out.shape[1]]
            store(5, vec_out)
        elif index >= 9:
            average = held[index - 3]
            average[...] += (held[index][...].astype(F32) - average[...]) / AVG_STEPS
            store(index - 3, average)
    for copy in stores:
        copy.wait()


def fused_body(
    wide_size,
    narrow_size,
    tokens,
    memory,
    w_wide,
    w_tall,
    vecs,
    avg_wide,
    avg_tall,
    avg_vecs,
    tgt_lengths,
    src_lengths,
    cotangent,
):
    count = (wide_size * narrow_size).bit_length() - 1
    rows, sources = tokens.shape[0], memory.shape[0]
    wide_rows, wide_columns = w_wide.shape
    tall_rows = w_tall.shape[0]
    vec_rows = vecs.shape[0]
    bits = (2,) * count
    hbm = pl.BlockSpec(memory_space=pl.ANY)
    smem = pl.BlockSpec(memory_space=pltpu.SMEM)
    inputs = dict(
        tgt_lengths=tgt_lengths,
        src_lengths=src_lengths,
        tokens_in=tokens,
        memory_in=memory,
        cotangent=cotangent,
        w_wide=w_wide,
        w_tall=w_tall,
        vecs=vecs,
    )
    outputs = dict(
        slots=jax.ShapeDtypeStruct((rows, D), BF16),
        grad_tokens=jax.ShapeDtypeStruct((rows, D), F32),
        grad_memory=jax.ShapeDtypeStruct((sources, D), F32),
        grad_wide=jax.ShapeDtypeStruct((wide_rows, wide_columns), F32),
        grad_tall=jax.ShapeDtypeStruct((tall_rows, D), F32),
        grad_vecs=jax.ShapeDtypeStruct((vec_rows, 128), F32),
    )

    def arrivals(shape, dtype=BF16):
        line = (1 << (count - 3)) - 1
        far = bits[3:]
        return [
            pltpu.VMEM(lead + shape, dtype) for lead in (bits[1:], far, far, far, (line,))
        ]

    scratch = dict(
        wide=pltpu.VMEM(bits + (wide_rows, wide_columns), BF16),
        tall=pltpu.VMEM(bits + (tall_rows, D), BF16),
        vec=pltpu.VMEM(bits + vecs.shape, BF16),
        grad_vec=pltpu.VMEM(bits + (vec_rows, 128), F32),
        tokens=pltpu.VMEM((rows, D), BF16),
        memory=pltpu.VMEM((sources, D), BF16),
        seed=pltpu.VMEM((rows, D), BF16),
        seed_next=pltpu.VMEM((rows, D), BF16),
        q=pltpu.VMEM((HEADS, AUG, rows), BF16),
        k=pltpu.VMEM((HEADS, AUG, rows), BF16),
        v=pltpu.VMEM((HEADS, AUG, rows), BF16),
        q2=pltpu.VMEM((HEADS, AUG, rows), BF16),
        k2=pltpu.VMEM((HEADS, AUG, sources), BF16),
        v2=pltpu.VMEM((HEADS, AUG, sources), BF16),
        mixed_grad=pltpu.VMEM((HEADS, AUG, rows), BF16),
        mixed=pltpu.VMEM((D, rows), BF16),
        mixed2=pltpu.VMEM((D, rows), BF16),
        active=pltpu.VMEM((rows, FF), BF16),
        slope=pltpu.VMEM(bits + (rows >> count, FF), BF16),
        res=pltpu.VMEM((rows, D), F32),
        low_grad=pltpu.VMEM((rows, D), BF16),
        shift=pltpu.VMEM((rows + 8, D), F32),
        key_sum=pltpu.VMEM((HEAD_DIM, rows), F32),
        value_sum=pltpu.VMEM((HEAD_DIM, rows), F32),
        inverse=pltpu.VMEM((rows, 128), F32),
        row_vectors=pltpu.VMEM((24, D), F32),
        grad_rows=pltpu.VMEM((128, D), F32),
        grad_columns=pltpu.VMEM((D, 128), F32),
        out_wide=pltpu.VMEM((wide_rows, wide_columns), F32),
        out_tall=pltpu.VMEM((tall_rows, D), F32),
        out_vec=pltpu.VMEM((vec_rows, 128), F32),
        normed=[pltpu.VMEM((rows, D), BF16) for _ in range(3)],
        low=[pltpu.VMEM((rows, D), BF16) for _ in range(3)],
        scores=[
            pltpu.VMEM((max(high - low for low, high in bands(rows, rows, 512)), TILE), F32)
            for _ in range(2)
        ],
        shares=[pltpu.VMEM((TILE, rows), BF16) for _ in range(2)],
        score_grads=[pltpu.VMEM((TILE, rows), BF16) for _ in range(2)],
        in_tall=arrivals((tall_rows, D)),
        in_up=arrivals((wide_rows, FF)),
        in_mid=arrivals((wide_rows, 5 * D)),
        in_self=[arrivals((wide_rows, PAIR)) for _ in range(HEADS // 2)],
        in_vec=arrivals((vec_rows, 128), F32),
        local=pltpu.SemaphoreType.DMA((20,)),
        own_done=pltpu.SemaphoreType.DMA((3 * HEADS // 2 + 1,)),
        out_done=pltpu.SemaphoreType.DMA((OUT_SEMAPHORES,)),
        gather_send=pltpu.SemaphoreType.DMA((7 + TALL_CUT, 3 + (1 << (count - 3)), 2)),
        gather_receive=pltpu.SemaphoreType.DMA((7 + TALL_CUT, 3 + (1 << (count - 3)), 2)),
        sum_send=pltpu.SemaphoreType.DMA((4 + HEADS // 2, 3 + (1 << (count - 3)), 1)),
        sum_receive=pltpu.SemaphoreType.DMA((4 + HEADS // 2, 3 + (1 << (count - 3)), 1)),
    )
    scratch_leaves, scratch_tree = jax.tree.flatten(scratch)
    input_leaves, output_leaves = list(inputs.values()), list(outputs.values())
    names = list(inputs) + list(outputs)
    spec = [smem if value.dtype == jnp.int32 else hbm for value in input_leaves]

    def kernel(*refs):
        held = dict(zip(names, refs))
        held.update(jax.tree.unflatten(scratch_tree, refs[len(names) :]))
        layer_kernel(types.SimpleNamespace(**held), wide_size, narrow_size)

    slots, grad_tokens, grad_memory, grad_wide, grad_tall, grad_vecs = pl.pallas_call(
        kernel,
        out_shape=output_leaves,
        in_specs=spec,
        out_specs=[hbm] * len(outputs),
        scratch_shapes=scratch_leaves,
        compiler_params=pltpu.CompilerParams(
            collective_id=0, has_side_effects=True, vmem_limit_bytes=67_000_000
        ),
    )(*input_leaves)
    done = [slots, grad_tokens, grad_memory, grad_wide, grad_tall, grad_vecs]
    done += [avg_wide, avg_tall, avg_vecs, w_wide, w_tall, vecs]
    shapes = outputs | dict(grad_vecs=jax.ShapeDtypeStruct(vecs.shape, F32))
    return pl.pallas_call(
        finish_kernel,
        out_shape=list(shapes.values())
        + [jax.ShapeDtypeStruct(value.shape, F32) for value in (avg_wide, avg_tall, avg_vecs)],
        in_specs=[hbm] * len(done),
        out_specs=[hbm] * 9,
        scratch_shapes=[pltpu.VMEM(value.shape, value.dtype) for value in done]
        + [pltpu.VMEM(vecs.shape, F32), pltpu.SemaphoreType.DMA((21,))],
    )(*done)


def solution(mesh):
    in_specs = (
        P(("wide", "narrow"), None),
        P(("wide", "narrow"), None),
        P(("wide", "narrow"), None),
        P(("wide", "narrow"), None),
        P(("wide", "narrow"), None),
        P(("wide", "narrow"), None),
        P(("wide", "narrow"), None),
        P(("wide", "narrow"), None),
        P(("wide", "narrow"), None),
        P(("wide", "narrow"), None),
        P(("wide", "narrow"), None),
    )
    out_specs = (
        P(("wide", "narrow"), None),
        P(("wide", "narrow"), None),
        P(("wide", "narrow"), None),
        P(("wide", "narrow"), None),
        P(("wide", "narrow"), None),
        P(("wide", "narrow"), None),
        P(("wide", "narrow"), None),
        P(("wide", "narrow"), None),
        P(("wide", "narrow"), None),
    )
    devices = mesh.shape["wide"] * mesh.shape["narrow"]
    bits = devices.bit_length() - 1

    def body(*args):
        if args[2].shape[0] % 16 or args[3].shape[0] % 16 or devices != 1 << bits or bits < 3:
            return plain_body(*args)
        return fused_body(mesh.shape["wide"], mesh.shape["narrow"], *args)

    return jax.shard_map(body, mesh=mesh, in_specs=in_specs, out_specs=out_specs, check_vma=False)
```
